32 devices in a mesh: blk: 16 (over z, y, core), sub: 2 (over x).
Axes of the slice: x: 2, y: 2, z: 4, core: 2. Of those that a mesh axis runs over, the one named last changes fastest.
Arguments:
- spectra: bfloat16 [32768, 2048], P(('blk', 'sub')), as said below
- class_scores: bfloat16 [32768, 128], P(('blk', 'sub')), may hold values from -8 to 8
- reach: int32 [64], replicated, may hold values from 0 to 2, as said below
Outputs:
- propagated: float32 [32768, 128], P(('blk', 'sub'))
The draws below stay inside these ranges and needn't reach their ends.
Inputs may be any that keep to these rules, and one draw needn't show every extreme that they name: `spectra`: intensities are positive in every bin. Block i is paired with blocks i to i + reach[i], and i + reach[i] <= 63. In each aligned group of 2 blocks the reaches sum to at most 4; in every draw the first group and the next-to-last group reach that sum with reach 2 at their last two blocks.
All inputs are finite; a program needn't handle non-finite values.
Results may differ from the reference program's by a relative error of at most 0.0028.
Values may be sent and summed in bfloat16 or wider, within the bound.
A program may use at most 64 MiB of HBM per device.

```python
import jax
import jax.numpy as jnp
from jax import lax

BINS = 2048
BLOCK = 512
FEAT = 128
REACH = 2
PAIR_CAP = 4
BLK_DEV = 2
NBLOCKS = 64
SPECTRA = 32768


def draw_spectra(key, part):
    keys = jax.random.split(key, 7)
    family_rows = BLOCK // 4
    families = SPECTRA // family_rows + 16
    row_index = jnp.arange(SPECTRA)
    family = row_index // family_rows + jax.random.randint(keys[0], (SPECTRA,), 0, 16)
    profile_on = jax.random.bernoulli(keys[1], 0.12, (families, BINS))
    profile_size = jnp.exp(jax.random.uniform(keys[2], (families, BINS), jnp.float32, jnp.log(0.05), 0.0))
    own_size = jnp.exp(jax.random.uniform(keys[5], (SPECTRA, BINS), jnp.float32, jnp.log(0.05), 0.0))
    profile = jnp.where(profile_on, profile_size, 0.0)
    jitter = jnp.exp(jax.random.uniform(keys[3], (SPECTRA, BINS), jnp.float32, -0.7, 0.7))
    shared = profile[family] * jitter
    own_on = jax.random.bernoulli(keys[4], 0.08, (SPECTRA, BINS))
    baseline = jnp.exp(jax.random.uniform(keys[6], (SPECTRA, BINS), jnp.float32, jnp.log(0.0001), jnp.log(0.001)))
    return (shared + jnp.where(own_on, own_size, 0.0) + baseline).astype(jnp.bfloat16)


def draw_reach(key, part):
    key_crowd, key_drawn, key_chosen = jax.random.split(key, 3)
    groups = NBLOCKS // BLK_DEV
    crowded = (jax.random.randint(key_crowd, (groups,), 0, 6) == 0).astype(jnp.int32)
    drawn = jax.random.randint(key_drawn, (groups, BLK_DEV), 0, REACH + 1) * crowded[:, None]
    chosen = jax.random.randint(key_chosen, (), 0, groups - 1)
    columns = jnp.arange(BLK_DEV)
    forced = jnp.where(columns >= BLK_DEV - 2, REACH, 0).astype(jnp.int32)
    group_ids = jnp.arange(groups)
    pinned = (group_ids == chosen) | (group_ids == 0) | (group_ids == groups - 2)
    drawn = jnp.where(pinned[:, None], forced[None, :], drawn)
    before = jnp.cumsum(drawn, axis=1) - drawn
    capped = jnp.minimum(jnp.maximum(PAIR_CAP - before, 0), drawn)
    reaches = capped.reshape(NBLOCKS)
    room_left = NBLOCKS - 1 - jnp.arange(NBLOCKS)
    return jnp.minimum(reaches, room_left).astype(jnp.int32)


def steps_of(key, shape, cuts, smallest, top_value):
    level, own = 1.0, jax.random.fold_in(key, 6)
    for axis_at, parts in cuts:
        draws = jnp.exp(jax.random.uniform(jax.random.fold_in(own, axis_at), (parts,), jnp.float32, smallest / len(cuts), top_value / len(cuts)))
        level = level * jnp.repeat(draws, shape[axis_at] // parts).reshape([-1 if axis == axis_at else 1 for axis in range(len(shape))])
    return level


def gaussian(own_key, shape, scale, bound, shards=(), kind=jnp.bfloat16):
    array = jax.random.normal(own_key, shape, jnp.float32) * scale
    if len(shards) > 0:
        array = steps_of(own_key, shape, shards, -0.22, 0.18) * array
    return jnp.clip(array, min=-bound, max=bound).astype(kind)


def setup_inputs(seed: int = 0) -> dict:
    streams_of = jax.random.split(jax.random.key(seed), 4)
    return {
        "spectra": draw_spectra(jax.random.fold_in(streams_of[3], 71), 0),
        "class_scores": gaussian(streams_of[1], (SPECTRA, FEAT), 2.0, 8.0, ((0, 32),)),
        "reach": draw_reach(jax.random.fold_in(streams_of[3], 71), 0),
    }


def normalize_rows(block_rows):
    values = block_rows.astype(jnp.float32)
    total = lax.optimization_barrier(jnp.sum(values, axis=1, keepdims=True))
    return (jnp.sqrt(values) / jnp.sqrt(total + 1e-06)).astype(jnp.bfloat16)

def pair_terms(operands):
    left_unit, right_unit, left_scores, right_scores = operands
    cosine = jnp.dot(left_unit.astype(jnp.float32), right_unit.astype(jnp.float32).T, precision=lax.Precision.HIGHEST)
    rounded = (cosine * cosine * cosine).astype(jnp.bfloat16)
    weight = lax.optimization_barrier(rounded).astype(jnp.float32)
    forward = jnp.dot(weight, right_scores.astype(jnp.float32), precision=lax.Precision.HIGHEST)
    backward = jnp.dot(weight.T, left_scores.astype(jnp.float32), precision=lax.Precision.HIGHEST)
    return (forward, lax.optimization_barrier(jnp.sum(weight, axis=1)), backward, lax.optimization_barrier(jnp.sum(weight, axis=0)))

def skipped_terms(operands):
    blank_scores = jnp.zeros((BLOCK, FEAT), jnp.float32)
    blank_sums = jnp.zeros((BLOCK,), jnp.float32)
    return (blank_scores, blank_sums, blank_scores, blank_sums)

def reference(spectra, class_scores, reach):
    unit_spectra = lax.map(normalize_rows, spectra.reshape(NBLOCKS, BLOCK, BINS))
    scores = class_scores.reshape(NBLOCKS, BLOCK, FEAT)
    totals = jnp.zeros((NBLOCKS, BLOCK, FEAT), jnp.float32)
    degrees = jnp.zeros((NBLOCKS, BLOCK), jnp.float32)

    def visit_block(index, carry):
        totals, degrees = carry
        left_unit = unit_spectra[index]
        left_scores = scores[index]
        for offset in range(REACH + 1):
            partner = jnp.minimum(index + offset, NBLOCKS - 1)
            operands = (left_unit, unit_spectra[partner], left_scores, scores[partner])
            contrib = lax.cond(offset <= reach[index], pair_terms, skipped_terms, operands)
            totals = totals.at[index].add(contrib[0])
            degrees = degrees.at[index].add(contrib[1])
            if offset > 0:
                totals = totals.at[partner].add(contrib[2])
                degrees = degrees.at[partner].add(contrib[3])
        return (totals, degrees)
    totals, degrees = lax.fori_loop(0, NBLOCKS, visit_block, (totals, degrees))
    return (totals / degrees[:, :, None]).reshape(SPECTRA, FEAT)
```

```python
import functools

import jax
import jax.numpy as jnp
from jax import lax
from jax.experimental import pallas as pl
from jax.experimental.pallas import tpu as pltpu
from jax.sharding import PartitionSpec as P

BLOCK = 512
AXES = ("blk", "sub")
GROUP = 4
MESH = pl.DeviceIdType.MESH
HALF = BLOCK // 2
PART = HALF + 16 * (HALF // 128)
SHIP = 2 * PART
NEAR, FAR, EDGE = 2, 3, 4


def kernel(two_blocks, group_edge, reach, spectra, scores, out, units, own, part, ship, ret, offer, kept,
           send_sem, recv_sem):
    bins = spectra.shape[1]
    feat = scores.shape[1]
    subs = lax.axis_size("sub")
    count = lax.axis_size("blk") * subs
    position = lax.axis_index("blk") * subs + lax.axis_index("sub")
    place = lax.rem(position, GROUP)
    odd = lax.rem(place, 2)
    across = position + 1 - 2 * odd
    core = jnp.where(place < 2, position + 2, position - 2)
    beside = position - 1 + 2 * odd
    middle = (place == 1) | (place == 2)
    outer = jnp.logical_not(middle)
    low = place < 2
    high = jnp.logical_not(low)
    has_edge = ((place == 0) & (position > 0)) | ((place == 3) & (position < count - 1))
    first = odd
    second = 1 - odd

    def copy(index, source, target, device):
        return pltpu.make_async_remote_copy(
            src_ref=source,
            dst_ref=target,
            send_sem=send_sem.at[index],
            recv_sem=recv_sem.at[index],
            device_id=(device // subs, lax.rem(device, subs)),
            device_id_type=MESH,
        )

    barrier = pltpu.get_barrier_semaphore()

    def greet(device):
        pl.semaphore_signal(
            barrier,
            inc=1,
            device_id=(device // subs, lax.rem(device, subs)),
            device_id_type=MESH,
        )

    greet(across)
    greet(core)
    beside_used = middle if two_blocks else (place < 0)
    if group_edge:
        beside_used = beside_used | has_edge

    @pl.when(beside_used)
    def _():
        greet(beside)

    def normalize(block):
        def step(i, carry):
            rows = pl.ds(pl.multiple_of(i * 64, 64), 64)
            source = pl.ds(pl.multiple_of(block * BLOCK + i * 64, 64), 64)
            values = spectra[source, :].astype(jnp.float32)
            total = jnp.sum(values, axis=1, keepdims=True)
            unit = jnp.sqrt(values) * (1.0 / jnp.sqrt(total + 1e-06))
            units[block, rows, :bins] = unit.astype(jnp.bfloat16)
            units[block, rows, bins:] = scores[source, :]
            return carry

        lax.fori_loop(0, BLOCK // 64, step, 0)

    def own_reach(index):
        return reach[2 * position + index]

    previous = jnp.maximum(2 * position - 2, 0)

    def flag(condition):
        return jnp.where(condition, 1.0, 0.0).astype(jnp.float32)

    to_next0 = flag(own_reach(0) >= 2)
    to_next1 = flag(own_reach(1) >= 1)
    to_next2 = flag(own_reach(1) >= 2)
    from_prev0 = flag(reach[previous] >= 2)
    from_prev1 = flag(reach[previous + 1] >= 1)
    from_prev2 = flag(reach[previous + 1] >= 2)
    inside = flag(own_reach(0) >= 1)

    def weights(row, column, scale, start=0, size=BLOCK):
        cosine = lax.dot_general(
            units[row, :, :bins],
            units[column, start : start + size, :bins],
            (((1,), (1,)), ((), ())),
            preferred_element_type=jnp.float32,
        )
        return (cosine * cosine * cosine * scale).astype(jnp.bfloat16)

    def forward(column, weight, start=0, size=BLOCK):
        column_scores = units[column, start : start + size, bins:]
        extended = jnp.concatenate([column_scores, jnp.ones_like(column_scores)], axis=1)
        return jnp.dot(weight, extended, preferred_element_type=jnp.float32)

    def local_pairs():
        def step(row, carry):
            own[row] = forward(row, weights(row, row, 1.0))
            own[row] += forward(1 - row, weights(row, 1 - row, inside))
            return carry

        lax.fori_loop(0, 2, step, 0)

    def remote_pairs(column, slot, scale0, scale1, halves=(0, 1)):
        start, size = halves[0] * HALF, HALF * len(halves)
        part[...] = jnp.zeros_like(part)

        def step(row, carry):
            scale = jnp.where(row == 0, scale0, scale1)
            weight = weights(row, column, scale, start, size)
            own[row] += forward(column, weight, start, size)
            part[:size, :] += lax.dot_general(
                weight,
                units[row, :, bins:],
                (((0,), (0,)), ((), ())),
                preferred_element_type=jnp.float32,
            )
            sums = jnp.dot(
                jnp.ones((8, BLOCK), jnp.bfloat16), weight, preferred_element_type=jnp.float32
            )
            for q in range(size // 128):
                part[BLOCK + 8 * q : BLOCK + 8 * q + 8, :] += sums[:, 128 * q : 128 * q + 128]
            return carry

        lax.fori_loop(0, 2, step, 0)
        for place_in, half in enumerate(halves):
            base = half * PART
            ship[slot, base : base + HALF, :] = part[
                place_in * HALF : place_in * HALF + HALF, :
            ].astype(jnp.bfloat16)
            for q in range(HALF // 128):
                row = BLOCK + 8 * (place_in * (HALF // 128) + q)
                line = part[row : row + 8, :]
                high_part = line.astype(jnp.bfloat16).astype(jnp.float32)
                ship[slot, base + HALF + 16 * q : base + HALF + 16 * q + 16, :] = jnp.concatenate(
                    [high_part, line - high_part], axis=0
                ).astype(jnp.bfloat16)

    def add_back(block, slot, scale=1.0, halves=(0, 1)):
        for half in halves:
            base = half * PART
            rows = slice(half * HALF, half * HALF + HALF)
            own[block, rows, :feat] += ret[slot, base : base + HALF, :].astype(jnp.float32) * scale
            for q in range(HALF // 128):
                line = ret[slot, base + HALF + 16 * q : base + HALF + 16 * q + 16, :]
                line = line.astype(jnp.float32)
                line = (line[0:1, :] + line[8:9, :]) * scale
                rows = slice(half * HALF + 128 * q, half * HALF + 128 * q + 128)
                own[block, rows, feat:] += jnp.broadcast_to(line, (128, 128)).T

    if group_edge:
        edge_copy = copy(0, units.at[first], units.at[EDGE], beside)
        edge_back = copy(1, ship.at[2], ret.at[2], beside)

    normalize(first)

    @pl.when(beside_used)
    def _():
        pl.semaphore_wait(barrier, 3)

    @pl.when(jnp.logical_not(beside_used))
    def _():
        pl.semaphore_wait(barrier, 2)

    if two_blocks:
        first_copy = copy(2, units.at[first], units.at[NEAR], across)
        second_copies = [
            copy(
                3 + 5 * h,
                units.at[second, pl.ds(h * HALF, HALF)],
                units.at[FAR, pl.ds(h * HALF, HALF)],
                across,
            )
            for h in range(2)
        ]
        pass_copy = copy(4, units.at[NEAR], units.at[NEAR], core)
        first_back = copy(5, ship.at[0], ret.at[0], across)
        second_backs = [
            copy(
                6 + 3 * h,
                ship.at[1, pl.ds(h * PART, PART)],
                ret.at[1, pl.ds(h * PART, PART)],
                across,
            )
            for h in range(2)
        ]
        beside_back = copy(7, ship.at[0], ret.at[2], beside)

        @pl.when(middle)
        def _():
            first_copy.start()

    if group_edge:

        @pl.when(has_edge)
        def _():
            edge_copy.start()

    normalize(second)

    def edge_pairs():
        @pl.when(has_edge)
        def _():
            edge_copy.wait_recv()
            is_left = place == 3
            remote_pairs(
                EDGE,
                2,
                jnp.where(is_left, to_next0, 0.0),
                jnp.where(is_left, to_next1, from_prev2),
            )
            edge_back.start()

    def edge_end():
        @pl.when(has_edge)
        def _():
            edge_back.wait_recv()
            add_back(first, 2)
            edge_copy.wait_send()
            edge_back.wait_send()

    if two_blocks:
        local_pairs()

        @pl.when(middle)
        def _():
            first_copy.wait_send()
            for half in range(2):
                second_copies[half].start()
            pass_copy.wait_recv()
            is_left = place == 1
            remote_pairs(
                NEAR,
                0,
                jnp.where(is_left, to_next0, 0.0),
                jnp.where(is_left, to_next1, from_prev2),
            )
            beside_back.start()
            beside_back.wait_recv()
            add_back(first, 2)
            first_back.wait_recv()
            add_back(first, 0)
            for half in range(2):
                second_copies[half].wait_send()
                second_backs[half].wait_recv()
                add_back(second, 1, halves=(half,))
            beside_back.wait_send()

        @pl.when(outer)
        def _():
            first_copy.wait_recv()
            pass_copy.start()
            is_left = place == 0
            remote_pairs(
                NEAR,
                0,
                jnp.where(is_left, 0.0, from_prev0),
                jnp.where(is_left, to_next2, 0.0),
            )
            first_back.start()

        if group_edge:
            edge_pairs()

        @pl.when(outer)
        def _():
            is_left = place == 0
            for half in range(2):
                second_copies[half].wait_recv()
                remote_pairs(
                    FAR,
                    1,
                    jnp.where(is_left, to_next0, from_prev1),
                    jnp.where(is_left, to_next1, from_prev2),
                    halves=(half,),
                )
                second_backs[half].start()
            pass_copy.wait_send()
            first_back.wait_send()
            for half in range(2):
                second_backs[half].wait_send()

    else:
        leads = jnp.where(place < 3, jnp.maximum(to_next0, to_next1), 0.0)
        follows = jnp.where(place > 0, jnp.maximum(from_prev0, from_prev1), 0.0)
        has_role = jnp.maximum(leads, follows)
        gather_copies, cross_copies, pass_copies = [], [], []
        for half in range(2):
            rows = pl.ds(half * HALF, HALF)
            near = units.at[NEAR, rows]
            gather_copies.append(copy(2 + 6 * half, offer.at[rows], kept.at[rows], core))
            cross_copies.append(copy(3 + 6 * half, offer.at[rows], near, across))
            pass_copies.append(copy(4 + 6 * half, near, near, core))
        gather_back = copy(5, ship.at[0], ret.at[0], core)
        cross_back = copy(6, ship.at[0], ret.at[1], across)
        pass_back = copy(7, ret.at[1], ret.at[1], core)

        def blend(target, yes, no, scale, rows):
            def step(i, carry):
                chunk = pl.ds(pl.multiple_of(i * rows, rows), rows)
                a = yes[chunk, :].astype(jnp.float32) * scale
                b = no[chunk, :].astype(jnp.float32) * (1.0 - scale)
                target[chunk, :] = (a + b).astype(target.dtype)
                return carry

            lax.fori_loop(0, target.shape[0] // rows, step, 0)

        for half in range(2):
            rows = pl.ds(half * HALF, HALF)
            blend(offer.at[rows], units.at[1, rows], units.at[0, rows], leads, 64)

            @pl.when(high)
            def _():
                gather_copies[half].start()

        @pl.when(low)
        def _():
            for half in range(2):
                rows = pl.ds(half * HALF, HALF)
                gather_copies[half].wait_recv()
                blend(offer.at[rows], offer.at[rows], kept.at[rows], has_role, 64)
                cross_copies[half].start()

        local_pairs()

        @pl.when(low)
        def _():
            for half in range(2):
                cross_copies[half].wait_recv()
                pass_copies[half].start()

        @pl.when(high)
        def _():
            for half in range(2):
                pass_copies[half].wait_recv()

        remote_pairs(
            NEAR,
            0,
            jnp.where(place < 3, to_next0, 0.0) * leads,
            jnp.where(place < 3, to_next1, 0.0) * leads + from_prev2 * follows,
        )

        @pl.when(high)
        def _():
            gather_back.start()

        @pl.when(low)
        def _():
            gather_back.wait_recv()
            blend(ship.at[0], ship.at[0], ret.at[0], has_role, SHIP)
            cross_back.start()

        if group_edge:
            edge_pairs()

        @pl.when(low)
        def _():
            cross_back.wait_recv()
            pass_back.start()

        @pl.when(high)
        def _():
            pass_back.wait_recv()

        add_back(1, 1, leads)
        add_back(0, 1, follows)

        @pl.when(low)
        def _():
            for half in range(2):
                cross_copies[half].wait_send()
                pass_copies[half].wait_send()
            cross_back.wait_send()
            pass_back.wait_send()

        @pl.when(high)
        def _():
            for half in range(2):
                gather_copies[half].wait_send()
            gather_back.wait_send()

    if group_edge:
        edge_end()

    for block in range(2):
        out[block * BLOCK : (block + 1) * BLOCK, :] = own[block, :, :feat] / own[block, :, feat:]


def plan(two_blocks, group_edge, spectra, scores, reach):
    rows, bins = spectra.shape
    feat = scores.shape[1]
    width = bins + feat
    vmem = pl.BlockSpec(memory_space=pltpu.VMEM)
    return pl.pallas_call(
        functools.partial(kernel, two_blocks, group_edge),
        out_shape=jax.ShapeDtypeStruct((rows, feat), jnp.float32),
        in_specs=[pl.BlockSpec(memory_space=pltpu.SMEM), vmem, vmem],
        out_specs=vmem,
        scratch_shapes=[
            pltpu.VMEM((5, BLOCK, width), jnp.bfloat16),
            pltpu.VMEM((2, BLOCK, 2 * feat), jnp.float32),
            pltpu.VMEM((BLOCK + 8 * (BLOCK // 128), feat), jnp.float32),
            pltpu.VMEM((3, SHIP, feat), jnp.bfloat16),
            pltpu.VMEM((3, SHIP, feat), jnp.bfloat16),
            pltpu.VMEM((16 if two_blocks else BLOCK, width), jnp.bfloat16),
            pltpu.VMEM((16 if two_blocks else BLOCK, width), jnp.bfloat16),
            pltpu.SemaphoreType.DMA((12,)),
            pltpu.SemaphoreType.DMA((12,)),
        ],
        compiler_params=pltpu.CompilerParams(
            collective_id=2 * int(two_blocks) + int(group_edge),
            has_side_effects=True,
            vmem_limit_bytes=48 * 2**20,
        ),
        cost_estimate=pl.CostEstimate(
            flops=8 * 2 * BLOCK * BLOCK * bins,
            bytes_accessed=2 * rows * width,
            transcendentals=rows * bins,
        ),
        name="network",
    )(reach, spectra, scores)


CHUNK = 128
PIECE = CHUNK // 2
STEPS = BLOCK // CHUNK
LINES = CHUNK + 16
AHEAD = 2
EX, XS, FW, PRE, POST, RX, RF, RE = 0, 8, 16, 24, 32, 40, 48, 56


def slots_kernel(slots, edges, reach, spectra, scores, out, raw, units, mate, pre, offer, got, past, own, part, ship,
                 ship_edge, ret, ret_mate, ret_edge, load_sem, send_sem, recv_sem):
    bins = spectra.shape[1]
    feat = scores.shape[1]
    total_steps = slots * STEPS
    subs = lax.axis_size("sub")
    count = lax.axis_size("blk") * subs
    position = lax.axis_index("blk") * subs + lax.axis_index("sub")
    place = lax.rem(position, GROUP)
    group = position // GROUP
    side = lax.rem(place, 2)
    core = place // 2
    base = position - place
    odd_group = lax.rem(group, 2) == 1
    even_group = lax.rem(group, 2) == 0
    across = position + 1 - 2 * side
    partner = position + 2 - 4 * core
    at_end = (place == 0) | (place == 3)
    has_edge = ((place == 0) & (position > 0)) | ((place == 3) & (position < count - 1))
    beside = jnp.where(place == 0, position - 1, position + 1)
    is_edge = has_edge & even_group
    host = jnp.where(side == 0, base - GROUP, base + GROUP) + side
    is_host = odd_group & ((side == 1) | (base + GROUP < count))
    guest = jnp.where(side == 0, base + GROUP, base - GROUP + 3)

    def place_of(device):
        return (device // subs, lax.rem(device, subs))

    def copy(index, source, target, device):
        return pltpu.make_async_remote_copy(
            src_ref=source,
            dst_ref=target,
            send_sem=send_sem.at[index],
            recv_sem=recv_sem.at[index],
            device_id=place_of(device),
            device_id_type=MESH,
        )

    def load_copy(k, block):
        rows = pl.ds(pl.multiple_of(block * BLOCK + k * CHUNK, CHUNK), CHUNK)
        return pltpu.make_async_copy(spectra.at[rows], raw.at[rows], load_sem.at[2 * k + block])

    for k in range(STEPS):
        for block in range(2):
            load_copy(k, block).start()

    barrier = pltpu.get_barrier_semaphore()

    def greet(device):
        pl.semaphore_signal(barrier, inc=1, device_id=place_of(device), device_id_type=MESH)

    greet(across)
    greet(partner)
    if edges:

        @pl.when(has_edge)
        def _():
            greet(beside)

        @pl.when(is_edge)
        def _():
            greet(host)
            greet(host + 2)

        @pl.when(is_host)
        def _():
            greet(guest)

    def active(boundary):
        inside = (boundary >= 0) & (boundary < count - 1)
        at = jnp.clip(boundary, 0, count - 2)
        a, b = reach[2 * at], reach[2 * at + 1]
        right = jnp.where(inside & (b == 2), 1, 0)
        left = jnp.where(inside & ((a == 2) | (b == 1)), 1, 0)
        return right, left

    bounds = [active(base + i - 1) for i in range(5)]
    rights = [b[0] for b in bounds]
    lefts = [b[1] for b in bounds]
    hosts = jnp.where(odd_group, 1, 0) if edges else 0

    def assign(inner, late, early):
        d1, d2, d3 = inner
        if slots == 1:
            return ((d1, d2, d3, late * hosts, early * hosts),)
        late, early = late * hosts, early * hosts
        free = 1 - late
        f1 = d1 * free
        f2 = d2 * (1 - d1) * free
        f3 = d3 * (1 - d1) * (1 - d2) * free
        return ((f1, f2, f3, late, 0), (d1 - f1, d2 - f2, d3 - f3, 0, early))

    going = assign((rights[1], lefts[2], rights[3]), lefts[0], lefts[4])
    coming = assign((lefts[1], rights[2], lefts[3]), rights[4], rights[0])

    def pick(options, index):
        value = options[-1]
        for i in range(len(options) - 2, -1, -1):
            value = jnp.where(index == i, options[i], value)
        return value

    def slot_flags(slot):
        q, r = going[slot], coming[slot]
        right_out = pick([q[0], r[1], q[2], r[3]], place)
        left_out = pick([q[3], r[0], q[1], r[2]], place)
        mate_right = pick([q[2], r[3], q[0], r[1]], place)
        mate_left = pick([q[1], r[2], q[3], r[0]], place)
        guest_in = jnp.where(side == 0, q[4], r[4])
        right_in = pick([r[4], q[0], r[1], q[2]], place)
        left_in = pick([r[0], q[1], r[2], q[4]], place)
        return right_out, left_out, mate_right, mate_left, guest_in, right_in, left_in

    flags = [slot_flags(s) for s in range(slots)]

    def flag_at(step, which):
        if slots == 1:
            return flags[0][which]
        return jnp.where(step < STEPS, flags[0][which], flags[1][which])

    own0, own1 = reach[2 * position], reach[2 * position + 1]
    close0 = jnp.where(own0 == 2, 1, 0)
    close1 = jnp.where(own1 == 1, 1, 0)
    inside = jnp.where(own0 >= 1, 1.0, 0.0).astype(jnp.float32)

    edge_right_in = jnp.where(place == 0, rights[0], 0)
    edge_left_in = jnp.where(place == 3, lefts[4], 0)
    edge_out0 = jnp.where(place == 0, lefts[0], 0).astype(jnp.float32)
    edge_out1 = jnp.where(place == 3, rights[4], 0).astype(jnp.float32)

    def chunk_of(step):
        return lax.rem(step, STEPS)

    def normalize(k):
        def one(i, carry):
            block = i // 2
            row = k * CHUNK + lax.rem(i, 2) * 64
            rows = pl.ds(pl.multiple_of(row, 64), 64)
            source = pl.ds(pl.multiple_of(block * BLOCK + row, 64), 64)
            values = raw[source, :].astype(jnp.float32)
            total = jnp.sum(values, axis=1, keepdims=True)
            unit = jnp.sqrt(values) * (1.0 / jnp.sqrt(total + 1e-06))
            units[block, rows, :bins] = unit.astype(jnp.bfloat16)
            units[block, rows, bins:] = scores[source, :]
            return carry

        for block in range(2):
            load_copy(k, block).wait()
        lax.fori_loop(0, 4, one, 0)

    def piece(k, which):
        return pl.ds(pl.multiple_of(k * CHUNK + which * PIECE, PIECE), PIECE)

    def mate_copy(k, block):
        return copy(EX + 2 * k + block, units.at[block, piece(k, 1 - core)], mate.at[k, block], partner)

    def pre_copy(k, which):
        block = jnp.where(place == 0, 0, 1)
        return copy(PRE + 2 * k + which, units.at[block, piece(k, which)], pre.at[k], host + 2 * which)

    def pre_recv(k):
        return copy(PRE + 2 * k + core, pre.at[k], pre.at[k], across)

    def cross_copy(step):
        rows = pl.ds(pl.multiple_of(core * PIECE, PIECE), PIECE)
        return copy(XS + step, offer.at[step], got.at[step, rows], across)

    def forward_copy(step):
        rows = pl.ds(pl.multiple_of(core * PIECE, PIECE), PIECE)
        return copy(FW + step, got.at[step, rows], got.at[step, rows], partner)

    def post_copy(step):
        rows = pl.ds(pl.multiple_of(core * PIECE, PIECE), PIECE)
        return copy(POST + 2 * step + core, got.at[step, rows], past.at[step, rows], guest)

    def post_recv(k, which):
        rows = pl.ds(which * PIECE, PIECE)
        return copy(POST + 2 * k + which, past.at[k, rows], past.at[k, rows], across)

    def back_copy(step):
        return copy(RX + step, ship.at[step], ret.at[step], across)

    def back_mate(step):
        return copy(RF + step, ret.at[step], ret_mate.at[step], partner)

    def edge_back(k, source):
        return copy(RE + k, source, ret_edge.at[k], beside)

    early_slot = slots - 1

    def send(step):
        k = chunk_of(step)

        @pl.when(step < STEPS)
        def _():
            for block in range(2):
                mate_copy(k, block).wait_recv()

        right_out = flag_at(step, 0)
        mate_right = flag_at(step, 2)
        mate_left = flag_at(step, 3)
        guest_in = flag_at(step, 4)

        def one(i, carry):
            at = pl.ds(pl.multiple_of(i * 16, 16), 16)
            mine = pl.ds(pl.multiple_of(k * CHUNK + core * PIECE + i * 16, 16), 16)
            value = jnp.where(right_out == 1, units[1, mine, :], units[0, mine, :])
            value = jnp.where(mate_right == 1, mate[k, 1, at, :], value)
            value = jnp.where(mate_left == 1, mate[k, 0, at, :], value)
            offer[step, at, :] = value
            return carry

        lax.fori_loop(0, PIECE // 16, one, 0)
        if edges:

            @pl.when(is_host & (step >= early_slot * STEPS))
            def _():
                pre_recv(k).wait_recv()

                def swap(i, carry):
                    at = pl.ds(pl.multiple_of(i * 16, 16), 16)
                    offer[step, at, :] = jnp.where(guest_in == 1, pre[k, at, :], offer[step, at, :])
                    return carry

                lax.fori_loop(0, PIECE // 16, swap, 0)

        cross_copy(step).start()

    def tile(row, column_units, scale):
        cosine = lax.dot_general(
            units[row, :, :bins],
            column_units,
            (((1,), (1,)), ((), ())),
            preferred_element_type=jnp.float32,
        )
        return (cosine * cosine * cosine * scale).astype(jnp.bfloat16)

    def ahead(weight, column_scores):
        extended = jnp.concatenate([column_scores, jnp.ones_like(column_scores)], axis=1)
        return jnp.dot(weight, extended, preferred_element_type=jnp.float32)

    def local_pairs():
        def one(row, carry):
            own[row] = ahead(tile(row, units[row, :, :bins], 1.0), units[row, :, bins:])
            other = 1 - row
            own[row] += ahead(tile(row, units[other, :, :bins], inside), units[other, :, bins:])
            return carry

        lax.fori_loop(0, 2, one, 0)

    def chunk_pairs(read, scale0, scale1, target):
        part[...] = jnp.zeros_like(part)

        def one(row, carry):
            scale = jnp.where(row == 0, scale0, scale1).astype(jnp.float32)
            weight = tile(row, read(slice(0, bins)), scale)
            own[row] += ahead(weight, read(slice(bins, bins + feat)))
            part[:CHUNK, :] += lax.dot_general(
                weight,
                units[row, :, bins:],
                (((0,), (0,)), ((), ())),
                preferred_element_type=jnp.float32,
            )
            part[CHUNK:, :] += jnp.dot(
                jnp.ones((8, BLOCK), jnp.bfloat16), weight, preferred_element_type=jnp.float32
            )
            return carry

        lax.fori_loop(0, 2, one, 0)
        target[:CHUNK, :] = part[:CHUNK, :].astype(jnp.bfloat16)
        line = part[CHUNK:, :]
        high_part = line.astype(jnp.bfloat16).astype(jnp.float32)
        target[CHUNK:, :] = jnp.concatenate([high_part, line - high_part], axis=0).astype(jnp.bfloat16)

    def add_back(k, lines, scale0, scale1):
        rows = pl.ds(pl.multiple_of(k * CHUNK, CHUNK), CHUNK)
        sums = lines[:CHUNK, :].astype(jnp.float32)
        line = lines[CHUNK:, :].astype(jnp.float32)
        line = line[0:1, :] + line[8:9, :]
        degree = jnp.broadcast_to(line, (CHUNK, CHUNK)).T
        for block, scale in enumerate((scale0, scale1)):
            own[block, rows, :feat] += sums * scale
            own[block, rows, feat:] += degree * scale

    greetings = 2
    if edges:
        greetings = (
            2 + jnp.where(has_edge, 1, 0) + jnp.where(is_edge, 2, 0) + jnp.where(is_host, 1, 0)
        )

    def prepare(k, carry):
        normalize(k)

        @pl.when(k == 0)
        def _():
            pl.semaphore_wait(barrier, greetings)

        for block in range(2):
            mate_copy(k, block).start()
        if edges:

            @pl.when(is_edge)
            def _():
                for which in range(2):
                    pre_copy(k, which).start()

        @pl.when(k < AHEAD)
        def _():
            send(k)

        return carry

    lax.fori_loop(0, STEPS, prepare, 0)
    local_pairs()

    def edge_step(k):
        for which in range(2):
            post_recv(k, which).wait_recv()
        first = edge_right_in + edge_left_in * close0
        second = edge_right_in + edge_left_in * close1
        chunk_pairs(lambda columns: past[k, :, columns], first, second, ship_edge.at[k])
        edge_back(k, ship_edge.at[k]).start()

    def step_fn(step, carry):
        @pl.when(step < total_steps)
        def _():
            cross_copy(step).wait_recv()
            forward_copy(step).start()
            if edges:

                @pl.when(is_host & (step < STEPS))
                def _():
                    post_copy(step).start()

            @pl.when(step + AHEAD < total_steps)
            def _():
                send(step + AHEAD)

            forward_wait(step)
            right_in = flag_at(step, 5)
            left_in = flag_at(step, 6)
            first = right_in + left_in * close0
            second = right_in + left_in * close1
            chunk_pairs(lambda columns: got[step, :, columns], first, second, ship.at[step])
            back_copy(step).start()
            if edges:

                @pl.when(has_edge & odd_group & (step >= early_slot * STEPS))
                def _():
                    edge_back(chunk_of(step), ship.at[step]).start()

        if edges:

            @pl.when(is_edge & (step >= STEPS - 1) & (step < 2 * STEPS - 1))
            def _():
                edge_step(step - (STEPS - 1))

        @pl.when((step >= 1) & (step <= total_steps))
        def _():
            back_copy(step - 1).wait_recv()
            back_mate(step - 1).start()

        @pl.when(step >= 2)
        def _():
            done = step - 2
            back_mate(done).wait_recv()
            scale0 = flag_at(done, 1).astype(jnp.float32)
            scale1 = flag_at(done, 0).astype(jnp.float32)
            both = ret[done].astype(jnp.float32) + ret_mate[done].astype(jnp.float32)
            add_back(chunk_of(done), both, scale0, scale1)

        return carry

    def forward_wait(step):
        rows = pl.ds(pl.multiple_of((1 - core) * PIECE, PIECE), PIECE)
        copy(FW + step, got.at[step, rows], got.at[step, rows], partner).wait_recv()

    last = max(total_steps + 2, 2 * STEPS - 1 if edges else 0)
    lax.fori_loop(0, last, step_fn, 0)

    if edges:

        @pl.when(has_edge)
        def _():
            def one(k, carry):
                edge_back(k, ship_edge.at[k]).wait_recv()
                add_back(k, ret_edge[k], edge_out0, edge_out1)
                return carry

            lax.fori_loop(0, STEPS, one, 0)

    for block in range(2):
        out[block * BLOCK : (block + 1) * BLOCK, :] = own[block, :, :feat] / own[block, :, feat:]

    def finish(step, carry):
        cross_copy(step).wait_send()
        forward_copy(step).wait_send()
        back_copy(step).wait_send()
        back_mate(step).wait_send()
        return carry

    lax.fori_loop(0, total_steps, finish, 0)

    def finish_chunk(k, carry):
        for block in range(2):
            mate_copy(k, block).wait_send()
        if edges:

            @pl.when(has_edge)
            def _():
                edge_back(k, ship_edge.at[k]).wait_send()

            @pl.when(is_edge)
            def _():
                for which in range(2):
                    pre_copy(k, which).wait_send()

            @pl.when(is_host)
            def _():
                post_copy(k).wait_send()

        return carry

    lax.fori_loop(0, STEPS, finish_chunk, 0)


def slots_plan(slots, edges, spectra, scores, reach):
    rows, bins = spectra.shape
    feat = scores.shape[1]
    width = bins + feat
    steps = slots * STEPS
    extra = STEPS if edges else 1
    vmem = pl.BlockSpec(memory_space=pltpu.VMEM)
    bf16 = jnp.bfloat16
    return pl.pallas_call(
        functools.partial(slots_kernel, slots, edges),
        out_shape=jax.ShapeDtypeStruct((rows, feat), jnp.float32),
        in_specs=[pl.BlockSpec(memory_space=pltpu.SMEM), pl.BlockSpec(memory_space=pltpu.HBM), vmem],
        out_specs=vmem,
        scratch_shapes=[
            pltpu.VMEM((rows, bins), bf16),
            pltpu.VMEM((2, BLOCK, width), bf16),
            pltpu.VMEM((STEPS, 2, PIECE, width), bf16),
            pltpu.VMEM((extra, PIECE, width), bf16),
            pltpu.VMEM((steps, PIECE, width), bf16),
            pltpu.VMEM((steps, CHUNK, width), bf16),
            pltpu.VMEM((extra, CHUNK, width), bf16),
            pltpu.VMEM((2, BLOCK, 2 * feat), jnp.float32),
            pltpu.VMEM((CHUNK + 8, feat), jnp.float32),
            pltpu.VMEM((steps, LINES, feat), bf16),
            pltpu.VMEM((extra, LINES, feat), bf16),
            pltpu.VMEM((steps, LINES, feat), bf16),
            pltpu.VMEM((steps, LINES, feat), bf16),
            pltpu.VMEM((extra, LINES, feat), bf16),
            pltpu.SemaphoreType.DMA((2 * STEPS,)),
            pltpu.SemaphoreType.DMA((60,)),
            pltpu.SemaphoreType.DMA((60,)),
        ],
        compiler_params=pltpu.CompilerParams(
            collective_id=4 + 2 * (slots - 1) + int(edges),
            has_side_effects=True,
            vmem_limit_bytes=48 * 2**20,
        ),
        cost_estimate=pl.CostEstimate(
            flops=8 * 2 * BLOCK * BLOCK * bins,
            bytes_accessed=2 * rows * width,
            transcendentals=rows * bins,
        ),
        name="slots",
    )(reach, spectra, scores)


def choose(reach):
    size = reach.shape[0]
    group = 2 * GROUP
    padded = jnp.pad(reach, (2, group))

    def at(shift):
        return padded[2 + shift : 2 + shift + size]

    def right(boundary):
        return jnp.where(at(2 * boundary + 1) == 2, 1, 0)

    def left(boundary):
        return jnp.where((at(2 * boundary) == 2) | (at(2 * boundary + 1) == 1), 1, 0)

    index = lax.iota(jnp.int32, size)
    lead = lax.rem(index, group) == 0
    hosts = jnp.where(lax.rem(index, 2 * group) == group, 1, 0)
    going = right(0) + left(1) + right(2) + hosts * (left(-1) + left(3))
    coming = left(0) + right(1) + left(2) + hosts * (right(-1) + right(3))
    load = jnp.maximum(going, coming)
    edge = right(3) + left(3)
    level = jnp.where(load > 2, 2, jnp.where((load > 1) | (edge > 0), 1, 0))
    return jnp.max(jnp.where(lead, level, 0)).astype(jnp.int32)


def body(spectra, class_scores, reach):
    if reach.shape[0] % 16:
        return plan(True, True, spectra, class_scores, reach)
    branches = [
        functools.partial(slots_plan, 1, False),
        functools.partial(slots_plan, 2, True),
        functools.partial(plan, True, True),
    ]
    return lax.switch(choose(reach), branches, spectra, class_scores, reach)


def solution(mesh):
    return jax.shard_map(
        body,
        mesh=mesh,
        in_specs=(P(AXES, None), P(AXES, None), P()),
        out_specs=P(AXES, None),
        check_vma=False,
    )
```

```python
import functools

import jax
import jax.numpy as jnp
from jax import lax
from jax.experimental import pallas as pl
from jax.experimental.pallas import tpu as pltpu
from jax.sharding import PartitionSpec as P

BLOCK = 512
AXES = ("blk", "sub")
GROUP = 4
MESH = pl.DeviceIdType.MESH
HALF = BLOCK // 2
PART = HALF + 16 * (HALF // 128)
SHIP = 2 * PART
NEAR, FAR, EDGE = 2, 3, 4


def kernel(two_blocks, group_edge, reach, spectra, scores, out, units, own, part, ship, ret, offer, kept,
           send_sem, recv_sem):
    bins = spectra.shape[1]
    feat = scores.shape[1]
    subs = lax.axis_size("sub")
    count = lax.axis_size("blk") * subs
    position = lax.axis_index("blk") * subs + lax.axis_index("sub")
    place = lax.rem(position, GROUP)
    odd = lax.rem(place, 2)
    across = position + 1 - 2 * odd
    core = jnp.where(place < 2, position + 2, position - 2)
    beside = position - 1 + 2 * odd
    middle = (place == 1) | (place == 2)
    outer = jnp.logical_not(middle)
    low = place < 2
    high = jnp.logical_not(low)
    has_edge = ((place == 0) & (position > 0)) | ((place == 3) & (position < count - 1))
    first = odd
    second = 1 - odd

    def copy(index, source, target, device):
        return pltpu.make_async_remote_copy(
            src_ref=source,
            dst_ref=target,
            send_sem=send_sem.at[index],
            recv_sem=recv_sem.at[index],
            device_id=(device // subs, lax.rem(device, subs)),
            device_id_type=MESH,
        )

    barrier = pltpu.get_barrier_semaphore()

    def greet(device):
        pl.semaphore_signal(
            barrier,
            inc=1,
            device_id=(device // subs, lax.rem(device, subs)),
            device_id_type=MESH,
        )

    greet(across)
    greet(core)
    beside_used = middle if two_blocks else (place < 0)
    if group_edge:
        beside_used = beside_used | has_edge

    @pl.when(beside_used)
    def _():
        greet(beside)

    def normalize(block):
        def step(i, carry):
            rows = pl.ds(pl.multiple_of(i * 64, 64), 64)
            source = pl.ds(pl.multiple_of(block * BLOCK + i * 64, 64), 64)
            values = spectra[source, :].astype(jnp.float32)
            total = jnp.sum(values, axis=1, keepdims=True)
            unit = jnp.sqrt(values) * (1.0 / jnp.sqrt(total + 1e-06))
            units[block, rows, :bins] = unit.astype(jnp.bfloat16)
            units[block, rows, bins:] = scores[source, :]
            return carry

        lax.fori_loop(0, BLOCK // 64, step, 0)

    def own_reach(index):
        return reach[2 * position + index]

    previous = jnp.maximum(2 * position - 2, 0)

    def flag(condition):
        return jnp.where(condition, 1.0, 0.0).astype(jnp.float32)

    to_next0 = flag(own_reach(0) >= 2)
    to_next1 = flag(own_reach(1) >= 1)
    to_next2 = flag(own_reach(1) >= 2)
    from_prev0 = flag(reach[previous] >= 2)
    from_prev1 = flag(reach[previous + 1] >= 1)
    from_prev2 = flag(reach[previous + 1] >= 2)
    inside = flag(own_reach(0) >= 1)

    def weights(row, column, scale, start=0, size=BLOCK):
        cosine = lax.dot_general(
            units[row, :, :bins],
            units[column, start : start + size, :bins],
            (((1,), (1,)), ((), ())),
            preferred_element_type=jnp.float32,
        )
        return (cosine * cosine * cosine * scale).astype(jnp.bfloat16)

    def forward(column, weight, start=0, size=BLOCK):
        column_scores = units[column, start : start + size, bins:]
        extended = jnp.concatenate([column_scores, jnp.ones_like(column_scores)], axis=1)
        return jnp.dot(weight, extended, preferred_element_type=jnp.float32)

    def local_pairs():
        def step(row, carry):
            own[row] = forward(row, weights(row, row, 1.0))
            own[row] += forward(1 - row, weights(row, 1 - row, inside))
            return carry

        lax.fori_loop(0, 2, step, 0)

    def remote_pairs(column, slot, scale0, scale1, halves=(0, 1)):
        start, size = halves[0] * HALF, HALF * len(halves)
        part[...] = jnp.zeros_like(part)

        def step(row, carry):
            scale = jnp.where(row == 0, scale0, scale1)
            weight = weights(row, column, scale, start, size)
            own[row] += forward(column, weight, start, size)
            part[:size, :] += lax.dot_general(
                weight,
                units[row, :, bins:],
                (((0,), (0,)), ((), ())),
                preferred_element_type=jnp.float32,
            )
            sums = jnp.dot(
                jnp.ones((8, BLOCK), jnp.bfloat16), weight, preferred_element_type=jnp.float32
            )
            for q in range(size // 128):
                part[BLOCK + 8 * q : BLOCK + 8 * q + 8, :] += sums[:, 128 * q : 128 * q + 128]
            return carry

        lax.fori_loop(0, 2, step, 0)
        for place_in, half in enumerate(halves):
            base = half * PART
            ship[slot, base : base + HALF, :] = part[
                place_in * HALF : place_in * HALF + HALF, :
            ].astype(jnp.bfloat16)
            for q in range(HALF // 128):
                row = BLOCK + 8 * (place_in * (HALF // 128) + q)
                line = part[row : row + 8, :]
                high_part = line.astype(jnp.bfloat16).astype(jnp.float32)
                ship[slot, base + HALF + 16 * q : base + HALF + 16 * q + 16, :] = jnp.concatenate(
                    [high_part, line - high_part], axis=0
                ).astype(jnp.bfloat16)

    def add_back(block, slot, scale=1.0, halves=(0, 1)):
        for half in halves:
            base = half * PART
            rows = slice(half * HALF, half * HALF + HALF)
            own[block, rows, :feat] += ret[slot, base : base + HALF, :].astype(jnp.float32) * scale
            for q in range(HALF // 128):
                line = ret[slot, base + HALF + 16 * q : base + HALF + 16 * q + 16, :]
                line = line.astype(jnp.float32)
                line = (line[0:1, :] + line[8:9, :]) * scale
                rows = slice(half * HALF + 128 * q, half * HALF + 128 * q + 128)
                own[block, rows, feat:] += jnp.broadcast_to(line, (128, 128)).T

    if group_edge:
        edge_copy = copy(0, units.at[first], units.at[EDGE], beside)
        edge_back = copy(1, ship.at[2], ret.at[2], beside)

    normalize(first)

    @pl.when(beside_used)
    def _():
        pl.semaphore_wait(barrier, 3)

    @pl.when(jnp.logical_not(beside_used))
    def _():
        pl.semaphore_wait(barrier, 2)

    if two_blocks:
        first_copy = copy(2, units.at[first], units.at[NEAR], across)
        second_copies = [
            copy(
                3 + 5 * h,
                units.at[second, pl.ds(h * HALF, HALF)],
                units.at[FAR, pl.ds(h * HALF, HALF)],
                across,
            )
            for h in range(2)
        ]
        pass_copy = copy(4, units.at[NEAR], units.at[NEAR], core)
        first_back = copy(5, ship.at[0], ret.at[0], across)
        second_backs = [
            copy(
                6 + 3 * h,
                ship.at[1, pl.ds(h * PART, PART)],
                ret.at[1, pl.ds(h * PART, PART)],
                across,
            )
            for h in range(2)
        ]
        beside_back = copy(7, ship.at[0], ret.at[2], beside)

        @pl.when(middle)
        def _():
            first_copy.start()

    if group_edge:

        @pl.when(has_edge)
        def _():
            edge_copy.start()

    normalize(second)

    def edge_pairs():
        @pl.when(has_edge)
        def _():
            edge_copy.wait_recv()
            is_left = place == 3
            remote_pairs(
                EDGE,
                2,
                jnp.where(is_left, to_next0, 0.0),
                jnp.where(is_left, to_next1, from_prev2),
            )
            edge_back.start()

    def edge_end():
        @pl.when(has_edge)
        def _():
            edge_back.wait_recv()
            add_back(first, 2)
            edge_copy.wait_send()
            edge_back.wait_send()

    if two_blocks:
        local_pairs()

        @pl.when(middle)
        def _():
            first_copy.wait_send()
            for half in range(2):
                second_copies[half].start()
            pass_copy.wait_recv()
            is_left = place == 1
            remote_pairs(
                NEAR,
                0,
                jnp.where(is_left, to_next0, 0.0),
                jnp.where(is_left, to_next1, from_prev2),
            )
            beside_back.start()
            beside_back.wait_recv()
            add_back(first, 2)
            first_back.wait_recv()
            add_back(first, 0)
            for half in range(2):
                second_copies[half].wait_send()
                second_backs[half].wait_recv()
                add_back(second, 1, halves=(half,))
            beside_back.wait_send()

        @pl.when(outer)
        def _():
            first_copy.wait_recv()
            pass_copy.start()
            is_left = place == 0
            remote_pairs(
                NEAR,
                0,
                jnp.where(is_left, 0.0, from_prev0),
                jnp.where(is_left, to_next2, 0.0),
            )
            first_back.start()

        if group_edge:
            edge_pairs()

        @pl.when(outer)
        def _():
            is_left = place == 0
            for half in range(2):
                second_copies[half].wait_recv()
                remote_pairs(
                    FAR,
                    1,
                    jnp.where(is_left, to_next0, from_prev1),
                    jnp.where(is_left, to_next1, from_prev2),
                    halves=(half,),
                )
                second_backs[half].start()
            pass_copy.wait_send()
            first_back.wait_send()
            for half in range(2):
                second_backs[half].wait_send()

    else:
        leads = jnp.where(place < 3, jnp.maximum(to_next0, to_next1), 0.0)
        follows = jnp.where(place > 0, jnp.maximum(from_prev0, from_prev1), 0.0)
        has_role = jnp.maximum(leads, follows)
        gather_copies, cross_copies, pass_copies = [], [], []
        for half in range(2):
            rows = pl.ds(half * HALF, HALF)
            near = units.at[NEAR, rows]
            gather_copies.append(copy(2 + 6 * half, offer.at[rows], kept.at[rows], core))
            cross_copies.append(copy(3 + 6 * half, offer.at[rows], near, across))
            pass_copies.append(copy(4 + 6 * half, near, near, core))
        gather_back = copy(5, ship.at[0], ret.at[0], core)
        cross_back = copy(6, ship.at[0], ret.at[1], across)
        pass_back = copy(7, ret.at[1], ret.at[1], core)

        def blend(target, yes, no, scale, rows):
            def step(i, carry):
                chunk = pl.ds(pl.multiple_of(i * rows, rows), rows)
                a = yes[chunk, :].astype(jnp.float32) * scale
                b = no[chunk, :].astype(jnp.float32) * (1.0 - scale)
                target[chunk, :] = (a + b).astype(target.dtype)
                return carry

            lax.fori_loop(0, target.shape[0] // rows, step, 0)

        for half in range(2):
            rows = pl.ds(half * HALF, HALF)
            blend(offer.at[rows], units.at[1, rows], units.at[0, rows], leads, 64)

            @pl.when(high)
            def _():
                gather_copies[half].start()

        @pl.when(low)
        def _():
            for half in range(2):
                rows = pl.ds(half * HALF, HALF)
                gather_copies[half].wait_recv()
                blend(offer.at[rows], offer.at[rows], kept.at[rows], has_role, 64)
                cross_copies[half].start()

        local_pairs()

        @pl.when(low)
        def _():
            for half in range(2):
                cross_copies[half].wait_recv()
                pass_copies[half].start()

        @pl.when(high)
        def _():
            for half in range(2):
                pass_copies[half].wait_recv()

        remote_pairs(
            NEAR,
            0,
            jnp.where(place < 3, to_next0, 0.0) * leads,
            jnp.where(place < 3, to_next1, 0.0) * leads + from_prev2 * follows,
        )

        @pl.when(high)
        def _():
            gather_back.start()

        @pl.when(low)
        def _():
            gather_back.wait_recv()
            blend(ship.at[0], ship.at[0], ret.at[0], has_role, SHIP)
            cross_back.start()

        if group_edge:
            edge_pairs()

        @pl.when(low)
        def _():
            cross_back.wait_recv()
            pass_back.start()

        @pl.when(high)
        def _():
            pass_back.wait_recv()

        add_back(1, 1, leads)
        add_back(0, 1, follows)

        @pl.when(low)
        def _():
            for half in range(2):
                cross_copies[half].wait_send()
                pass_copies[half].wait_send()
            cross_back.wait_send()
            pass_back.wait_send()

        @pl.when(high)
        def _():
            for half in range(2):
                gather_copies[half].wait_send()
            gather_back.wait_send()

    if group_edge:
        edge_end()

    for block in range(2):
        out[block * BLOCK : (block + 1) * BLOCK, :] = own[block, :, :feat] / own[block, :, feat:]


def plan(two_blocks, group_edge, spectra, scores, reach):
    rows, bins = spectra.shape
    feat = scores.shape[1]
    width = bins + feat
    vmem = pl.BlockSpec(memory_space=pltpu.VMEM)
    return pl.pallas_call(
        functools.partial(kernel, two_blocks, group_edge),
        out_shape=jax.ShapeDtypeStruct((rows, feat), jnp.float32),
        in_specs=[pl.BlockSpec(memory_space=pltpu.SMEM), vmem, vmem],
        out_specs=vmem,
        scratch_shapes=[
            pltpu.VMEM((5, BLOCK, width), jnp.bfloat16),
            pltpu.VMEM((2, BLOCK, 2 * feat), jnp.float32),
            pltpu.VMEM((BLOCK + 8 * (BLOCK // 128), feat), jnp.float32),
            pltpu.VMEM((3, SHIP, feat), jnp.bfloat16),
            pltpu.VMEM((3, SHIP, feat), jnp.bfloat16),
            pltpu.VMEM((16 if two_blocks else BLOCK, width), jnp.bfloat16),
            pltpu.VMEM((16 if two_blocks else BLOCK, width), jnp.bfloat16),
            pltpu.SemaphoreType.DMA((12,)),
            pltpu.SemaphoreType.DMA((12,)),
        ],
        compiler_params=pltpu.CompilerParams(
            collective_id=2 * int(two_blocks) + int(group_edge),
            has_side_effects=True,
            vmem_limit_bytes=48 * 2**20,
        ),
        cost_estimate=pl.CostEstimate(
            flops=8 * 2 * BLOCK * BLOCK * bins,
            bytes_accessed=2 * rows * width,
            transcendentals=rows * bins,
        ),
        name="network",
    )(reach, spectra, scores)


CHUNK = 128
PIECE = CHUNK // 2
STEPS = BLOCK // CHUNK
LINES = CHUNK + 16
AHEAD = 2
DELAY = 3
EX, XS, FW, PRE, POST, RX, RF, RE = 0, 8, 16, 24, 32, 40, 48, 56


def slots_kernel(slots, edges, reach, spectra, scores, out, raw, units, mate, pre, offer, got, past, own, part, ship,
                 ship_edge, ret, ret_mate, ret_edge, load_sem, send_sem, recv_sem):
    bins = spectra.shape[1]
    feat = scores.shape[1]
    total_steps = slots * STEPS
    subs = lax.axis_size("sub")
    count = lax.axis_size("blk") * subs
    position = lax.axis_index("blk") * subs + lax.axis_index("sub")
    place = lax.rem(position, GROUP)
    group = position // GROUP
    side = lax.rem(place, 2)
    core = place // 2
    base = position - place
    odd_group = lax.rem(group, 2) == 1
    even_group = lax.rem(group, 2) == 0
    across = position + 1 - 2 * side
    partner = position + 2 - 4 * core
    at_end = (place == 0) | (place == 3)
    has_edge = ((place == 0) & (position > 0)) | ((place == 3) & (position < count - 1))
    beside = jnp.where(place == 0, position - 1, position + 1)
    is_edge = has_edge & even_group
    host = jnp.where(side == 0, base - GROUP, base + GROUP) + side
    is_host = odd_group & ((side == 1) | (base + GROUP < count))
    guest = jnp.where(side == 0, base + GROUP, base - GROUP + 3)

    def place_of(device):
        return (device // subs, lax.rem(device, subs))

    def copy(index, source, target, device):
        return pltpu.make_async_remote_copy(
            src_ref=source,
            dst_ref=target,
            send_sem=send_sem.at[index],
            recv_sem=recv_sem.at[index],
            device_id=place_of(device),
            device_id_type=MESH,
        )

    def load_copy(k, block):
        rows = pl.ds(pl.multiple_of(block * BLOCK + k * CHUNK, CHUNK), CHUNK)
        return pltpu.make_async_copy(spectra.at[rows], raw.at[rows], load_sem.at[2 * k + block])

    for k in range(STEPS):
        for block in range(2):
            load_copy(k, block).start()

    barrier = pltpu.get_barrier_semaphore()

    def greet(device):
        pl.semaphore_signal(barrier, inc=1, device_id=place_of(device), device_id_type=MESH)

    greet(across)
    greet(partner)
    if edges:

        @pl.when(has_edge)
        def _():
            greet(beside)

        @pl.when(is_edge)
        def _():
            greet(host)
            greet(host + 2)

        @pl.when(is_host)
        def _():
            greet(guest)

    def active(boundary):
        inside = (boundary >= 0) & (boundary < count - 1)
        at = jnp.clip(boundary, 0, count - 2)
        a, b = reach[2 * at], reach[2 * at + 1]
        right = jnp.where(inside & (b == 2), 1, 0)
        left = jnp.where(inside & ((a == 2) | (b == 1)), 1, 0)
        return right, left

    bounds = [active(base + i - 1) for i in range(5)]
    rights = [b[0] for b in bounds]
    lefts = [b[1] for b in bounds]
    hosts = jnp.where(odd_group, 1, 0) if edges else 0

    def assign(inner, late, early):
        d1, d2, d3 = inner
        if slots == 1:
            return ((d1, d2, d3, late * hosts, early * hosts),)
        late, early = late * hosts, early * hosts
        free = 1 - late
        f1 = d1 * free
        f2 = d2 * (1 - d1) * free
        f3 = d3 * (1 - d1) * (1 - d2) * free
        return ((f1, f2, f3, late, 0), (d1 - f1, d2 - f2, d3 - f3, 0, early))

    going = assign((rights[1], lefts[2], rights[3]), lefts[0], lefts[4])
    coming = assign((lefts[1], rights[2], lefts[3]), rights[4], rights[0])

    def pick(options, index):
        value = options[-1]
        for i in range(len(options) - 2, -1, -1):
            value = jnp.where(index == i, options[i], value)
        return value

    def slot_flags(slot):
        q, r = going[slot], coming[slot]
        right_out = pick([q[0], r[1], q[2], r[3]], place)
        left_out = pick([q[3], r[0], q[1], r[2]], place)
        mate_right = pick([q[2], r[3], q[0], r[1]], place)
        mate_left = pick([q[1], r[2], q[3], r[0]], place)
        guest_in = jnp.where(side == 0, q[4], r[4])
        right_in = pick([r[4], q[0], r[1], q[2]], place)
        left_in = pick([r[0], q[1], r[2], q[4]], place)
        return right_out, left_out, mate_right, mate_left, guest_in, right_in, left_in

    flags = [slot_flags(s) for s in range(slots)]

    def flag_at(step, which):
        if slots == 1:
            return flags[0][which]
        return jnp.where(step < STEPS, flags[0][which], flags[1][which])

    own0, own1 = reach[2 * position], reach[2 * position + 1]
    close0 = jnp.where(own0 == 2, 1, 0)
    close1 = jnp.where(own1 == 1, 1, 0)
    inside = jnp.where(own0 >= 1, 1.0, 0.0).astype(jnp.float32)

    edge_right_in = jnp.where(place == 0, rights[0], 0)
    edge_left_in = jnp.where(place == 3, lefts[4], 0)
    edge_out0 = jnp.where(place == 0, lefts[0], 0).astype(jnp.float32)
    edge_out1 = jnp.where(place == 3, rights[4], 0).astype(jnp.float32)

    def chunk_of(step):
        return lax.rem(step, STEPS)

    def normalize(k):
        def one(i, carry):
            block = i // 2
            row = k * CHUNK + lax.rem(i, 2) * 64
            rows = pl.ds(pl.multiple_of(row, 64), 64)
            source = pl.ds(pl.multiple_of(block * BLOCK + row, 64), 64)
            values = raw[source, :].astype(jnp.float32)
            total = jnp.sum(values, axis=1, keepdims=True)
            unit = jnp.sqrt(values) * (1.0 / jnp.sqrt(total + 1e-06))
            units[block, rows, :bins] = unit.astype(jnp.bfloat16)
            units[block, rows, bins:] = scores[source, :]
            return carry

        for block in range(2):
            load_copy(k, block).wait()
        lax.fori_loop(0, 4, one, 0)

    def piece(k, which):
        return pl.ds(pl.multiple_of(k * CHUNK + which * PIECE, PIECE), PIECE)

    def mate_copy(k, block):
        return copy(EX + 2 * k + block, units.at[block, piece(k, 1 - core)], mate.at[k, block], partner)

    def pre_copy(k, which):
        block = jnp.where(place == 0, 0, 1)
        return copy(PRE + 2 * k + which, units.at[block, piece(k, which)], pre.at[k], host + 2 * which)

    def pre_recv(k):
        return copy(PRE + 2 * k + core, pre.at[k], pre.at[k], across)

    def cross_copy(step):
        rows = pl.ds(pl.multiple_of(core * PIECE, PIECE), PIECE)
        return copy(XS + step, offer.at[step], got.at[step, rows], across)

    def forward_copy(step):
        rows = pl.ds(pl.multiple_of(core * PIECE, PIECE), PIECE)
        return copy(FW + step, got.at[step, rows], got.at[step, rows], partner)

    def post_copy(step):
        rows = pl.ds(pl.multiple_of(core * PIECE, PIECE), PIECE)
        return copy(POST + 2 * step + core, got.at[step, rows], past.at[step, rows], guest)

    def post_recv(k, which):
        rows = pl.ds(which * PIECE, PIECE)
        return copy(POST + 2 * k + which, past.at[k, rows], past.at[k, rows], across)

    def back_copy(step):
        return copy(RX + step, ship.at[step], ret.at[step], across)

    def back_mate(step):
        return copy(RF + step, ret.at[step], ret_mate.at[step], partner)

    def edge_back(k, source):
        return copy(RE + k, source, ret_edge.at[k], beside)

    early_slot = slots - 1

    def send(step):
        k = chunk_of(step)

        @pl.when(step < STEPS)
        def _():
            for block in range(2):
                mate_copy(k, block).wait_recv()

        right_out = flag_at(step, 0)
        mate_right = flag_at(step, 2)
        mate_left = flag_at(step, 3)
        guest_in = flag_at(step, 4)

        def one(i, carry):
            at = pl.ds(pl.multiple_of(i * 16, 16), 16)
            mine = pl.ds(pl.multiple_of(k * CHUNK + core * PIECE + i * 16, 16), 16)
            value = jnp.where(right_out == 1, units[1, mine, :], units[0, mine, :])
            value = jnp.where(mate_right == 1, mate[k, 1, at, :], value)
            value = jnp.where(mate_left == 1, mate[k, 0, at, :], value)
            offer[step, at, :] = value
            return carry

        lax.fori_loop(0, PIECE // 16, one, 0)
        if edges:

            @pl.when(is_host & (step >= early_slot * STEPS))
            def _():
                pre_recv(k).wait_recv()

                def swap(i, carry):
                    at = pl.ds(pl.multiple_of(i * 16, 16), 16)
                    offer[step, at, :] = jnp.where(guest_in == 1, pre[k, at, :], offer[step, at, :])
                    return carry

                lax.fori_loop(0, PIECE // 16, swap, 0)

        cross_copy(step).start()

    def tile(row, column_units, scale):
        cosine = lax.dot_general(
            units[row, :, :bins],
            column_units,
            (((1,), (1,)), ((), ())),
            preferred_element_type=jnp.float32,
        )
        return (cosine * cosine * cosine * scale).astype(jnp.bfloat16)

    def ahead(weight, column_scores):
        extended = jnp.concatenate([column_scores, jnp.ones_like(column_scores)], axis=1)
        return jnp.dot(weight, extended, preferred_element_type=jnp.float32)

    def local_pairs():
        def one(row, carry):
            own[row] = ahead(tile(row, units[row, :, :bins], 1.0), units[row, :, bins:])
            other = 1 - row
            own[row] += ahead(tile(row, units[other, :, :bins], inside), units[other, :, bins:])
            return carry

        lax.fori_loop(0, 2, one, 0)

    def chunk_pairs(read, scale0, scale1, target):
        part[...] = jnp.zeros_like(part)

        def one(row, carry):
            scale = jnp.where(row == 0, scale0, scale1).astype(jnp.float32)
            weight = tile(row, read(slice(0, bins)), scale)
            own[row] += ahead(weight, read(slice(bins, bins + feat)))
            part[:CHUNK, :] += lax.dot_general(
                weight,
                units[row, :, bins:],
                (((0,), (0,)), ((), ())),
                preferred_element_type=jnp.float32,
            )
            part[CHUNK:, :] += jnp.dot(
                jnp.ones((8, BLOCK), jnp.bfloat16), weight, preferred_element_type=jnp.float32
            )
            return carry

        lax.fori_loop(0, 2, one, 0)
        target[:CHUNK, :] = part[:CHUNK, :].astype(jnp.bfloat16)
        line = part[CHUNK:, :]
        high_part = line.astype(jnp.bfloat16).astype(jnp.float32)
        target[CHUNK:, :] = jnp.concatenate([high_part, line - high_part], axis=0).astype(jnp.bfloat16)

    def add_back(k, lines, scale0, scale1):
        rows = pl.ds(pl.multiple_of(k * CHUNK, CHUNK), CHUNK)
        sums = lines[:CHUNK, :].astype(jnp.float32)
        line = lines[CHUNK:, :].astype(jnp.float32)
        line = line[0:1, :] + line[8:9, :]
        degree = jnp.broadcast_to(line, (CHUNK, CHUNK)).T
        for block, scale in enumerate((scale0, scale1)):
            own[block, rows, :feat] += sums * scale
            own[block, rows, feat:] += degree * scale

    greetings = 2
    if edges:
        greetings = (
            2 + jnp.where(has_edge, 1, 0) + jnp.where(is_edge, 2, 0) + jnp.where(is_host, 1, 0)
        )

    def prepare(k, carry):
        normalize(k)

        @pl.when(k == 0)
        def _():
            pl.semaphore_wait(barrier, greetings)

        for block in range(2):
            mate_copy(k, block).start()
        if edges:

            @pl.when(is_edge)
            def _():
                for which in range(2):
                    pre_copy(k, which).start()

        @pl.when(k < AHEAD)
        def _():
            send(k)

        return carry

    lax.fori_loop(0, STEPS, prepare, 0)
    local_pairs()

    def edge_step(k):
        for which in range(2):
            post_recv(k, which).wait_recv()
        first = edge_right_in + edge_left_in * close0
        second = edge_right_in + edge_left_in * close1
        chunk_pairs(lambda columns: past[k, :, columns], first, second, ship_edge.at[k])
        edge_back(k, ship_edge.at[k]).start()

    def step_fn(step, carry):
        @pl.when(step < total_steps)
        def _():
            cross_copy(step).wait_recv()
            forward_copy(step).start()
            if edges:

                @pl.when(is_host & (step < STEPS))
                def _():
                    post_copy(step).start()

            @pl.when(step + AHEAD < total_steps)
            def _():
                send(step + AHEAD)

            forward_wait(step)
            right_in = flag_at(step, 5)
            left_in = flag_at(step, 6)
            first = right_in + left_in * close0
            second = right_in + left_in * close1
            chunk_pairs(lambda columns: got[step, :, columns], first, second, ship.at[step])
            back_copy(step).start()
            if edges:

                @pl.when(has_edge & odd_group & (step >= early_slot * STEPS))
                def _():
                    edge_back(chunk_of(step), ship.at[step]).start()

        if edges:

            @pl.when(is_edge & (step >= STEPS - 1) & (step < 2 * STEPS - 1))
            def _():
                edge_step(step - (STEPS - 1))

        @pl.when((step >= DELAY) & (step < total_steps + DELAY))
        def _():
            back_copy(step - DELAY).wait_recv()
            back_mate(step - DELAY).start()

        @pl.when(step > DELAY)
        def _():
            done = step - DELAY - 1
            back_mate(done).wait_recv()
            scale0 = flag_at(done, 1).astype(jnp.float32)
            scale1 = flag_at(done, 0).astype(jnp.float32)
            both = ret[done].astype(jnp.float32) + ret_mate[done].astype(jnp.float32)
            add_back(chunk_of(done), both, scale0, scale1)

        return carry

    def forward_wait(step):
        rows = pl.ds(pl.multiple_of((1 - core) * PIECE, PIECE), PIECE)
        copy(FW + step, got.at[step, rows], got.at[step, rows], partner).wait_recv()

    lax.fori_loop(0, total_steps + DELAY + 1, step_fn, 0)

    if edges:

        @pl.when(has_edge)
        def _():
            def one(k, carry):
                edge_back(k, ship_edge.at[k]).wait_recv()
                add_back(k, ret_edge[k], edge_out0, edge_out1)
                return carry

            lax.fori_loop(0, STEPS, one, 0)

    for block in range(2):
        out[block * BLOCK : (block + 1) * BLOCK, :] = own[block, :, :feat] / own[block, :, feat:]

    def finish(step, carry):
        cross_copy(step).wait_send()
        forward_copy(step).wait_send()
        back_copy(step).wait_send()
        back_mate(step).wait_send()
        return carry

    lax.fori_loop(0, total_steps, finish, 0)

    def finish_chunk(k, carry):
        for block in range(2):
            mate_copy(k, block).wait_send()
        if edges:

            @pl.when(has_edge)
            def _():
                edge_back(k, ship_edge.at[k]).wait_send()

            @pl.when(is_edge)
            def _():
                for which in range(2):
                    pre_copy(k, which).wait_send()

            @pl.when(is_host)
            def _():
                post_copy(k).wait_send()

        return carry

    lax.fori_loop(0, STEPS, finish_chunk, 0)


def slots_plan(slots, edges, spectra, scores, reach):
    rows, bins = spectra.shape
    feat = scores.shape[1]
    width = bins + feat
    steps = slots * STEPS
    extra = STEPS if edges else 1
    vmem = pl.BlockSpec(memory_space=pltpu.VMEM)
    bf16 = jnp.bfloat16
    return pl.pallas_call(
        functools.partial(slots_kernel, slots, edges),
        out_shape=jax.ShapeDtypeStruct((rows, feat), jnp.float32),
        in_specs=[pl.BlockSpec(memory_space=pltpu.SMEM), pl.BlockSpec(memory_space=pltpu.HBM), vmem],
        out_specs=vmem,
        scratch_shapes=[
            pltpu.VMEM((rows, bins), bf16),
            pltpu.VMEM((2, BLOCK, width), bf16),
            pltpu.VMEM((STEPS, 2, PIECE, width), bf16),
            pltpu.VMEM((extra, PIECE, width), bf16),
            pltpu.VMEM((steps, PIECE, width), bf16),
            pltpu.VMEM((steps, CHUNK, width), bf16),
            pltpu.VMEM((extra, CHUNK, width), bf16),
            pltpu.VMEM((2, BLOCK, 2 * feat), jnp.float32),
            pltpu.VMEM((CHUNK + 8, feat), jnp.float32),
            pltpu.VMEM((steps, LINES, feat), bf16),
            pltpu.VMEM((extra, LINES, feat), bf16),
            pltpu.VMEM((steps, LINES, feat), bf16),
            pltpu.VMEM((steps, LINES, feat), bf16),
            pltpu.VMEM((extra, LINES, feat), bf16),
            pltpu.SemaphoreType.DMA((2 * STEPS,)),
            pltpu.SemaphoreType.DMA((60,)),
            pltpu.SemaphoreType.DMA((60,)),
        ],
        compiler_params=pltpu.CompilerParams(
            collective_id=4 + 2 * (slots - 1) + int(edges),
            has_side_effects=True,
            vmem_limit_bytes=48 * 2**20,
        ),
        cost_estimate=pl.CostEstimate(
            flops=8 * 2 * BLOCK * BLOCK * bins,
            bytes_accessed=2 * rows * width,
            transcendentals=rows * bins,
        ),
        name="slots",
    )(reach, spectra, scores)


TICKS = 2 * STEPS
QUARTER = CHUNK // 4
LEAD = 3
OPEN = 2
P_EX, P_XS, P_FW, P_RX, P_RF, P_PRE, P_POST, P_PF, P_RE = 0, 8, 16, 24, 32, 40, 44, 48, 52


def pair_kernel(parity, reach, spectra, scores, out, raw, units, mate, lend, borrow, offer, offer_pair, got, own, part,
                ship, ret, ret_mate, ret_edge, load_sem, send_sem, recv_sem):
    bins = spectra.shape[1]
    feat = scores.shape[1]
    subs = lax.axis_size("sub")
    count = lax.axis_size("blk") * subs
    position = lax.axis_index("blk") * subs + lax.axis_index("sub")
    place = lax.rem(position, GROUP)
    group = position // GROUP
    side = lax.rem(place, 2)
    core = place // 2
    base = position - place
    upper = lax.rem(group + parity, 2)
    across = position + 1 - 2 * side
    partner = position + 2 - 4 * core
    shift = jnp.where(upper == 1, count - GROUP, GROUP)
    pair = lax.rem(position + shift, count)
    pair_base = pair - place
    low_base = jnp.where(upper == 1, pair_base, base)

    def place_of(device):
        return (device // subs, lax.rem(device, subs))

    def copy(index, source, target, device):
        return pltpu.make_async_remote_copy(
            src_ref=source,
            dst_ref=target,
            send_sem=send_sem.at[index],
            recv_sem=recv_sem.at[index],
            device_id=place_of(device),
            device_id_type=MESH,
        )

    def load_copy(k, block):
        rows = pl.ds(pl.multiple_of(block * BLOCK + k * CHUNK, CHUNK), CHUNK)
        return pltpu.make_async_copy(spectra.at[rows], raw.at[rows], load_sem.at[2 * k + block])

    for k in range(STEPS):
        for block in range(2):
            load_copy(k, block).start()

    barrier = pltpu.get_barrier_semaphore()
    for device in (across, partner, pair):
        pl.semaphore_signal(barrier, inc=1, device_id=place_of(device), device_id_type=MESH)

    def active(boundary):
        within = boundary < count - 1
        at = jnp.minimum(boundary, count - 2)
        a, b = reach[2 * at], reach[2 * at + 1]
        right = jnp.where(within & (b == 2), 1, 0)
        left = jnp.where(within & ((a == 2) | (b == 1)), 1, 0)
        return right, left

    def lanes(first):
        (r0, l0), (r1, l1), (r2, l2) = [active(first + i) for i in range(3)]
        result = []
        for d1, d2, d3 in ((r0, l1, r2), (l0, r1, l2)):
            f1, f2, f3 = d1, d2 * (1 - d1), d3 * (1 - d1) * (1 - d2)
            result.append(((f1, f2, f3), (d1 - f1, d2 - f2, d3 - f3)))
        return result

    going, coming = lanes(base)
    pair_going, pair_coming = lanes(pair_base)
    edge_right, edge_left = active(low_base + 3)
    up = upper
    down = 1 - upper

    def pick(options):
        value = options[-1]
        for i in range(len(options) - 2, -1, -1):
            value = jnp.where(place == i, options[i], value)
        return value

    def lane_flags(which):
        q, r = going[which], coming[which]
        last = 1 if which else 0
        right_out = pick([q[0], r[1], q[2], 0])
        left_out = pick([0, r[0], q[1], r[2]])
        mate_right = pick([q[2], last * edge_right * down, q[0], r[1]])
        mate_left = pick([q[1], r[2], last * edge_left * up, r[0]])
        right_in = pick([last * edge_right * up, q[0], r[1], q[2]])
        left_in = pick([r[0], q[1], r[2], last * edge_left * down])
        return right_out, left_out, mate_right, mate_left, right_in, left_in

    own_lane, pair_lane = lane_flags(0), lane_flags(1)
    edge_out0 = jnp.where(place == 0, edge_left * up, 0)
    edge_out1 = jnp.where(place == 3, edge_right * down, 0)
    pair_sum = jnp.where(
        side == 0,
        sum(pair_going[1]) + edge_left * down,
        sum(pair_coming[1]) + edge_right * up,
    )

    own0, own1 = reach[2 * position], reach[2 * position + 1]
    close0 = jnp.where(own0 == 2, 1, 0)
    close1 = jnp.where(own1 == 1, 1, 0)
    inside = jnp.where(own0 >= 1, 1.0, 0.0).astype(jnp.float32)

    sends_edge = ((upper == 0) & (place == 0)) | ((upper == 1) & (place == 3))
    takes_edge = ((upper == 1) & (place == 0)) | ((upper == 0) & (place == 3))

    def shared(tick):
        return (tick >= OPEN) & (tick < OPEN + STEPS)

    def alone(tick):
        return ((tick >= 0) & (tick < OPEN)) | ((tick >= OPEN + STEPS) & (tick < TICKS))

    def chunk_of(tick):
        return jnp.where(tick < OPEN, tick, tick - STEPS)

    def normalize(k):
        def one(i, carry):
            block = i // 2
            row = k * CHUNK + lax.rem(i, 2) * 64
            source = pl.ds(pl.multiple_of(block * BLOCK + row, 64), 64)
            values = raw[source, :].astype(jnp.float32)
            total = jnp.sum(values, axis=1, keepdims=True)
            unit = jnp.sqrt(values) * (1.0 / jnp.sqrt(total + 1e-06))
            units[source, :bins] = unit.astype(jnp.bfloat16)
            units[source, bins:] = scores[source, :]
            return carry

        for block in range(2):
            load_copy(k, block).wait()
        lax.fori_loop(0, 4, one, 0)

    def half_rows(tick, which):
        return got.at[pl.ds(pl.multiple_of(tick * CHUNK + which * PIECE, PIECE), PIECE)]

    def quarter_rows(tick, which, level):
        start = tick * CHUNK + which * PIECE + level * QUARTER
        return got.at[pl.ds(pl.multiple_of(start, QUARTER), QUARTER)]

    def mate_copy(k, block):
        rows = pl.ds(pl.multiple_of(block * BLOCK + k * CHUNK + (1 - core) * PIECE, PIECE), PIECE)
        return copy(P_EX + 2 * k + block, units.at[rows], mate.at[k, block], partner)

    def pre_copy(k):
        return copy(P_PRE + k, lend.at[k], borrow.at[k], pair)

    def cross_alone(tick):
        return copy(P_XS + tick, offer.at[chunk_of(tick)], half_rows(tick, core), across)

    def cross_shared(tick):
        return copy(P_XS + tick, offer_pair.at[tick - OPEN], quarter_rows(tick, core, upper), across)

    def forward_alone(tick, which):
        rows = half_rows(tick, which)
        return copy(P_FW + tick, rows, rows, partner)

    def forward_shared(tick, which):
        rows = quarter_rows(tick, which, upper)
        return copy(P_FW + tick, rows, rows, partner)

    def post_copy(k, level):
        rows = quarter_rows(k + OPEN, core, level)
        return copy(P_POST + k, rows, rows, pair)

    def post_forward(k, which):
        rows = quarter_rows(k + OPEN, which, 1 - upper)
        return copy(P_PF + k, rows, rows, partner)

    def back_copy(tick):
        return copy(P_RX + tick, ship.at[tick], ret.at[tick], across)

    def back_mate(tick):
        return copy(P_RF + tick, ret.at[tick], ret_mate.at[tick], partner)

    def edge_back(k):
        return copy(P_RE + k, ret_mate.at[k + OPEN], ret_edge.at[k], pair)

    def choose_rows(flags, k, start, i):
        right_out, left_out, mate_right, mate_left = flags
        at = pl.ds(pl.multiple_of(start + i * 16, 16), 16)
        first = k * CHUNK + core * PIECE + start + i * 16
        mine0 = pl.ds(pl.multiple_of(first, 16), 16)
        mine1 = pl.ds(pl.multiple_of(BLOCK + first, 16), 16)
        value = jnp.where(right_out == 1, units[mine1, :], units[mine0, :])
        value = jnp.where(mate_right == 1, mate[k, 1, at, :], value)
        return jnp.where(mate_left == 1, mate[k, 0, at, :], value)

    pair_right_out = pair_lane[0] + edge_out1
    pair_flags = (pair_right_out,) + pair_lane[1:4]

    def offer_to_pair(k):
        def one(i, carry):
            rows = pl.ds(pl.multiple_of(i * 16, 16), 16)
            lend[k, rows, :] = choose_rows(pair_flags, k, (1 - upper) * QUARTER, i)
            return carry

        lax.fori_loop(0, QUARTER // 16, one, 0)
        pre_copy(k).start()

    def send_alone(tick):
        k = chunk_of(tick)

        def one(i, carry):
            rows = pl.ds(pl.multiple_of(i * 16, 16), 16)
            offer[k, rows, :] = choose_rows(own_lane[:4], k, 0, i)
            return carry

        lax.fori_loop(0, PIECE // 16, one, 0)
        cross_alone(tick).start()

    def send_shared(tick):
        k = tick - OPEN
        pre_copy(k).wait_recv()

        def one(i, carry):
            rows = pl.ds(pl.multiple_of(i * 16, 16), 16)
            value = choose_rows(pair_flags, k, upper * QUARTER, i)
            offer_pair[k, rows, :] = jnp.where(pair_sum > 0, borrow[k, rows, :], value)
            return carry

        lax.fori_loop(0, QUARTER // 16, one, 0)
        cross_shared(tick).start()

    def send(tick):
        @pl.when(alone(tick))
        def _():
            send_alone(tick)

        @pl.when(shared(tick))
        def _():
            send_shared(tick)

    def local_pairs():
        def one(row, carry):
            rows = pl.ds(pl.multiple_of(row * BLOCK, BLOCK), BLOCK)
            cosine = lax.dot_general(
                units[rows, :bins],
                units[:, :bins],
                (((1,), (1,)), ((), ())),
                preferred_element_type=jnp.float32,
            )
            column = lax.broadcasted_iota(jnp.int32, (1, 2 * BLOCK), 1) // BLOCK
            scale = jnp.where(column == row, 1.0, inside)
            weight = (cosine * cosine * cosine * scale).astype(jnp.bfloat16)
            extended = jnp.concatenate([units[:, bins:], jnp.ones((2 * BLOCK, feat), jnp.bfloat16)], axis=1)
            own[rows, :] = jnp.dot(weight, extended, preferred_element_type=jnp.float32)
            return carry

        lax.fori_loop(0, 2, one, 0)

    def chunk_pairs(tick, chunks, flags):
        first = (flags[4] + flags[5] * close0).astype(jnp.float32)
        second = (flags[4] + flags[5] * close1).astype(jnp.float32)
        size = chunks * CHUNK
        rows = pl.ds(pl.multiple_of(tick * CHUNK, CHUNK), size)
        cosine = lax.dot_general(
            got[rows, :bins],
            units[:, :bins],
            (((1,), (1,)), ((), ())),
            preferred_element_type=jnp.float32,
        )
        column = lax.broadcasted_iota(jnp.int32, (1, 2 * BLOCK), 1)
        scale = jnp.where(column < BLOCK, first, second)
        weight = (cosine * cosine * cosine * scale).astype(jnp.bfloat16)
        extended = jnp.concatenate([units[:, bins:], jnp.ones((2 * BLOCK, feat), jnp.bfloat16)], axis=1)
        part[:size, :] = jnp.dot(weight, extended, preferred_element_type=jnp.float32)
        extended = jnp.concatenate([got[rows, bins:], jnp.ones((size, feat), jnp.bfloat16)], axis=1)
        own[...] += lax.dot_general(
            weight, extended, (((0,), (0,)), ((), ())), preferred_element_type=jnp.float32
        )
        for i in range(chunks):
            lines = slice(i * CHUNK, i * CHUNK + CHUNK)
            ship[tick + i, :CHUNK, :] = part[lines, :feat].astype(jnp.bfloat16)
            line = part[lines, feat:].T[:8, :]
            high_part = line.astype(jnp.bfloat16).astype(jnp.float32)
            ship[tick + i, CHUNK:, :] = jnp.concatenate([high_part, line - high_part], axis=0).astype(
                jnp.bfloat16
            )
            back_copy(tick + i).start()

    def add_back(k, lines, scale0, scale1):
        sums = lines[:CHUNK, :].astype(jnp.float32)
        line = lines[CHUNK:, :].astype(jnp.float32)
        line = line[0:1, :] + line[8:9, :]
        degree = jnp.broadcast_to(line, (CHUNK, CHUNK)).T
        for block, scale in enumerate((scale0, scale1)):
            factor = scale.astype(jnp.float32)
            rows = pl.ds(pl.multiple_of(block * BLOCK + k * CHUNK, CHUNK), CHUNK)
            own[rows, :feat] += sums * factor
            own[rows, feat:] += degree * factor

    def prepare(k, carry):
        normalize(k)

        @pl.when(k == 0)
        def _():
            pl.semaphore_wait(barrier, 3)

        for block in range(2):
            mate_copy(k, block).start()

        @pl.when(k == 0)
        def _():
            lend_rows(0)
            send_alone(0)

        @pl.when(k >= 2)
        def _():
            lend_rows(k - 1)
            send(k - 1)

        return carry

    def lend_rows(k):
        for block in range(2):
            mate_copy(k, block).wait_recv()
        offer_to_pair(k)

    lax.fori_loop(0, STEPS, prepare, 0)
    lend_rows(STEPS - 1)
    local_pairs()

    def shared_pairs(k):
        for i in range(2):
            forward_shared(k + i + OPEN, 1 - core).wait_recv()
            post_forward(k + i, 1 - core).wait_recv()
        chunk_pairs(k + OPEN, 2, pair_lane)

    def collect(tick):
        back_copy(tick).wait_recv()
        back_mate(tick).start()

    def tick_fn(tick, carry):
        @pl.when((tick >= OPEN + 1) & (tick < OPEN + 1 + STEPS))
        def _():
            post_copy(tick - OPEN - 1, 1 - upper).wait_recv()
            post_forward(tick - OPEN - 1, core).start()

        @pl.when(tick == TICKS - 1)
        def _():
            forward_alone(TICKS - 2, 1 - core).wait_recv()
            chunk_pairs(TICKS - 2, 1, own_lane)

        @pl.when(alone(tick))
        def _():
            cross_alone(tick).wait_recv()
            forward_alone(tick, core).start()

        @pl.when(shared(tick))
        def _():
            cross_shared(tick).wait_recv()
            forward_shared(tick, core).start()
            post_copy(tick - OPEN, upper).start()

        @pl.when(tick + LEAD < TICKS)
        def _():
            send(tick + LEAD)

        @pl.when(tick == OPEN)
        def _():
            for i in range(OPEN):
                forward_alone(i, 1 - core).wait_recv()
            chunk_pairs(0, 2, own_lane)

        @pl.when((tick == OPEN + 3) | (tick == OPEN + 4))
        def _():
            shared_pairs(2 * (tick - OPEN - 3))

        @pl.when(tick == TICKS - 1)
        def _():
            forward_alone(TICKS - 1, 1 - core).wait_recv()
            chunk_pairs(TICKS - 1, 1, own_lane)

        return carry

    lax.fori_loop(0, TICKS, tick_fn, 0)

    def collect_fn(tick, carry):
        collect(tick)
        return carry

    lax.fori_loop(0, TICKS - 1, collect_fn, 0)

    def gather(done, k, flags):
        back_mate(done).wait_recv()
        both = ret[done].astype(jnp.float32) + ret_mate[done].astype(jnp.float32)
        add_back(k, both, flags[1], flags[0])

    def shared_fn(k, carry):
        gather(k + OPEN, k, pair_lane)

        @pl.when(sends_edge)
        def _():
            edge_back(k).start()

        return carry

    lax.fori_loop(0, STEPS, shared_fn, 0)

    def alone_fn(k, carry):
        gather(jnp.where(k < OPEN, k, k + STEPS), k, own_lane)
        return carry

    lax.fori_loop(0, STEPS - 1, alone_fn, 0)
    collect(TICKS - 1)
    @pl.when(takes_edge)
    def _():
        def one(k, carry):
            edge_back(k).wait_recv()
            add_back(k, ret_edge[k], edge_out0, edge_out1)
            return carry

        lax.fori_loop(0, STEPS, one, 0)

    gather(TICKS - 1, STEPS - 1, own_lane)
    out[...] = own[:, :feat] / own[:, feat:]

    def finish(tick, carry):
        @pl.when(alone(tick))
        def _():
            cross_alone(tick).wait_send()
            forward_alone(tick, core).wait_send()

        @pl.when(shared(tick))
        def _():
            cross_shared(tick).wait_send()
            forward_shared(tick, core).wait_send()

        back_copy(tick).wait_send()
        back_mate(tick).wait_send()
        return carry

    lax.fori_loop(0, TICKS, finish, 0)

    def finish_chunk(k, carry):
        for block in range(2):
            mate_copy(k, block).wait_send()
        pre_copy(k).wait_send()
        post_copy(k, upper).wait_send()
        post_forward(k, core).wait_send()

        @pl.when(sends_edge)
        def _():
            edge_back(k).wait_send()

        return carry

    lax.fori_loop(0, STEPS, finish_chunk, 0)


def pair_plan(parity, spectra, scores, reach):
    rows, bins = spectra.shape
    feat = scores.shape[1]
    width = bins + feat
    vmem = pl.BlockSpec(memory_space=pltpu.VMEM)
    bf16 = jnp.bfloat16
    return pl.pallas_call(
        functools.partial(pair_kernel, parity),
        out_shape=jax.ShapeDtypeStruct((rows, feat), jnp.float32),
        in_specs=[pl.BlockSpec(memory_space=pltpu.SMEM), pl.BlockSpec(memory_space=pltpu.HBM), vmem],
        out_specs=vmem,
        scratch_shapes=[
            pltpu.VMEM((rows, bins), bf16),
            pltpu.VMEM((rows, width), bf16),
            pltpu.VMEM((STEPS, 2, PIECE, width), bf16),
            pltpu.VMEM((STEPS, QUARTER, width), bf16),
            pltpu.VMEM((STEPS, QUARTER, width), bf16),
            pltpu.VMEM((STEPS, PIECE, width), bf16),
            pltpu.VMEM((STEPS, QUARTER, width), bf16),
            pltpu.VMEM((TICKS * CHUNK, width), bf16),
            pltpu.VMEM((rows, 2 * feat), jnp.float32),
            pltpu.VMEM((2 * CHUNK, 2 * feat), jnp.float32),
            pltpu.VMEM((TICKS, LINES, feat), bf16),
            pltpu.VMEM((TICKS, LINES, feat), bf16),
            pltpu.VMEM((TICKS, LINES, feat), bf16),
            pltpu.VMEM((STEPS, LINES, feat), bf16),
            pltpu.SemaphoreType.DMA((2 * STEPS,)),
            pltpu.SemaphoreType.DMA((56,)),
            pltpu.SemaphoreType.DMA((56,)),
        ],
        compiler_params=pltpu.CompilerParams(
            collective_id=8 + parity,
            has_side_effects=True,
            vmem_limit_bytes=48 * 2**20,
        ),
        cost_estimate=pl.CostEstimate(
            flops=8 * 2 * BLOCK * BLOCK * bins,
            bytes_accessed=2 * rows * width,
            transcendentals=rows * bins,
        ),
        name="pairs",
    )(reach, spectra, scores)


def branch(reach):
    size = reach.shape[0]
    group = 2 * GROUP
    margin = 2
    padded = jnp.pad(reach, (margin, 2 * group))
    index = lax.iota(jnp.int32, size)

    def at(shift):
        return padded[margin + shift : margin + shift + size]

    def right(boundary):
        return jnp.where(at(2 * boundary + 1) == 2, 1, 0)

    def left(boundary):
        return jnp.where((at(2 * boundary) == 2) | (at(2 * boundary + 1) == 1), 1, 0)

    def lanes(first):
        going = right(first) + left(first + 1) + right(first + 2)
        coming = left(first) + right(first + 1) + left(first + 2)
        return going, coming

    def over(lane):
        return jnp.maximum(lane - 1, 0)

    def flag(condition, place):
        return jnp.where(condition, 2**place, 0)

    odd = lax.rem(index, 2 * group) == group
    hosts = jnp.where(odd, 1, 0)
    going, coming = lanes(0)
    next_going, next_coming = lanes(GROUP)
    edge_right, edge_left = right(3), left(3)
    edge = edge_right + edge_left > 0
    over_going, over_coming = over(going), over(coming)
    shared = jnp.maximum(
        over_going + over(next_going) + edge_left, over_coming + over(next_coming) + edge_right
    )
    two = jnp.maximum(going + hosts * (left(-1) + edge_left), coming + hosts * (right(-1) + edge_right))
    full = over_going + over_coming > 0
    ends = (index == 0) | (index == size - group)
    tally = (
        flag(full | edge, 0)
        + flag(jnp.where(odd, edge, shared > 1), 7)
        + flag(jnp.where(odd, shared > 1, edge), 14)
        + flag(two > 2, 21)
        + flag(full & ends, 28)
    )
    total = jnp.sum(jnp.where(lax.rem(index, group) == 0, tally, 0))

    def count(place):
        return lax.shift_right_logical(total, place) & 127

    chosen = jnp.where(count(21) == 0, 3, 4)
    chosen = jnp.where((count(14) == 0) & (count(28) < 2), 2, chosen)
    chosen = jnp.where(count(7) == 0, 1, chosen)
    return jnp.where(count(0) == 0, 0, chosen).astype(jnp.int32)


def body(spectra, class_scores, reach):
    if reach.shape[0] % 16:
        return plan(True, True, spectra, class_scores, reach)
    branches = [
        functools.partial(slots_plan, 1, False),
        functools.partial(pair_plan, 0),
        functools.partial(pair_plan, 1),
        functools.partial(slots_plan, 2, True),
        functools.partial(plan, True, True),
    ]
    return lax.switch(branch(reach), branches, spectra, class_scores, reach)


def solution(mesh):
    return jax.shard_map(
        body,
        mesh=mesh,
        in_specs=(P(AXES, None), P(AXES, None), P()),
        out_specs=P(AXES, None),
        check_vma=False,
    )
```

```python
import functools

import jax
import jax.numpy as jnp
from jax import lax
from jax.experimental import pallas as pl
from jax.experimental.pallas import tpu as pltpu
from jax.sharding import PartitionSpec as P

BLOCK = 512
AXES = ("blk", "sub")
GROUP = 4
MESH = pl.DeviceIdType.MESH
HALF = BLOCK // 2
PART = HALF + 16 * (HALF // 128)
SHIP = 2 * PART
NEAR, FAR, EDGE = 2, 3, 4


def kernel(two_blocks, group_edge, reach, spectra, scores, out, units, own, part, ship, ret, offer, kept,
           send_sem, recv_sem):
    bins = spectra.shape[1]
    feat = scores.shape[1]
    subs = lax.axis_size("sub")
    count = lax.axis_size("blk") * subs
    position = lax.axis_index("blk") * subs + lax.axis_index("sub")
    place = lax.rem(position, GROUP)
    odd = lax.rem(place, 2)
    across = position + 1 - 2 * odd
    core = jnp.where(place < 2, position + 2, position - 2)
    beside = position - 1 + 2 * odd
    middle = (place == 1) | (place == 2)
    outer = jnp.logical_not(middle)
    low = place < 2
    high = jnp.logical_not(low)
    has_edge = ((place == 0) & (position > 0)) | ((place == 3) & (position < count - 1))
    first = odd
    second = 1 - odd

    def copy(index, source, target, device):
        return pltpu.make_async_remote_copy(
            src_ref=source,
            dst_ref=target,
            send_sem=send_sem.at[index],
            recv_sem=recv_sem.at[index],
            device_id=(device // subs, lax.rem(device, subs)),
            device_id_type=MESH,
        )

    barrier = pltpu.get_barrier_semaphore()

    def greet(device):
        pl.semaphore_signal(
            barrier,
            inc=1,
            device_id=(device // subs, lax.rem(device, subs)),
            device_id_type=MESH,
        )

    greet(across)
    greet(core)
    beside_used = middle if two_blocks else (place < 0)
    if group_edge:
        beside_used = beside_used | has_edge

    @pl.when(beside_used)
    def _():
        greet(beside)

    def normalize(block):
        def step(i, carry):
            rows = pl.ds(pl.multiple_of(i * 64, 64), 64)
            source = pl.ds(pl.multiple_of(block * BLOCK + i * 64, 64), 64)
            values = spectra[source, :].astype(jnp.float32)
            total = jnp.sum(values, axis=1, keepdims=True)
            unit = jnp.sqrt(values) * (1.0 / jnp.sqrt(total + 1e-06))
            units[block, rows, :bins] = unit.astype(jnp.bfloat16)
            units[block, rows, bins:] = scores[source, :]
            return carry

        lax.fori_loop(0, BLOCK // 64, step, 0)

    def own_reach(index):
        return reach[2 * position + index]

    previous = jnp.maximum(2 * position - 2, 0)

    def flag(condition):
        return jnp.where(condition, 1.0, 0.0).astype(jnp.float32)

    to_next0 = flag(own_reach(0) >= 2)
    to_next1 = flag(own_reach(1) >= 1)
    to_next2 = flag(own_reach(1) >= 2)
    from_prev0 = flag(reach[previous] >= 2)
    from_prev1 = flag(reach[previous + 1] >= 1)
    from_prev2 = flag(reach[previous + 1] >= 2)
    inside = flag(own_reach(0) >= 1)

    def weights(row, column, scale, start=0, size=BLOCK):
        cosine = lax.dot_general(
            units[row, :, :bins],
            units[column, start : start + size, :bins],
            (((1,), (1,)), ((), ())),
            preferred_element_type=jnp.float32,
        )
        return (cosine * cosine * cosine * scale).astype(jnp.bfloat16)

    def forward(column, weight, start=0, size=BLOCK):
        column_scores = units[column, start : start + size, bins:]
        extended = jnp.concatenate([column_scores, jnp.ones_like(column_scores)], axis=1)
        return jnp.dot(weight, extended, preferred_element_type=jnp.float32)

    def local_pairs():
        def step(row, carry):
            own[row] = forward(row, weights(row, row, 1.0))
            own[row] += forward(1 - row, weights(row, 1 - row, inside))
            return carry

        lax.fori_loop(0, 2, step, 0)

    def remote_pairs(column, slot, scale0, scale1, halves=(0, 1)):
        start, size = halves[0] * HALF, HALF * len(halves)
        part[...] = jnp.zeros_like(part)

        def step(row, carry):
            scale = jnp.where(row == 0, scale0, scale1)
            weight = weights(row, column, scale, start, size)
            own[row] += forward(column, weight, start, size)
            part[:size, :] += lax.dot_general(
                weight,
                units[row, :, bins:],
                (((0,), (0,)), ((), ())),
                preferred_element_type=jnp.float32,
            )
            sums = jnp.dot(
                jnp.ones((8, BLOCK), jnp.bfloat16), weight, preferred_element_type=jnp.float32
            )
            for q in range(size // 128):
                part[BLOCK + 8 * q : BLOCK + 8 * q + 8, :] += sums[:, 128 * q : 128 * q + 128]
            return carry

        lax.fori_loop(0, 2, step, 0)
        for place_in, half in enumerate(halves):
            base = half * PART
            ship[slot, base : base + HALF, :] = part[
                place_in * HALF : place_in * HALF + HALF, :
            ].astype(jnp.bfloat16)
            for q in range(HALF // 128):
                row = BLOCK + 8 * (place_in * (HALF // 128) + q)
                line = part[row : row + 8, :]
                high_part = line.astype(jnp.bfloat16).astype(jnp.float32)
                ship[slot, base + HALF + 16 * q : base + HALF + 16 * q + 16, :] = jnp.concatenate(
                    [high_part, line - high_part], axis=0
                ).astype(jnp.bfloat16)

    def add_back(block, slot, scale=1.0, halves=(0, 1)):
        for half in halves:
            base = half * PART
            rows = slice(half * HALF, half * HALF + HALF)
            own[block, rows, :feat] += ret[slot, base : base + HALF, :].astype(jnp.float32) * scale
            for q in range(HALF // 128):
                line = ret[slot, base + HALF + 16 * q : base + HALF + 16 * q + 16, :]
                line = line.astype(jnp.float32)
                line = (line[0:1, :] + line[8:9, :]) * scale
                rows = slice(half * HALF + 128 * q, half * HALF + 128 * q + 128)
                own[block, rows, feat:] += jnp.broadcast_to(line, (128, 128)).T

    if group_edge:
        edge_copy = copy(0, units.at[first], units.at[EDGE], beside)
        edge_back = copy(1, ship.at[2], ret.at[2], beside)

    normalize(first)

    @pl.when(beside_used)
    def _():
        pl.semaphore_wait(barrier, 3)

    @pl.when(jnp.logical_not(beside_used))
    def _():
        pl.semaphore_wait(barrier, 2)

    if two_blocks:
        first_copy = copy(2, units.at[first], units.at[NEAR], across)
        second_copies = [
            copy(
                3 + 5 * h,
                units.at[second, pl.ds(h * HALF, HALF)],
                units.at[FAR, pl.ds(h * HALF, HALF)],
                across,
            )
            for h in range(2)
        ]
        pass_copy = copy(4, units.at[NEAR], units.at[NEAR], core)
        first_back = copy(5, ship.at[0], ret.at[0], across)
        second_backs = [
            copy(
                6 + 3 * h,
                ship.at[1, pl.ds(h * PART, PART)],
                ret.at[1, pl.ds(h * PART, PART)],
                across,
            )
            for h in range(2)
        ]
        beside_back = copy(7, ship.at[0], ret.at[2], beside)

        @pl.when(middle)
        def _():
            first_copy.start()

    if group_edge:

        @pl.when(has_edge)
        def _():
            edge_copy.start()

    normalize(second)

    def edge_pairs():
        @pl.when(has_edge)
        def _():
            edge_copy.wait_recv()
            is_left = place == 3
            remote_pairs(
                EDGE,
                2,
                jnp.where(is_left, to_next0, 0.0),
                jnp.where(is_left, to_next1, from_prev2),
            )
            edge_back.start()

    def edge_end():
        @pl.when(has_edge)
        def _():
            edge_back.wait_recv()
            add_back(first, 2)
            edge_copy.wait_send()
            edge_back.wait_send()

    if two_blocks:
        local_pairs()

        @pl.when(middle)
        def _():
            first_copy.wait_send()
            for half in range(2):
                second_copies[half].start()
            pass_copy.wait_recv()
            is_left = place == 1
            remote_pairs(
                NEAR,
                0,
                jnp.where(is_left, to_next0, 0.0),
                jnp.where(is_left, to_next1, from_prev2),
            )
            beside_back.start()
            beside_back.wait_recv()
            add_back(first, 2)
            first_back.wait_recv()
            add_back(first, 0)
            for half in range(2):
                second_copies[half].wait_send()
                second_backs[half].wait_recv()
                add_back(second, 1, halves=(half,))
            beside_back.wait_send()

        @pl.when(outer)
        def _():
            first_copy.wait_recv()
            pass_copy.start()
            is_left = place == 0
            remote_pairs(
                NEAR,
                0,
                jnp.where(is_left, 0.0, from_prev0),
                jnp.where(is_left, to_next2, 0.0),
            )
            first_back.start()

        if group_edge:
            edge_pairs()

        @pl.when(outer)
        def _():
            is_left = place == 0
            for half in range(2):
                second_copies[half].wait_recv()
                remote_pairs(
                    FAR,
                    1,
                    jnp.where(is_left, to_next0, from_prev1),
                    jnp.where(is_left, to_next1, from_prev2),
                    halves=(half,),
                )
                second_backs[half].start()
            pass_copy.wait_send()
            first_back.wait_send()
            for half in range(2):
                second_backs[half].wait_send()

    else:
        leads = jnp.where(place < 3, jnp.maximum(to_next0, to_next1), 0.0)
        follows = jnp.where(place > 0, jnp.maximum(from_prev0, from_prev1), 0.0)
        has_role = jnp.maximum(leads, follows)
        gather_copies, cross_copies, pass_copies = [], [], []
        for half in range(2):
            rows = pl.ds(half * HALF, HALF)
            near = units.at[NEAR, rows]
            gather_copies.append(copy(2 + 6 * half, offer.at[rows], kept.at[rows], core))
            cross_copies.append(copy(3 + 6 * half, offer.at[rows], near, across))
            pass_copies.append(copy(4 + 6 * half, near, near, core))
        gather_back = copy(5, ship.at[0], ret.at[0], core)
        cross_back = copy(6, ship.at[0], ret.at[1], across)
        pass_back = copy(7, ret.at[1], ret.at[1], core)

        def blend(target, yes, no, scale, rows):
            def step(i, carry):
                chunk = pl.ds(pl.multiple_of(i * rows, rows), rows)
                a = yes[chunk, :].astype(jnp.float32) * scale
                b = no[chunk, :].astype(jnp.float32) * (1.0 - scale)
                target[chunk, :] = (a + b).astype(target.dtype)
                return carry

            lax.fori_loop(0, target.shape[0] // rows, step, 0)

        for half in range(2):
            rows = pl.ds(half * HALF, HALF)
            blend(offer.at[rows], units.at[1, rows], units.at[0, rows], leads, 64)

            @pl.when(high)
            def _():
                gather_copies[half].start()

        @pl.when(low)
        def _():
            for half in range(2):
                rows = pl.ds(half * HALF, HALF)
                gather_copies[half].wait_recv()
                blend(offer.at[rows], offer.at[rows], kept.at[rows], has_role, 64)
                cross_copies[half].start()

        local_pairs()

        @pl.when(low)
        def _():
            for half in range(2):
                cross_copies[half].wait_recv()
                pass_copies[half].start()

        @pl.when(high)
        def _():
            for half in range(2):
                pass_copies[half].wait_recv()

        remote_pairs(
            NEAR,
            0,
            jnp.where(place < 3, to_next0, 0.0) * leads,
            jnp.where(place < 3, to_next1, 0.0) * leads + from_prev2 * follows,
        )

        @pl.when(high)
        def _():
            gather_back.start()

        @pl.when(low)
        def _():
            gather_back.wait_recv()
            blend(ship.at[0], ship.at[0], ret.at[0], has_role, SHIP)
            cross_back.start()

        if group_edge:
            edge_pairs()

        @pl.when(low)
        def _():
            cross_back.wait_recv()
            pass_back.start()

        @pl.when(high)
        def _():
            pass_back.wait_recv()

        add_back(1, 1, leads)
        add_back(0, 1, follows)

        @pl.when(low)
        def _():
            for half in range(2):
                cross_copies[half].wait_send()
                pass_copies[half].wait_send()
            cross_back.wait_send()
            pass_back.wait_send()

        @pl.when(high)
        def _():
            for half in range(2):
                gather_copies[half].wait_send()
            gather_back.wait_send()

    if group_edge:
        edge_end()

    for block in range(2):
        out[block * BLOCK : (block + 1) * BLOCK, :] = own[block, :, :feat] / own[block, :, feat:]


def plan(two_blocks, group_edge, spectra, scores, reach):
    rows, bins = spectra.shape
    feat = scores.shape[1]
    width = bins + feat
    vmem = pl.BlockSpec(memory_space=pltpu.VMEM)
    return pl.pallas_call(
        functools.partial(kernel, two_blocks, group_edge),
        out_shape=jax.ShapeDtypeStruct((rows, feat), jnp.float32),
        in_specs=[pl.BlockSpec(memory_space=pltpu.SMEM), vmem, vmem],
        out_specs=vmem,
        scratch_shapes=[
            pltpu.VMEM((5, BLOCK, width), jnp.bfloat16),
            pltpu.VMEM((2, BLOCK, 2 * feat), jnp.float32),
            pltpu.VMEM((BLOCK + 8 * (BLOCK // 128), feat), jnp.float32),
            pltpu.VMEM((3, SHIP, feat), jnp.bfloat16),
            pltpu.VMEM((3, SHIP, feat), jnp.bfloat16),
            pltpu.VMEM((16 if two_blocks else BLOCK, width), jnp.bfloat16),
            pltpu.VMEM((16 if two_blocks else BLOCK, width), jnp.bfloat16),
            pltpu.SemaphoreType.DMA((12,)),
            pltpu.SemaphoreType.DMA((12,)),
        ],
        compiler_params=pltpu.CompilerParams(
            collective_id=2 * int(two_blocks) + int(group_edge),
            has_side_effects=True,
            vmem_limit_bytes=48 * 2**20,
        ),
        cost_estimate=pl.CostEstimate(
            flops=8 * 2 * BLOCK * BLOCK * bins,
            bytes_accessed=2 * rows * width,
            transcendentals=rows * bins,
        ),
        name="network",
    )(reach, spectra, scores)


CHUNK = 128
PIECE = CHUNK // 2
STEPS = BLOCK // CHUNK
LINES = CHUNK + 16
AHEAD = 2
DELAY = 3
EX, XS, FW, PRE, POST, RX, RF, RE = 0, 8, 16, 24, 32, 40, 48, 56


def slots_kernel(slots, edges, reach, spectra, marks, out, raw, scores, units, mate, pre, offer, got, past, own, part, ship,
                 ship_edge, ret, ret_mate, ret_edge, load_sem, send_sem, recv_sem):
    bins = spectra.shape[1]
    feat = marks.shape[1]
    total_steps = slots * STEPS
    subs = lax.axis_size("sub")
    count = lax.axis_size("blk") * subs
    position = lax.axis_index("blk") * subs + lax.axis_index("sub")
    place = lax.rem(position, GROUP)
    group = position // GROUP
    side = lax.rem(place, 2)
    core = place // 2
    base = position - place
    odd_group = lax.rem(group, 2) == 1
    even_group = lax.rem(group, 2) == 0
    across = position + 1 - 2 * side
    partner = position + 2 - 4 * core
    corner = across + 2 - 4 * core
    at_end = (place == 0) | (place == 3)
    has_edge = ((place == 0) & (position > 0)) | ((place == 3) & (position < count - 1))
    beside = jnp.where(place == 0, position - 1, position + 1)
    is_edge = has_edge & even_group
    host = jnp.where(side == 0, base - GROUP, base + GROUP) + side
    is_host = odd_group & ((side == 1) | (base + GROUP < count))
    guest = jnp.where(side == 0, base + GROUP, base - GROUP + 3)

    def place_of(device):
        return (device // subs, lax.rem(device, subs))

    def copy(index, source, target, device):
        return pltpu.make_async_remote_copy(
            src_ref=source,
            dst_ref=target,
            send_sem=send_sem.at[index],
            recv_sem=recv_sem.at[index],
            device_id=place_of(device),
            device_id_type=MESH,
        )

    def load_copy(k, block):
        rows = pl.ds(pl.multiple_of(block * BLOCK + k * CHUNK, CHUNK), CHUNK)
        return pltpu.make_async_copy(spectra.at[rows], raw.at[rows], load_sem.at[2 * k + block])

    mark_copy = pltpu.make_async_copy(marks, scores, load_sem.at[2 * STEPS])
    for block in range(2):
        load_copy(0, block).start()
    mark_copy.start()
    for k in range(1, STEPS):
        for block in range(2):
            load_copy(k, block).start()

    barrier = pltpu.get_barrier_semaphore()

    def greet(device):
        pl.semaphore_signal(barrier, inc=1, device_id=place_of(device), device_id_type=MESH)

    greet(across)
    greet(partner)
    greet(corner)
    if edges:

        @pl.when(has_edge)
        def _():
            greet(beside)

        @pl.when(is_edge)
        def _():
            greet(host)
            greet(host + 2)

        @pl.when(is_host)
        def _():
            greet(guest)

    def active(boundary):
        inside = (boundary >= 0) & (boundary < count - 1)
        at = jnp.clip(boundary, 0, count - 2)
        a, b = reach[2 * at], reach[2 * at + 1]
        right = jnp.where(inside & (b == 2), 1, 0)
        left = jnp.where(inside & ((a == 2) | (b == 1)), 1, 0)
        return right, left

    bounds = [active(base + i - 1) for i in range(5)]
    rights = [b[0] for b in bounds]
    lefts = [b[1] for b in bounds]
    hosts = jnp.where(odd_group, 1, 0) if edges else 0

    def assign(inner, late, early):
        d1, d2, d3 = inner
        if slots == 1:
            return ((d1, d2, d3, late * hosts, early * hosts),)
        late, early = late * hosts, early * hosts
        free = 1 - late
        f1 = d1 * free
        f2 = d2 * (1 - d1) * free
        f3 = d3 * (1 - d1) * (1 - d2) * free
        return ((f1, f2, f3, late, 0), (d1 - f1, d2 - f2, d3 - f3, 0, early))

    going = assign((rights[1], lefts[2], rights[3]), lefts[0], lefts[4])
    coming = assign((lefts[1], rights[2], lefts[3]), rights[4], rights[0])

    def pick(options, index):
        value = options[-1]
        for i in range(len(options) - 2, -1, -1):
            value = jnp.where(index == i, options[i], value)
        return value

    def slot_flags(slot):
        q, r = going[slot], coming[slot]
        right_out = pick([q[0], r[1], q[2], r[3]], place)
        left_out = pick([q[3], r[0], q[1], r[2]], place)
        mate_right = pick([q[2], r[3], q[0], r[1]], place)
        mate_left = pick([q[1], r[2], q[3], r[0]], place)
        guest_in = jnp.where(side == 0, q[4], r[4])
        right_in = pick([r[4], q[0], r[1], q[2]], place)
        left_in = pick([r[0], q[1], r[2], q[4]], place)
        return right_out, left_out, mate_right, mate_left, guest_in, right_in, left_in

    flags = [slot_flags(s) for s in range(slots)]

    def flag_at(step, which):
        if slots == 1:
            return flags[0][which]
        return jnp.where(step < STEPS, flags[0][which], flags[1][which])

    own0, own1 = reach[2 * position], reach[2 * position + 1]
    close0 = jnp.where(own0 == 2, 1, 0)
    close1 = jnp.where(own1 == 1, 1, 0)
    inside = jnp.where(own0 >= 1, 1.0, 0.0).astype(jnp.float32)

    edge_right_in = jnp.where(place == 0, rights[0], 0)
    edge_left_in = jnp.where(place == 3, lefts[4], 0)
    edge_out0 = jnp.where(place == 0, lefts[0], 0).astype(jnp.float32)
    edge_out1 = jnp.where(place == 3, rights[4], 0).astype(jnp.float32)

    def chunk_of(step):
        return lax.rem(step, STEPS)

    def normalize(k, which):
        def one(block, carry):
            row = k * CHUNK + which * PIECE
            rows = pl.ds(pl.multiple_of(row, 64), 64)
            source = pl.ds(pl.multiple_of(block * BLOCK + row, 64), 64)
            values = raw[source, :].astype(jnp.float32)
            total = jnp.sum(values, axis=1, keepdims=True)
            unit = jnp.sqrt(values) * (1.0 / jnp.sqrt(total + 1e-06))
            units[block, rows, :bins] = unit.astype(jnp.bfloat16)
            units[block, rows, bins:] = scores[source, :]
            return carry

        lax.fori_loop(0, 2, one, 0)

    def piece(k, which):
        return pl.ds(pl.multiple_of(k * CHUNK + which * PIECE, PIECE), PIECE)

    def mate_copy(k, block):
        return copy(EX + 2 * k + block, units.at[block, piece(k, 1 - core)], mate.at[k, block], partner)

    def pre_copy(k, which):
        block = jnp.where(place == 0, 0, 1)
        return copy(PRE + 2 * k + which, units.at[block, piece(k, which)], pre.at[k], host + 2 * which)

    def pre_recv(k):
        return copy(PRE + 2 * k + core, pre.at[k], pre.at[k], across)

    def cross_copy(step):
        rows = pl.ds(pl.multiple_of(core * PIECE, PIECE), PIECE)
        return copy(XS + step, offer.at[step], got.at[step, rows], across)

    def forward_copy(step):
        rows = pl.ds(pl.multiple_of(core * PIECE, PIECE), PIECE)
        return copy(FW + step, got.at[step, rows], got.at[step, rows], partner)

    def post_copy(step):
        rows = pl.ds(pl.multiple_of(core * PIECE, PIECE), PIECE)
        return copy(POST + 2 * step + core, got.at[step, rows], past.at[step, rows], guest)

    def post_recv(k, which):
        rows = pl.ds(which * PIECE, PIECE)
        return copy(POST + 2 * k + which, past.at[k, rows], past.at[k, rows], across)

    def back_copy(step):
        return copy(RX + step, ship.at[step], ret.at[step], across)

    def back_mate(step):
        return copy(RF + step, ret.at[step], ret_mate.at[step], partner)

    final = total_steps - 1

    def back_corner():
        return copy(RF + final, ship.at[final], ret_mate.at[final], corner)

    def edge_back(k, source):
        return copy(RE + k, source, ret_edge.at[k], beside)

    early_slot = slots - 1

    def send(step):
        k = chunk_of(step)

        @pl.when(step < STEPS)
        def _():
            for block in range(2):
                mate_copy(k, block).wait_recv()

        right_out = flag_at(step, 0)
        mate_right = flag_at(step, 2)
        mate_left = flag_at(step, 3)
        guest_in = flag_at(step, 4)

        def one(i, carry):
            at = pl.ds(pl.multiple_of(i * 16, 16), 16)
            mine = pl.ds(pl.multiple_of(k * CHUNK + core * PIECE + i * 16, 16), 16)
            value = jnp.where(right_out == 1, units[1, mine, :], units[0, mine, :])
            value = jnp.where(mate_right == 1, mate[k, 1, at, :], value)
            value = jnp.where(mate_left == 1, mate[k, 0, at, :], value)
            offer[step, at, :] = value
            return carry

        lax.fori_loop(0, PIECE // 16, one, 0)
        if edges:

            @pl.when(is_host & (step >= early_slot * STEPS))
            def _():
                pre_recv(k).wait_recv()

                def swap(i, carry):
                    at = pl.ds(pl.multiple_of(i * 16, 16), 16)
                    offer[step, at, :] = jnp.where(guest_in == 1, pre[k, at, :], offer[step, at, :])
                    return carry

                lax.fori_loop(0, PIECE // 16, swap, 0)

        cross_copy(step).start()

    def tile(row, column_units, scale):
        cosine = lax.dot_general(
            units[row, :, :bins],
            column_units,
            (((1,), (1,)), ((), ())),
            preferred_element_type=jnp.float32,
        )
        return (cosine * cosine * cosine * scale).astype(jnp.bfloat16)

    def ahead(weight, column_scores):
        extended = jnp.concatenate([column_scores, jnp.ones_like(column_scores)], axis=1)
        return jnp.dot(weight, extended, preferred_element_type=jnp.float32)

    def local_pairs():
        def one(row, carry):
            own[row] = ahead(tile(row, units[row, :, :bins], 1.0), units[row, :, bins:])
            other = 1 - row
            own[row] += ahead(tile(row, units[other, :, :bins], inside), units[other, :, bins:])
            return carry

        lax.fori_loop(0, 2, one, 0)

    def chunk_pairs(read, scale0, scale1, target):
        part[...] = jnp.zeros_like(part)

        def one(row, carry):
            scale = jnp.where(row == 0, scale0, scale1).astype(jnp.float32)
            weight = tile(row, read(slice(0, bins)), scale)
            own[row] += ahead(weight, read(slice(bins, bins + feat)))
            part[:CHUNK, :] += lax.dot_general(
                weight,
                units[row, :, bins:],
                (((0,), (0,)), ((), ())),
                preferred_element_type=jnp.float32,
            )
            part[CHUNK:, :] += jnp.dot(
                jnp.ones((8, BLOCK), jnp.bfloat16), weight, preferred_element_type=jnp.float32
            )
            return carry

        lax.fori_loop(0, 2, one, 0)
        target[:CHUNK, :] = part[:CHUNK, :].astype(jnp.bfloat16)
        line = part[CHUNK:, :]
        high_part = line.astype(jnp.bfloat16).astype(jnp.float32)
        target[CHUNK:, :] = jnp.concatenate([high_part, line - high_part], axis=0).astype(jnp.bfloat16)

    def add_back(k, lines, scale0, scale1):
        rows = pl.ds(pl.multiple_of(k * CHUNK, CHUNK), CHUNK)
        sums = lines[:CHUNK, :].astype(jnp.float32)
        line = lines[CHUNK:, :].astype(jnp.float32)
        line = line[0:1, :] + line[8:9, :]
        degree = jnp.broadcast_to(line, (CHUNK, CHUNK)).T
        for block, scale in enumerate((scale0, scale1)):
            own[block, rows, :feat] += sums * scale
            own[block, rows, feat:] += degree * scale

    greetings = 3
    if edges:
        greetings = (
            3 + jnp.where(has_edge, 1, 0) + jnp.where(is_edge, 2, 0) + jnp.where(is_host, 1, 0)
        )

    mark_copy.wait()

    def prepare(k, carry):
        for block in range(2):
            load_copy(k, block).wait()
        normalize(k, 1 - core)

        @pl.when(k == 0)
        def _():
            pl.semaphore_wait(barrier, greetings)

        for block in range(2):
            mate_copy(k, block).start()
        normalize(k, core)
        if edges:

            @pl.when(is_edge)
            def _():
                for which in range(2):
                    pre_copy(k, which).start()

        @pl.when(k < AHEAD)
        def _():
            send(k)

        return carry

    lax.fori_loop(0, STEPS, prepare, 0)
    local_pairs()

    def edge_step(k):
        for which in range(2):
            post_recv(k, which).wait_recv()
        first = edge_right_in + edge_left_in * close0
        second = edge_right_in + edge_left_in * close1
        chunk_pairs(lambda columns: past[k, :, columns], first, second, ship_edge.at[k])
        edge_back(k, ship_edge.at[k]).start()

    def step_fn(step, carry):
        @pl.when(step < total_steps)
        def _():
            cross_copy(step).wait_recv()
            forward_copy(step).start()
            if edges:

                @pl.when(is_host & (step < STEPS))
                def _():
                    post_copy(step).start()

            @pl.when(step + AHEAD < total_steps)
            def _():
                send(step + AHEAD)

            forward_wait(step)
            right_in = flag_at(step, 5)
            left_in = flag_at(step, 6)
            first = right_in + left_in * close0
            second = right_in + left_in * close1
            chunk_pairs(lambda columns: got[step, :, columns], first, second, ship.at[step])
            back_copy(step).start()

            @pl.when(step == final)
            def _():
                back_corner().start()

            if edges:

                @pl.when(has_edge & odd_group & (step >= early_slot * STEPS))
                def _():
                    edge_back(chunk_of(step), ship.at[step]).start()

        if edges:

            @pl.when(is_edge & (step >= STEPS - 1) & (step < 2 * STEPS - 1))
            def _():
                edge_step(step - (STEPS - 1))

        @pl.when((step >= DELAY) & (step < total_steps + DELAY))
        def _():
            back_copy(step - DELAY).wait_recv()

            @pl.when(step - DELAY < final)
            def _():
                back_mate(step - DELAY).start()

        @pl.when(step > DELAY)
        def _():
            done = step - DELAY - 1
            back_mate(done).wait_recv()
            scale0 = flag_at(done, 1).astype(jnp.float32)
            scale1 = flag_at(done, 0).astype(jnp.float32)
            both = ret[done].astype(jnp.float32) + ret_mate[done].astype(jnp.float32)
            add_back(chunk_of(done), both, scale0, scale1)

        return carry

    def forward_wait(step):
        rows = pl.ds(pl.multiple_of((1 - core) * PIECE, PIECE), PIECE)
        copy(FW + step, got.at[step, rows], got.at[step, rows], partner).wait_recv()

    lax.fori_loop(0, total_steps + DELAY + 1, step_fn, 0)

    if edges:

        @pl.when(has_edge)
        def _():
            def one(k, carry):
                edge_back(k, ship_edge.at[k]).wait_recv()
                add_back(k, ret_edge[k], edge_out0, edge_out1)
                return carry

            lax.fori_loop(0, STEPS, one, 0)

    for block in range(2):
        out[block * BLOCK : (block + 1) * BLOCK, :] = own[block, :, :feat] / own[block, :, feat:]

    def finish(step, carry):
        cross_copy(step).wait_send()
        forward_copy(step).wait_send()
        back_copy(step).wait_send()
        back_mate(step).wait_send()
        return carry

    lax.fori_loop(0, total_steps, finish, 0)

    def finish_chunk(k, carry):
        for block in range(2):
            mate_copy(k, block).wait_send()
        if edges:

            @pl.when(has_edge)
            def _():
                edge_back(k, ship_edge.at[k]).wait_send()

            @pl.when(is_edge)
            def _():
                for which in range(2):
                    pre_copy(k, which).wait_send()

            @pl.when(is_host)
            def _():
                post_copy(k).wait_send()

        return carry

    lax.fori_loop(0, STEPS, finish_chunk, 0)


def slots_plan(slots, edges, spectra, scores, reach):
    rows, bins = spectra.shape
    feat = scores.shape[1]
    width = bins + feat
    steps = slots * STEPS
    extra = STEPS if edges else 1
    vmem = pl.BlockSpec(memory_space=pltpu.VMEM)
    bf16 = jnp.bfloat16
    return pl.pallas_call(
        functools.partial(slots_kernel, slots, edges),
        out_shape=jax.ShapeDtypeStruct((rows, feat), jnp.float32),
        in_specs=[pl.BlockSpec(memory_space=pltpu.SMEM)] + [pl.BlockSpec(memory_space=pltpu.HBM)] * 2,
        out_specs=vmem,
        scratch_shapes=[
            pltpu.VMEM((rows, bins), bf16),
            pltpu.VMEM((rows, feat), bf16),
            pltpu.VMEM((2, BLOCK, width), bf16),
            pltpu.VMEM((STEPS, 2, PIECE, width), bf16),
            pltpu.VMEM((extra, PIECE, width), bf16),
            pltpu.VMEM((steps, PIECE, width), bf16),
            pltpu.VMEM((steps, CHUNK, width), bf16),
            pltpu.VMEM((extra, CHUNK, width), bf16),
            pltpu.VMEM((2, BLOCK, 2 * feat), jnp.float32),
            pltpu.VMEM((CHUNK + 8, feat), jnp.float32),
            pltpu.VMEM((steps, LINES, feat), bf16),
            pltpu.VMEM((extra, LINES, feat), bf16),
            pltpu.VMEM((steps, LINES, feat), bf16),
            pltpu.VMEM((steps, LINES, feat), bf16),
            pltpu.VMEM((extra, LINES, feat), bf16),
            pltpu.SemaphoreType.DMA((2 * STEPS + 1,)),
            pltpu.SemaphoreType.DMA((60,)),
            pltpu.SemaphoreType.DMA((60,)),
        ],
        compiler_params=pltpu.CompilerParams(
            collective_id=4 + 2 * (slots - 1) + int(edges),
            has_side_effects=True,
            vmem_limit_bytes=48 * 2**20,
        ),
        cost_estimate=pl.CostEstimate(
            flops=8 * 2 * BLOCK * BLOCK * bins,
            bytes_accessed=2 * rows * width,
            transcendentals=rows * bins,
        ),
        name="slots",
    )(reach, spectra, scores)


TICKS = 2 * STEPS
QUARTER = CHUNK // 4
LEAD = 3
OPEN = 2
P_EX, P_XS, P_FW, P_RX, P_RF, P_PRE, P_POST, P_PF, P_RE = 0, 8, 16, 24, 32, 40, 44, 48, 52


def pair_kernel(parity, reach, spectra, marks, out, raw, scores, units, mate, lend, borrow, offer, offer_pair, got, own, part,
                ship, ret, ret_mate, ret_edge, load_sem, send_sem, recv_sem):
    bins = spectra.shape[1]
    feat = marks.shape[1]
    subs = lax.axis_size("sub")
    count = lax.axis_size("blk") * subs
    position = lax.axis_index("blk") * subs + lax.axis_index("sub")
    place = lax.rem(position, GROUP)
    group = position // GROUP
    side = lax.rem(place, 2)
    core = place // 2
    base = position - place
    upper = lax.rem(group + parity, 2)
    across = position + 1 - 2 * side
    partner = position + 2 - 4 * core
    corner = across + 2 - 4 * core
    shift = jnp.where(upper == 1, count - GROUP, GROUP)
    pair = lax.rem(position + shift, count)
    pair_base = pair - place
    low_base = jnp.where(upper == 1, pair_base, base)

    def place_of(device):
        return (device // subs, lax.rem(device, subs))

    def copy(index, source, target, device):
        return pltpu.make_async_remote_copy(
            src_ref=source,
            dst_ref=target,
            send_sem=send_sem.at[index],
            recv_sem=recv_sem.at[index],
            device_id=place_of(device),
            device_id_type=MESH,
        )

    def load_copy(k, block):
        rows = pl.ds(pl.multiple_of(block * BLOCK + k * CHUNK, CHUNK), CHUNK)
        return pltpu.make_async_copy(spectra.at[rows], raw.at[rows], load_sem.at[2 * k + block])

    mark_copy = pltpu.make_async_copy(marks, scores, load_sem.at[2 * STEPS])
    for block in range(2):
        load_copy(0, block).start()
    mark_copy.start()
    for k in range(1, STEPS):
        for block in range(2):
            load_copy(k, block).start()

    barrier = pltpu.get_barrier_semaphore()
    for device in (across, partner, corner, pair):
        pl.semaphore_signal(barrier, inc=1, device_id=place_of(device), device_id_type=MESH)

    def active(boundary):
        within = boundary < count - 1
        at = jnp.minimum(boundary, count - 2)
        a, b = reach[2 * at], reach[2 * at + 1]
        right = jnp.where(within & (b == 2), 1, 0)
        left = jnp.where(within & ((a == 2) | (b == 1)), 1, 0)
        return right, left

    def lanes(first):
        (r0, l0), (r1, l1), (r2, l2) = [active(first + i) for i in range(3)]
        result = []
        for d1, d2, d3 in ((r0, l1, r2), (l0, r1, l2)):
            f1, f2, f3 = d1, d2 * (1 - d1), d3 * (1 - d1) * (1 - d2)
            result.append(((f1, f2, f3), (d1 - f1, d2 - f2, d3 - f3)))
        return result

    going, coming = lanes(base)
    pair_going, pair_coming = lanes(pair_base)
    edge_right, edge_left = active(low_base + 3)
    up = upper
    down = 1 - upper

    def pick(options):
        value = options[-1]
        for i in range(len(options) - 2, -1, -1):
            value = jnp.where(place == i, options[i], value)
        return value

    def lane_flags(which):
        q, r = going[which], coming[which]
        last = 1 if which else 0
        right_out = pick([q[0], r[1], q[2], 0])
        left_out = pick([0, r[0], q[1], r[2]])
        mate_right = pick([q[2], last * edge_right * down, q[0], r[1]])
        mate_left = pick([q[1], r[2], last * edge_left * up, r[0]])
        right_in = pick([last * edge_right * up, q[0], r[1], q[2]])
        left_in = pick([r[0], q[1], r[2], last * edge_left * down])
        return right_out, left_out, mate_right, mate_left, right_in, left_in

    own_lane, pair_lane = lane_flags(0), lane_flags(1)
    edge_out0 = jnp.where(place == 0, edge_left * up, 0)
    edge_out1 = jnp.where(place == 3, edge_right * down, 0)
    pair_sum = jnp.where(
        side == 0,
        sum(pair_going[1]) + edge_left * down,
        sum(pair_coming[1]) + edge_right * up,
    )

    own0, own1 = reach[2 * position], reach[2 * position + 1]
    close0 = jnp.where(own0 == 2, 1, 0)
    close1 = jnp.where(own1 == 1, 1, 0)
    inside = jnp.where(own0 >= 1, 1.0, 0.0).astype(jnp.float32)

    sends_edge = ((upper == 0) & (place == 0)) | ((upper == 1) & (place == 3))
    takes_edge = ((upper == 1) & (place == 0)) | ((upper == 0) & (place == 3))

    def shared(tick):
        return (tick >= OPEN) & (tick < OPEN + STEPS)

    def alone(tick):
        return ((tick >= 0) & (tick < OPEN)) | ((tick >= OPEN + STEPS) & (tick < TICKS))

    def chunk_of(tick):
        return jnp.where(tick < OPEN, tick, tick - STEPS)

    def normalize(k, which):
        def one(block, carry):
            row = k * CHUNK + which * PIECE
            source = pl.ds(pl.multiple_of(block * BLOCK + row, 64), 64)
            values = raw[source, :].astype(jnp.float32)
            total = jnp.sum(values, axis=1, keepdims=True)
            unit = jnp.sqrt(values) * (1.0 / jnp.sqrt(total + 1e-06))
            units[source, :bins] = unit.astype(jnp.bfloat16)
            units[source, bins:] = scores[source, :]
            return carry

        lax.fori_loop(0, 2, one, 0)

    def half_rows(tick, which):
        return got.at[pl.ds(pl.multiple_of(tick * CHUNK + which * PIECE, PIECE), PIECE)]

    def quarter_rows(tick, which, level):
        start = tick * CHUNK + which * PIECE + level * QUARTER
        return got.at[pl.ds(pl.multiple_of(start, QUARTER), QUARTER)]

    def mate_copy(k, block):
        rows = pl.ds(pl.multiple_of(block * BLOCK + k * CHUNK + (1 - core) * PIECE, PIECE), PIECE)
        return copy(P_EX + 2 * k + block, units.at[rows], mate.at[k, block], partner)

    def pre_copy(k):
        return copy(P_PRE + k, lend.at[k], borrow.at[k], pair)

    def cross_alone(tick):
        return copy(P_XS + tick, offer.at[chunk_of(tick)], half_rows(tick, core), across)

    def cross_shared(tick):
        return copy(P_XS + tick, offer_pair.at[tick - OPEN], quarter_rows(tick, core, upper), across)

    def forward_alone(tick, which):
        rows = half_rows(tick, which)
        return copy(P_FW + tick, rows, rows, partner)

    def forward_shared(tick, which):
        rows = quarter_rows(tick, which, upper)
        return copy(P_FW + tick, rows, rows, partner)

    def post_copy(k, level):
        rows = quarter_rows(k + OPEN, core, level)
        return copy(P_POST + k, rows, rows, pair)

    def post_forward(k, which):
        rows = quarter_rows(k + OPEN, which, 1 - upper)
        return copy(P_PF + k, rows, rows, partner)

    def back_copy(tick):
        return copy(P_RX + tick, ship.at[tick], ret.at[tick], across)

    def back_mate(tick):
        return copy(P_RF + tick, ret.at[tick], ret_mate.at[tick], partner)

    def back_corner():
        return copy(P_RF + TICKS - 1, ship.at[TICKS - 1], ret_mate.at[TICKS - 1], corner)

    def edge_back(k):
        return copy(P_RE + k, ret_mate.at[k + OPEN], ret_edge.at[k], pair)

    def choose_rows(flags, k, start, i):
        right_out, left_out, mate_right, mate_left = flags
        at = pl.ds(pl.multiple_of(start + i * 16, 16), 16)
        first = k * CHUNK + core * PIECE + start + i * 16
        mine0 = pl.ds(pl.multiple_of(first, 16), 16)
        mine1 = pl.ds(pl.multiple_of(BLOCK + first, 16), 16)
        value = jnp.where(right_out == 1, units[mine1, :], units[mine0, :])
        value = jnp.where(mate_right == 1, mate[k, 1, at, :], value)
        return jnp.where(mate_left == 1, mate[k, 0, at, :], value)

    pair_right_out = pair_lane[0] + edge_out1
    pair_flags = (pair_right_out,) + pair_lane[1:4]

    def offer_to_pair(k):
        def one(i, carry):
            rows = pl.ds(pl.multiple_of(i * 16, 16), 16)
            lend[k, rows, :] = choose_rows(pair_flags, k, (1 - upper) * QUARTER, i)
            return carry

        lax.fori_loop(0, QUARTER // 16, one, 0)
        pre_copy(k).start()

    def send_alone(tick):
        k = chunk_of(tick)

        def one(i, carry):
            rows = pl.ds(pl.multiple_of(i * 16, 16), 16)
            offer[k, rows, :] = choose_rows(own_lane[:4], k, 0, i)
            return carry

        lax.fori_loop(0, PIECE // 16, one, 0)
        cross_alone(tick).start()

    def send_shared(tick):
        k = tick - OPEN
        pre_copy(k).wait_recv()

        def one(i, carry):
            rows = pl.ds(pl.multiple_of(i * 16, 16), 16)
            value = choose_rows(pair_flags, k, upper * QUARTER, i)
            offer_pair[k, rows, :] = jnp.where(pair_sum > 0, borrow[k, rows, :], value)
            return carry

        lax.fori_loop(0, QUARTER // 16, one, 0)
        cross_shared(tick).start()

    def send(tick):
        @pl.when(alone(tick))
        def _():
            send_alone(tick)

        @pl.when(shared(tick))
        def _():
            send_shared(tick)

    def local_pairs():
        def one(row, carry):
            rows = pl.ds(pl.multiple_of(row * BLOCK, BLOCK), BLOCK)
            cosine = lax.dot_general(
                units[rows, :bins],
                units[:, :bins],
                (((1,), (1,)), ((), ())),
                preferred_element_type=jnp.float32,
            )
            column = lax.broadcasted_iota(jnp.int32, (1, 2 * BLOCK), 1) // BLOCK
            scale = jnp.where(column == row, 1.0, inside)
            weight = (cosine * cosine * cosine * scale).astype(jnp.bfloat16)
            extended = jnp.concatenate([units[:, bins:], jnp.ones((2 * BLOCK, feat), jnp.bfloat16)], axis=1)
            own[rows, :] = jnp.dot(weight, extended, preferred_element_type=jnp.float32)
            return carry

        lax.fori_loop(0, 2, one, 0)

    def chunk_pairs(tick, chunks, flags):
        first = (flags[4] + flags[5] * close0).astype(jnp.float32)
        second = (flags[4] + flags[5] * close1).astype(jnp.float32)
        size = chunks * CHUNK
        rows = pl.ds(pl.multiple_of(tick * CHUNK, CHUNK), size)
        cosine = lax.dot_general(
            got[rows, :bins],
            units[:, :bins],
            (((1,), (1,)), ((), ())),
            preferred_element_type=jnp.float32,
        )
        column = lax.broadcasted_iota(jnp.int32, (1, 2 * BLOCK), 1)
        scale = jnp.where(column < BLOCK, first, second)
        weight = (cosine * cosine * cosine * scale).astype(jnp.bfloat16)
        extended = jnp.concatenate([units[:, bins:], jnp.ones((2 * BLOCK, feat), jnp.bfloat16)], axis=1)
        part[:size, :] = jnp.dot(weight, extended, preferred_element_type=jnp.float32)
        extended = jnp.concatenate([got[rows, bins:], jnp.ones((size, feat), jnp.bfloat16)], axis=1)
        own[...] += lax.dot_general(
            weight, extended, (((0,), (0,)), ((), ())), preferred_element_type=jnp.float32
        )
        for i in range(chunks):
            lines = slice(i * CHUNK, i * CHUNK + CHUNK)
            ship[tick + i, :CHUNK, :] = part[lines, :feat].astype(jnp.bfloat16)
            line = part[lines, feat:].T[:8, :]
            high_part = line.astype(jnp.bfloat16).astype(jnp.float32)
            ship[tick + i, CHUNK:, :] = jnp.concatenate([high_part, line - high_part], axis=0).astype(
                jnp.bfloat16
            )
            back_copy(tick + i).start()

    mark_copy.wait()

    def prepare(k, carry):
        for block in range(2):
            load_copy(k, block).wait()
        normalize(k, 1 - core)

        @pl.when(k == 0)
        def _():
            pl.semaphore_wait(barrier, 4)

        for block in range(2):
            mate_copy(k, block).start()
        normalize(k, core)

        @pl.when(k == 0)
        def _():
            lend_rows(0)
            send_alone(0)

        @pl.when(k >= 2)
        def _():
            lend_rows(k - 1)
            send(k - 1)

        return carry

    def lend_rows(k):
        for block in range(2):
            mate_copy(k, block).wait_recv()
        offer_to_pair(k)

    lax.fori_loop(0, STEPS, prepare, 0)
    lend_rows(STEPS - 1)
    local_pairs()

    def shared_pairs(k):
        for i in range(2):
            forward_shared(k + i + OPEN, 1 - core).wait_recv()
            post_forward(k + i, 1 - core).wait_recv()
        chunk_pairs(k + OPEN, 2, pair_lane)

    def collect(tick):
        back_copy(tick).wait_recv()
        back_mate(tick).start()

    def tick_fn(tick, carry):
        @pl.when((tick >= OPEN + 2) & (tick < OPEN + 2 + STEPS))
        def _():
            post_copy(tick - OPEN - 2, 1 - upper).wait_recv()
            post_forward(tick - OPEN - 2, core).start()

        @pl.when(tick == TICKS - 1)
        def _():
            forward_alone(TICKS - 2, 1 - core).wait_recv()
            chunk_pairs(TICKS - 2, 1, own_lane)
            shared_pairs(2)

        @pl.when(alone(tick))
        def _():
            cross_alone(tick).wait_recv()
            forward_alone(tick, core).start()

        @pl.when(shared(tick))
        def _():
            cross_shared(tick).wait_recv()
            forward_shared(tick, core).start()
            post_copy(tick - OPEN, upper).start()

        @pl.when(tick + LEAD < TICKS)
        def _():
            send(tick + LEAD)

        @pl.when(tick == OPEN)
        def _():
            for i in range(OPEN):
                forward_alone(i, 1 - core).wait_recv()
            chunk_pairs(0, 2, own_lane)

        @pl.when(tick == OPEN + STEPS)
        def _():
            shared_pairs(0)
            for i in range(OPEN):
                collect(i)

        @pl.when(tick == TICKS - 1)
        def _():
            forward_alone(TICKS - 1, 1 - core).wait_recv()
            chunk_pairs(TICKS - 1, 1, own_lane)
            back_corner().start()

        return carry

    lax.fori_loop(0, TICKS, tick_fn, 0)

    def collect_fn(tick, carry):
        collect(tick)
        return carry

    lax.fori_loop(OPEN, TICKS - 1, collect_fn, 0)

    def shared_fn(k, carry):
        back_mate(k + OPEN).wait_recv()

        @pl.when(sends_edge)
        def _():
            edge_back(k).start()

        return carry

    lax.fori_loop(0, STEPS, shared_fn, 0)

    def close(k, carry):
        tick = jnp.where(k < OPEN, k, k + STEPS)

        @pl.when(k == STEPS - 1)
        def _():
            back_copy(TICKS - 1).wait_recv()

        back_mate(tick).wait_recv()

        @pl.when(takes_edge)
        def _():
            edge_back(k).wait_recv()

        def both(at):
            return ret[at].astype(jnp.float32) + ret_mate[at].astype(jnp.float32)

        alone_sum, shared_sum = both(tick), both(k + OPEN)
        edge_sum = jnp.where(takes_edge, ret_edge[k].astype(jnp.float32), 0.0)
        for block, edge_flag in enumerate((edge_out0, edge_out1)):
            lines = (
                alone_sum * own_lane[1 - block].astype(jnp.float32)
                + shared_sum * pair_lane[1 - block].astype(jnp.float32)
                + edge_sum * edge_flag.astype(jnp.float32)
            )
            line = lines[CHUNK : CHUNK + 1, :] + lines[CHUNK + 8 : CHUNK + 9, :]
            degree = jnp.broadcast_to(line, (CHUNK, CHUNK)).T
            rows = pl.ds(pl.multiple_of(block * BLOCK + k * CHUNK, CHUNK), CHUNK)
            out[rows, :] = (own[rows, :feat] + lines[:CHUNK, :]) / (own[rows, feat:] + degree)
        return carry

    lax.fori_loop(0, STEPS, close, 0)

    def finish(tick, carry):
        @pl.when(alone(tick))
        def _():
            cross_alone(tick).wait_send()
            forward_alone(tick, core).wait_send()

        @pl.when(shared(tick))
        def _():
            cross_shared(tick).wait_send()
            forward_shared(tick, core).wait_send()

        back_copy(tick).wait_send()
        back_mate(tick).wait_send()
        return carry

    lax.fori_loop(0, TICKS, finish, 0)

    def finish_chunk(k, carry):
        for block in range(2):
            mate_copy(k, block).wait_send()
        pre_copy(k).wait_send()
        post_copy(k, upper).wait_send()
        post_forward(k, core).wait_send()

        @pl.when(sends_edge)
        def _():
            edge_back(k).wait_send()

        return carry

    lax.fori_loop(0, STEPS, finish_chunk, 0)


def pair_plan(parity, spectra, scores, reach):
    rows, bins = spectra.shape
    feat = scores.shape[1]
    width = bins + feat
    vmem = pl.BlockSpec(memory_space=pltpu.VMEM)
    bf16 = jnp.bfloat16
    return pl.pallas_call(
        functools.partial(pair_kernel, parity),
        out_shape=jax.ShapeDtypeStruct((rows, feat), jnp.float32),
        in_specs=[pl.BlockSpec(memory_space=pltpu.SMEM)] + [pl.BlockSpec(memory_space=pltpu.HBM)] * 2,
        out_specs=vmem,
        scratch_shapes=[
            pltpu.VMEM((rows, bins), bf16),
            pltpu.VMEM((rows, feat), bf16),
            pltpu.VMEM((rows, width), bf16),
            pltpu.VMEM((STEPS, 2, PIECE, width), bf16),
            pltpu.VMEM((STEPS, QUARTER, width), bf16),
            pltpu.VMEM((STEPS, QUARTER, width), bf16),
            pltpu.VMEM((STEPS, PIECE, width), bf16),
            pltpu.VMEM((STEPS, QUARTER, width), bf16),
            pltpu.VMEM((TICKS * CHUNK, width), bf16),
            pltpu.VMEM((rows, 2 * feat), jnp.float32),
            pltpu.VMEM((2 * CHUNK, 2 * feat), jnp.float32),
            pltpu.VMEM((TICKS, LINES, feat), bf16),
            pltpu.VMEM((TICKS, LINES, feat), bf16),
            pltpu.VMEM((TICKS, LINES, feat), bf16),
            pltpu.VMEM((STEPS, LINES, feat), bf16),
            pltpu.SemaphoreType.DMA((2 * STEPS + 1,)),
            pltpu.SemaphoreType.DMA((56,)),
            pltpu.SemaphoreType.DMA((56,)),
        ],
        compiler_params=pltpu.CompilerParams(
            collective_id=8 + parity,
            has_side_effects=True,
            vmem_limit_bytes=48 * 2**20,
        ),
        cost_estimate=pl.CostEstimate(
            flops=8 * 2 * BLOCK * BLOCK * bins,
            bytes_accessed=2 * rows * width,
            transcendentals=rows * bins,
        ),
        name="pairs",
    )(reach, spectra, scores)


def branch(reach):
    size = reach.shape[0]
    group = 2 * GROUP
    margin = 2
    padded = jnp.pad(reach, (margin, 2 * group))
    index = lax.iota(jnp.int32, size)

    def at(shift):
        return padded[margin + shift : margin + shift + size]

    def right(boundary):
        return jnp.where(at(2 * boundary + 1) == 2, 1, 0)

    def left(boundary):
        return jnp.where((at(2 * boundary) == 2) | (at(2 * boundary + 1) == 1), 1, 0)

    def lanes(first):
        going = right(first) + left(first + 1) + right(first + 2)
        coming = left(first) + right(first + 1) + left(first + 2)
        return going, coming

    def over(lane):
        return jnp.maximum(lane - 1, 0)

    def flag(condition, place):
        return jnp.where(condition, 2**place, 0)

    odd = lax.rem(index, 2 * group) == group
    hosts = jnp.where(odd, 1, 0)
    going, coming = lanes(0)
    next_going, next_coming = lanes(GROUP)
    edge_right, edge_left = right(3), left(3)
    edge = edge_right + edge_left > 0
    over_going, over_coming = over(going), over(coming)
    shared = jnp.maximum(
        over_going + over(next_going) + edge_left, over_coming + over(next_coming) + edge_right
    )
    two = jnp.maximum(going + hosts * (left(-1) + edge_left), coming + hosts * (right(-1) + edge_right))
    full = over_going + over_coming > 0
    misses = (
        flag(full | edge, 0)
        | flag(jnp.where(odd, edge, shared > 1), 1)
        | flag(jnp.where(odd, shared > 1, edge), 2)
        | flag(two > 2, 3)
        | flag(full & (index == 0), 5)
        | flag(full & (index == size - group), 6)
    )
    misses = jnp.where(lax.rem(index, group) == 0, misses, 0)
    missed = lax.reduce(misses, jnp.int32(0), lax.bitwise_or, (0,))
    missed = missed | (lax.shift_right_logical(missed, 3) & lax.shift_right_logical(missed, 4) & 4)
    return 31 - lax.clz(~missed & ((missed & 15) + 1))


def body(spectra, class_scores, reach):
    if reach.shape[0] % 16:
        return plan(True, True, spectra, class_scores, reach)
    branches = [
        functools.partial(slots_plan, 1, False),
        functools.partial(pair_plan, 0),
        functools.partial(pair_plan, 1),
        functools.partial(slots_plan, 2, True),
        functools.partial(plan, True, True),
    ]
    return lax.switch(branch(reach), branches, spectra, class_scores, reach)


def solution(mesh):
    return jax.shard_map(
        body,
        mesh=mesh,
        in_specs=(P(AXES, None), P(AXES, None), P()),
        out_specs=P(AXES, None),
        check_vma=False,
    )
```

```python
import functools

import jax
import jax.numpy as jnp
from jax import lax
from jax.experimental import pallas as pl
from jax.experimental.pallas import tpu as pltpu
from jax.sharding import PartitionSpec as P

BLOCK = 512
AXES = ("blk", "sub")
GROUP = 4
MESH = pl.DeviceIdType.MESH
HALF = BLOCK // 2
PART = HALF + 16 * (HALF // 128)
SHIP = 2 * PART
NEAR, FAR, EDGE = 2, 3, 4


def kernel(two_blocks, group_edge, reach, spectra, scores, out, units, own, part, ship, ret, offer, kept,
           send_sem, recv_sem):
    bins = spectra.shape[1]
    feat = scores.shape[1]
    subs = lax.axis_size("sub")
    count = lax.axis_size("blk") * subs
    position = lax.axis_index("blk") * subs + lax.axis_index("sub")
    place = lax.rem(position, GROUP)
    odd = lax.rem(place, 2)
    across = position + 1 - 2 * odd
    core = jnp.where(place < 2, position + 2, position - 2)
    beside = position - 1 + 2 * odd
    middle = (place == 1) | (place == 2)
    outer = jnp.logical_not(middle)
    low = place < 2
    high = jnp.logical_not(low)
    has_edge = ((place == 0) & (position > 0)) | ((place == 3) & (position < count - 1))
    first = odd
    second = 1 - odd

    def copy(index, source, target, device):
        return pltpu.make_async_remote_copy(
            src_ref=source,
            dst_ref=target,
            send_sem=send_sem.at[index],
            recv_sem=recv_sem.at[index],
            device_id=(device // subs, lax.rem(device, subs)),
            device_id_type=MESH,
        )

    barrier = pltpu.get_barrier_semaphore()

    def greet(device):
        pl.semaphore_signal(
            barrier,
            inc=1,
            device_id=(device // subs, lax.rem(device, subs)),
            device_id_type=MESH,
        )

    greet(across)
    greet(core)
    beside_used = middle if two_blocks else (place < 0)
    if group_edge:
        beside_used = beside_used | has_edge

    @pl.when(beside_used)
    def _():
        greet(beside)

    def normalize(block):
        def step(i, carry):
            rows = pl.ds(pl.multiple_of(i * 64, 64), 64)
            source = pl.ds(pl.multiple_of(block * BLOCK + i * 64, 64), 64)
            values = spectra[source, :].astype(jnp.float32)
            total = jnp.sum(values, axis=1, keepdims=True)
            unit = jnp.sqrt(values) * (1.0 / jnp.sqrt(total + 1e-06))
            units[block, rows, :bins] = unit.astype(jnp.bfloat16)
            units[block, rows, bins:] = scores[source, :]
            return carry

        lax.fori_loop(0, BLOCK // 64, step, 0)

    def own_reach(index):
        return reach[2 * position + index]

    previous = jnp.maximum(2 * position - 2, 0)

    def flag(condition):
        return jnp.where(condition, 1.0, 0.0).astype(jnp.float32)

    to_next0 = flag(own_reach(0) >= 2)
    to_next1 = flag(own_reach(1) >= 1)
    to_next2 = flag(own_reach(1) >= 2)
    from_prev0 = flag(reach[previous] >= 2)
    from_prev1 = flag(reach[previous + 1] >= 1)
    from_prev2 = flag(reach[previous + 1] >= 2)
    inside = flag(own_reach(0) >= 1)

    def weights(row, column, scale, start=0, size=BLOCK):
        cosine = lax.dot_general(
            units[row, :, :bins],
            units[column, start : start + size, :bins],
            (((1,), (1,)), ((), ())),
            preferred_element_type=jnp.float32,
        )
        return (cosine * cosine * cosine * scale).astype(jnp.bfloat16)

    def forward(column, weight, start=0, size=BLOCK):
        column_scores = units[column, start : start + size, bins:]
        extended = jnp.concatenate([column_scores, jnp.ones_like(column_scores)], axis=1)
        return jnp.dot(weight, extended, preferred_element_type=jnp.float32)

    def local_pairs():
        def step(row, carry):
            own[row] = forward(row, weights(row, row, 1.0))
            own[row] += forward(1 - row, weights(row, 1 - row, inside))
            return carry

        lax.fori_loop(0, 2, step, 0)

    def remote_pairs(column, slot, scale0, scale1, halves=(0, 1)):
        start, size = halves[0] * HALF, HALF * len(halves)
        part[...] = jnp.zeros_like(part)

        def step(row, carry):
            scale = jnp.where(row == 0, scale0, scale1)
            weight = weights(row, column, scale, start, size)
            own[row] += forward(column, weight, start, size)
            part[:size, :] += lax.dot_general(
                weight,
                units[row, :, bins:],
                (((0,), (0,)), ((), ())),
                preferred_element_type=jnp.float32,
            )
            sums = jnp.dot(
                jnp.ones((8, BLOCK), jnp.bfloat16), weight, preferred_element_type=jnp.float32
            )
            for q in range(size // 128):
                part[BLOCK + 8 * q : BLOCK + 8 * q + 8, :] += sums[:, 128 * q : 128 * q + 128]
            return carry

        lax.fori_loop(0, 2, step, 0)
        for place_in, half in enumerate(halves):
            base = half * PART
            ship[slot, base : base + HALF, :] = part[
                place_in * HALF : place_in * HALF + HALF, :
            ].astype(jnp.bfloat16)
            for q in range(HALF // 128):
                row = BLOCK + 8 * (place_in * (HALF // 128) + q)
                line = part[row : row + 8, :]
                high_part = line.astype(jnp.bfloat16).astype(jnp.float32)
                ship[slot, base + HALF + 16 * q : base + HALF + 16 * q + 16, :] = jnp.concatenate(
                    [high_part, line - high_part], axis=0
                ).astype(jnp.bfloat16)

    def add_back(block, slot, scale=1.0, halves=(0, 1)):
        for half in halves:
            base = half * PART
            rows = slice(half * HALF, half * HALF + HALF)
            own[block, rows, :feat] += ret[slot, base : base + HALF, :].astype(jnp.float32) * scale
            for q in range(HALF // 128):
                line = ret[slot, base + HALF + 16 * q : base + HALF + 16 * q + 16, :]
                line = line.astype(jnp.float32)
                line = (line[0:1, :] + line[8:9, :]) * scale
                rows = slice(half * HALF + 128 * q, half * HALF + 128 * q + 128)
                own[block, rows, feat:] += jnp.broadcast_to(line, (128, 128)).T

    if group_edge:
        edge_copy = copy(0, units.at[first], units.at[EDGE], beside)
        edge_back = copy(1, ship.at[2], ret.at[2], beside)

    normalize(first)

    @pl.when(beside_used)
    def _():
        pl.semaphore_wait(barrier, 3)

    @pl.when(jnp.logical_not(beside_used))
    def _():
        pl.semaphore_wait(barrier, 2)

    if two_blocks:
        first_copy = copy(2, units.at[first], units.at[NEAR], across)
        second_copies = [
            copy(
                3 + 5 * h,
                units.at[second, pl.ds(h * HALF, HALF)],
                units.at[FAR, pl.ds(h * HALF, HALF)],
                across,
            )
            for h in range(2)
        ]
        pass_copy = copy(4, units.at[NEAR], units.at[NEAR], core)
        first_back = copy(5, ship.at[0], ret.at[0], across)
        second_backs = [
            copy(
                6 + 3 * h,
                ship.at[1, pl.ds(h * PART, PART)],
                ret.at[1, pl.ds(h * PART, PART)],
                across,
            )
            for h in range(2)
        ]
        beside_back = copy(7, ship.at[0], ret.at[2], beside)

        @pl.when(middle)
        def _():
            first_copy.start()

    if group_edge:

        @pl.when(has_edge)
        def _():
            edge_copy.start()

    normalize(second)

    def edge_pairs():
        @pl.when(has_edge)
        def _():
            edge_copy.wait_recv()
            is_left = place == 3
            remote_pairs(
                EDGE,
                2,
                jnp.where(is_left, to_next0, 0.0),
                jnp.where(is_left, to_next1, from_prev2),
            )
            edge_back.start()

    def edge_end():
        @pl.when(has_edge)
        def _():
            edge_back.wait_recv()
            add_back(first, 2)
            edge_copy.wait_send()
            edge_back.wait_send()

    if two_blocks:
        local_pairs()

        @pl.when(middle)
        def _():
            first_copy.wait_send()
            for half in range(2):
                second_copies[half].start()
            pass_copy.wait_recv()
            is_left = place == 1
            remote_pairs(
                NEAR,
                0,
                jnp.where(is_left, to_next0, 0.0),
                jnp.where(is_left, to_next1, from_prev2),
            )
            beside_back.start()
            beside_back.wait_recv()
            add_back(first, 2)
            first_back.wait_recv()
            add_back(first, 0)
            for half in range(2):
                second_copies[half].wait_send()
                second_backs[half].wait_recv()
                add_back(second, 1, halves=(half,))
            beside_back.wait_send()

        @pl.when(outer)
        def _():
            first_copy.wait_recv()
            pass_copy.start()
            is_left = place == 0
            remote_pairs(
                NEAR,
                0,
                jnp.where(is_left, 0.0, from_prev0),
                jnp.where(is_left, to_next2, 0.0),
            )
            first_back.start()

        if group_edge:
            edge_pairs()

        @pl.when(outer)
        def _():
            is_left = place == 0
            for half in range(2):
                second_copies[half].wait_recv()
                remote_pairs(
                    FAR,
                    1,
                    jnp.where(is_left, to_next0, from_prev1),
                    jnp.where(is_left, to_next1, from_prev2),
                    halves=(half,),
                )
                second_backs[half].start()
            pass_copy.wait_send()
            first_back.wait_send()
            for half in range(2):
                second_backs[half].wait_send()

    else:
        leads = jnp.where(place < 3, jnp.maximum(to_next0, to_next1), 0.0)
        follows = jnp.where(place > 0, jnp.maximum(from_prev0, from_prev1), 0.0)
        has_role = jnp.maximum(leads, follows)
        gather_copies, cross_copies, pass_copies = [], [], []
        for half in range(2):
            rows = pl.ds(half * HALF, HALF)
            near = units.at[NEAR, rows]
            gather_copies.append(copy(2 + 6 * half, offer.at[rows], kept.at[rows], core))
            cross_copies.append(copy(3 + 6 * half, offer.at[rows], near, across))
            pass_copies.append(copy(4 + 6 * half, near, near, core))
        gather_back = copy(5, ship.at[0], ret.at[0], core)
        cross_back = copy(6, ship.at[0], ret.at[1], across)
        pass_back = copy(7, ret.at[1], ret.at[1], core)

        def blend(target, yes, no, scale, rows):
            def step(i, carry):
                chunk = pl.ds(pl.multiple_of(i * rows, rows), rows)
                a = yes[chunk, :].astype(jnp.float32) * scale
                b = no[chunk, :].astype(jnp.float32) * (1.0 - scale)
                target[chunk, :] = (a + b).astype(target.dtype)
                return carry

            lax.fori_loop(0, target.shape[0] // rows, step, 0)

        for half in range(2):
            rows = pl.ds(half * HALF, HALF)
            blend(offer.at[rows], units.at[1, rows], units.at[0, rows], leads, 64)

            @pl.when(high)
            def _():
                gather_copies[half].start()

        @pl.when(low)
        def _():
            for half in range(2):
                rows = pl.ds(half * HALF, HALF)
                gather_copies[half].wait_recv()
                blend(offer.at[rows], offer.at[rows], kept.at[rows], has_role, 64)
                cross_copies[half].start()

        local_pairs()

        @pl.when(low)
        def _():
            for half in range(2):
                cross_copies[half].wait_recv()
                pass_copies[half].start()

        @pl.when(high)
        def _():
            for half in range(2):
                pass_copies[half].wait_recv()

        remote_pairs(
            NEAR,
            0,
            jnp.where(place < 3, to_next0, 0.0) * leads,
            jnp.where(place < 3, to_next1, 0.0) * leads + from_prev2 * follows,
        )

        @pl.when(high)
        def _():
            gather_back.start()

        @pl.when(low)
        def _():
            gather_back.wait_recv()
            blend(ship.at[0], ship.at[0], ret.at[0], has_role, SHIP)
            cross_back.start()

        if group_edge:
            edge_pairs()

        @pl.when(low)
        def _():
            cross_back.wait_recv()
            pass_back.start()

        @pl.when(high)
        def _():
            pass_back.wait_recv()

        add_back(1, 1, leads)
        add_back(0, 1, follows)

        @pl.when(low)
        def _():
            for half in range(2):
                cross_copies[half].wait_send()
                pass_copies[half].wait_send()
            cross_back.wait_send()
            pass_back.wait_send()

        @pl.when(high)
        def _():
            for half in range(2):
                gather_copies[half].wait_send()
            gather_back.wait_send()

    if group_edge:
        edge_end()

    for block in range(2):
        out[block * BLOCK : (block + 1) * BLOCK, :] = own[block, :, :feat] / own[block, :, feat:]


def plan(two_blocks, group_edge, spectra, scores, reach):
    rows, bins = spectra.shape
    feat = scores.shape[1]
    width = bins + feat
    vmem = pl.BlockSpec(memory_space=pltpu.VMEM)
    return pl.pallas_call(
        functools.partial(kernel, two_blocks, group_edge),
        out_shape=jax.ShapeDtypeStruct((rows, feat), jnp.float32),
        in_specs=[pl.BlockSpec(memory_space=pltpu.SMEM), vmem, vmem],
        out_specs=vmem,
        scratch_shapes=[
            pltpu.VMEM((5, BLOCK, width), jnp.bfloat16),
            pltpu.VMEM((2, BLOCK, 2 * feat), jnp.float32),
            pltpu.VMEM((BLOCK + 8 * (BLOCK // 128), feat), jnp.float32),
            pltpu.VMEM((3, SHIP, feat), jnp.bfloat16),
            pltpu.VMEM((3, SHIP, feat), jnp.bfloat16),
            pltpu.VMEM((16 if two_blocks else BLOCK, width), jnp.bfloat16),
            pltpu.VMEM((16 if two_blocks else BLOCK, width), jnp.bfloat16),
            pltpu.SemaphoreType.DMA((12,)),
            pltpu.SemaphoreType.DMA((12,)),
        ],
        compiler_params=pltpu.CompilerParams(
            collective_id=2 * int(two_blocks) + int(group_edge),
            has_side_effects=True,
            vmem_limit_bytes=48 * 2**20,
        ),
        cost_estimate=pl.CostEstimate(
            flops=8 * 2 * BLOCK * BLOCK * bins,
            bytes_accessed=2 * rows * width,
            transcendentals=rows * bins,
        ),
        name="network",
    )(reach, spectra, scores)


CHUNK = 128
PIECE = CHUNK // 2
STEPS = BLOCK // CHUNK
LINES = CHUNK + 16
AHEAD = 3
DELAY = 4
EX, XS, FW, PRE, POST, RX, RF, RE = 0, 8, 16, 24, 32, 40, 48, 56


def slots_kernel(slots, edges, reach, spectra, marks, out, raw, scores, units, mate, pre, offer, got, past, own, part, ship,
                 ship_edge, ret, ret_mate, ret_edge, load_sem, send_sem, recv_sem):
    bins = spectra.shape[1]
    feat = marks.shape[1]
    total_steps = slots * STEPS
    subs = lax.axis_size("sub")
    count = lax.axis_size("blk") * subs
    position = lax.axis_index("blk") * subs + lax.axis_index("sub")
    place = lax.rem(position, GROUP)
    group = position // GROUP
    side = lax.rem(place, 2)
    core = place // 2
    base = position - place
    odd_group = lax.rem(group, 2) == 1
    even_group = lax.rem(group, 2) == 0
    across = position + 1 - 2 * side
    partner = position + 2 - 4 * core
    corner = across + 2 - 4 * core
    at_end = (place == 0) | (place == 3)
    has_edge = ((place == 0) & (position > 0)) | ((place == 3) & (position < count - 1))
    beside = jnp.where(place == 0, position - 1, position + 1)
    is_edge = has_edge & even_group
    host = jnp.where(side == 0, base - GROUP, base + GROUP) + side
    is_host = odd_group & ((side == 1) | (base + GROUP < count))
    guest = jnp.where(side == 0, base + GROUP, base - GROUP + 3)

    def place_of(device):
        return (device // subs, lax.rem(device, subs))

    def copy(index, source, target, device):
        return pltpu.make_async_remote_copy(
            src_ref=source,
            dst_ref=target,
            send_sem=send_sem.at[index],
            recv_sem=recv_sem.at[index],
            device_id=place_of(device),
            device_id_type=MESH,
        )

    def load_copy(k, block):
        rows = pl.ds(pl.multiple_of(block * BLOCK + k * CHUNK, CHUNK), CHUNK)
        return pltpu.make_async_copy(spectra.at[rows], raw.at[rows], load_sem.at[2 * k + block])

    mark_copy = pltpu.make_async_copy(marks, scores, load_sem.at[2 * STEPS])
    for block in range(2):
        load_copy(0, block).start()
    mark_copy.start()
    for k in range(1, STEPS):
        for block in range(2):
            load_copy(k, block).start()

    barrier = pltpu.get_barrier_semaphore()

    def greet(device):
        pl.semaphore_signal(barrier, inc=1, device_id=place_of(device), device_id_type=MESH)

    greet(across)
    greet(partner)
    greet(corner)
    if edges:

        @pl.when(has_edge)
        def _():
            greet(beside)

        @pl.when(is_edge)
        def _():
            greet(host)
            greet(host + 2)

        @pl.when(is_host)
        def _():
            greet(guest)

    def active(boundary):
        inside = (boundary >= 0) & (boundary < count - 1)
        at = jnp.clip(boundary, 0, count - 2)
        a, b = reach[2 * at], reach[2 * at + 1]
        right = jnp.where(inside & (b == 2), 1, 0)
        left = jnp.where(inside & ((a == 2) | (b == 1)), 1, 0)
        return right, left

    bounds = [active(base + i - 1) for i in range(5)]
    rights = [b[0] for b in bounds]
    lefts = [b[1] for b in bounds]
    hosts = jnp.where(odd_group, 1, 0) if edges else 0

    def assign(inner, late, early):
        d1, d2, d3 = inner
        if slots == 1:
            return ((d1, d2, d3, late * hosts, early * hosts),)
        late, early = late * hosts, early * hosts
        free = 1 - late
        f1 = d1 * free
        f2 = d2 * (1 - d1) * free
        f3 = d3 * (1 - d1) * (1 - d2) * free
        return ((f1, f2, f3, late, 0), (d1 - f1, d2 - f2, d3 - f3, 0, early))

    going = assign((rights[1], lefts[2], rights[3]), lefts[0], lefts[4])
    coming = assign((lefts[1], rights[2], lefts[3]), rights[4], rights[0])

    def pick(options, index):
        value = options[-1]
        for i in range(len(options) - 2, -1, -1):
            value = jnp.where(index == i, options[i], value)
        return value

    def slot_flags(slot):
        q, r = going[slot], coming[slot]
        right_out = pick([q[0], r[1], q[2], r[3]], place)
        left_out = pick([q[3], r[0], q[1], r[2]], place)
        mate_right = pick([q[2], r[3], q[0], r[1]], place)
        mate_left = pick([q[1], r[2], q[3], r[0]], place)
        guest_in = jnp.where(side == 0, q[4], r[4])
        right_in = pick([r[4], q[0], r[1], q[2]], place)
        left_in = pick([r[0], q[1], r[2], q[4]], place)
        return right_out, left_out, mate_right, mate_left, guest_in, right_in, left_in

    flags = [slot_flags(s) for s in range(slots)]

    def flag_at(step, which):
        if slots == 1:
            return flags[0][which]
        return jnp.where(step < STEPS, flags[0][which], flags[1][which])

    own0, own1 = reach[2 * position], reach[2 * position + 1]
    close0 = jnp.where(own0 == 2, 1, 0)
    close1 = jnp.where(own1 == 1, 1, 0)
    inside = jnp.where(own0 >= 1, 1.0, 0.0).astype(jnp.float32)

    edge_right_in = jnp.where(place == 0, rights[0], 0)
    edge_left_in = jnp.where(place == 3, lefts[4], 0)
    edge_out0 = jnp.where(place == 0, lefts[0], 0).astype(jnp.float32)
    edge_out1 = jnp.where(place == 3, rights[4], 0).astype(jnp.float32)

    def chunk_of(step):
        return lax.rem(step, STEPS)

    def normalize(k, which):
        def one(block, carry):
            row = k * CHUNK + which * PIECE
            source = pl.ds(pl.multiple_of(block * BLOCK + row, 64), 64)
            values = raw[source, :].astype(jnp.float32)
            total = jnp.sum(values, axis=1, keepdims=True)
            unit = jnp.sqrt(values) * (1.0 / jnp.sqrt(total + 1e-06))
            units[source, :bins] = unit.astype(jnp.bfloat16)
            units[source, bins:] = scores[source, :]
            return carry

        lax.fori_loop(0, 2, one, 0)

    def piece(block, k, which):
        start = block * BLOCK + k * CHUNK + which * PIECE
        return units.at[pl.ds(pl.multiple_of(start, PIECE), PIECE)]

    def mate_copy(k, block):
        return copy(EX + 2 * k + block, piece(block, k, 1 - core), mate.at[k, block], partner)

    def pre_copy(k, which):
        block = jnp.where(place == 0, 0, 1)
        return copy(PRE + 2 * k + which, piece(block, k, which), pre.at[k], host + 2 * which)

    def pre_recv(k):
        return copy(PRE + 2 * k + core, pre.at[k], pre.at[k], across)

    def cross_copy(step):
        rows = pl.ds(pl.multiple_of(core * PIECE, PIECE), PIECE)
        return copy(XS + step, offer.at[step], got.at[step, rows], across)

    def forward_copy(step):
        rows = pl.ds(pl.multiple_of(core * PIECE, PIECE), PIECE)
        return copy(FW + step, got.at[step, rows], got.at[step, rows], partner)

    def post_copy(step):
        rows = pl.ds(pl.multiple_of(core * PIECE, PIECE), PIECE)
        return copy(POST + 2 * step + core, got.at[step, rows], past.at[step, rows], guest)

    def post_recv(k, which):
        rows = pl.ds(which * PIECE, PIECE)
        return copy(POST + 2 * k + which, past.at[k, rows], past.at[k, rows], across)

    def back_copy(step):
        return copy(RX + step, ship.at[step], ret.at[step], across)

    def back_mate(step):
        return copy(RF + step, ret.at[step], ret_mate.at[step], partner)

    final = total_steps - 1

    def back_corner():
        return copy(RF + final, ship.at[final], ret_mate.at[final], corner)

    def edge_back(k, source):
        return copy(RE + k, source, ret_edge.at[k], beside)

    early_slot = slots - 1

    def send(step):
        k = chunk_of(step)

        @pl.when(step < STEPS)
        def _():
            for block in range(2):
                mate_copy(k, block).wait_recv()

        right_out = flag_at(step, 0)
        mate_right = flag_at(step, 2)
        mate_left = flag_at(step, 3)
        guest_in = flag_at(step, 4)

        def one(i, carry):
            at = pl.ds(pl.multiple_of(i * 16, 16), 16)
            first = k * CHUNK + core * PIECE + i * 16
            mine0 = pl.ds(pl.multiple_of(first, 16), 16)
            mine1 = pl.ds(pl.multiple_of(BLOCK + first, 16), 16)
            value = jnp.where(right_out == 1, units[mine1, :], units[mine0, :])
            value = jnp.where(mate_right == 1, mate[k, 1, at, :], value)
            value = jnp.where(mate_left == 1, mate[k, 0, at, :], value)
            offer[step, at, :] = value
            return carry

        lax.fori_loop(0, PIECE // 16, one, 0)
        if edges:

            @pl.when(is_host & (step >= early_slot * STEPS))
            def _():
                pre_recv(k).wait_recv()

                def swap(i, carry):
                    at = pl.ds(pl.multiple_of(i * 16, 16), 16)
                    offer[step, at, :] = jnp.where(guest_in == 1, pre[k, at, :], offer[step, at, :])
                    return carry

                lax.fori_loop(0, PIECE // 16, swap, 0)

        cross_copy(step).start()

    def local_pairs():
        def one(row, carry):
            rows = pl.ds(pl.multiple_of(row * BLOCK, BLOCK), BLOCK)
            cosine = lax.dot_general(
                units[rows, :bins],
                units[:, :bins],
                (((1,), (1,)), ((), ())),
                preferred_element_type=jnp.float32,
            )
            column = lax.broadcasted_iota(jnp.int32, (1, 2 * BLOCK), 1) // BLOCK
            scale = jnp.where(column == row, 1.0, inside)
            weight = (cosine * cosine * cosine * scale).astype(jnp.bfloat16)
            extended = jnp.concatenate([units[:, bins:], jnp.ones((2 * BLOCK, feat), jnp.bfloat16)], axis=1)
            own[rows, :] = jnp.dot(weight, extended, preferred_element_type=jnp.float32)
            return carry

        lax.fori_loop(0, 2, one, 0)

    def chunk_pairs(read, scale0, scale1, target):
        cosine = lax.dot_general(
            read(slice(0, bins)),
            units[:, :bins],
            (((1,), (1,)), ((), ())),
            preferred_element_type=jnp.float32,
        )
        column = lax.broadcasted_iota(jnp.int32, (1, 2 * BLOCK), 1)
        scale = jnp.where(column < BLOCK, scale0.astype(jnp.float32), scale1.astype(jnp.float32))
        weight = (cosine * cosine * cosine * scale).astype(jnp.bfloat16)
        extended = jnp.concatenate([units[:, bins:], jnp.ones((2 * BLOCK, feat), jnp.bfloat16)], axis=1)
        part[...] = jnp.dot(weight, extended, preferred_element_type=jnp.float32)
        column_scores = read(slice(bins, bins + feat))
        extended = jnp.concatenate([column_scores, jnp.ones_like(column_scores)], axis=1)
        own[...] += lax.dot_general(
            weight, extended, (((0,), (0,)), ((), ())), preferred_element_type=jnp.float32
        )
        target[:CHUNK, :] = part[:, :feat].astype(jnp.bfloat16)
        line = part[:, feat:].T[:8, :]
        high_part = line.astype(jnp.bfloat16).astype(jnp.float32)
        target[CHUNK:, :] = jnp.concatenate([high_part, line - high_part], axis=0).astype(jnp.bfloat16)

    def add_back(k, lines, scale0, scale1):
        sums = lines[:CHUNK, :].astype(jnp.float32)
        line = lines[CHUNK:, :].astype(jnp.float32)
        line = line[0:1, :] + line[8:9, :]
        degree = jnp.broadcast_to(line, (CHUNK, CHUNK)).T
        for block, scale in enumerate((scale0, scale1)):
            rows = pl.ds(pl.multiple_of(block * BLOCK + k * CHUNK, CHUNK), CHUNK)
            own[rows, :feat] += sums * scale
            own[rows, feat:] += degree * scale

    greetings = 3
    if edges:
        greetings = (
            3 + jnp.where(has_edge, 1, 0) + jnp.where(is_edge, 2, 0) + jnp.where(is_host, 1, 0)
        )

    mark_copy.wait()

    def prepare(k, carry):
        for block in range(2):
            load_copy(k, block).wait()
        normalize(k, 1 - core)

        @pl.when(k == 0)
        def _():
            pl.semaphore_wait(barrier, greetings)

        for block in range(2):
            mate_copy(k, block).start()
        normalize(k, core)
        if edges:

            @pl.when(is_edge)
            def _():
                for which in range(2):
                    pre_copy(k, which).start()

        @pl.when(k < AHEAD)
        def _():
            send(k)

        return carry

    lax.fori_loop(0, STEPS, prepare, 0)
    local_pairs()

    def edge_step(k):
        for which in range(2):
            post_recv(k, which).wait_recv()
        first = edge_right_in + edge_left_in * close0
        second = edge_right_in + edge_left_in * close1
        chunk_pairs(lambda columns: past[k, :, columns], first, second, ship_edge.at[k])
        edge_back(k, ship_edge.at[k]).start()

    def step_fn(step, carry):
        @pl.when(step < total_steps)
        def _():
            cross_copy(step).wait_recv()
            forward_copy(step).start()
            if edges:

                @pl.when(is_host & (step < STEPS))
                def _():
                    post_copy(step).start()

            @pl.when(step + AHEAD < total_steps)
            def _():
                send(step + AHEAD)

            forward_wait(step)
            right_in = flag_at(step, 5)
            left_in = flag_at(step, 6)
            first = right_in + left_in * close0
            second = right_in + left_in * close1
            chunk_pairs(lambda columns: got[step, :, columns], first, second, ship.at[step])
            back_copy(step).start()

            @pl.when(step == final)
            def _():
                back_corner().start()

            if edges:

                @pl.when(has_edge & odd_group & (step >= early_slot * STEPS))
                def _():
                    edge_back(chunk_of(step), ship.at[step]).start()

        if edges:

            @pl.when(is_edge & (step >= STEPS - 1) & (step < 2 * STEPS - 1))
            def _():
                edge_step(step - (STEPS - 1))

        @pl.when((step >= DELAY) & (step < total_steps + DELAY))
        def _():
            back_copy(step - DELAY).wait_recv()

            @pl.when(step - DELAY < final)
            def _():
                back_mate(step - DELAY).start()

        @pl.when(step > DELAY)
        def _():
            done = step - DELAY - 1
            back_mate(done).wait_recv()
            scale0 = flag_at(done, 1).astype(jnp.float32)
            scale1 = flag_at(done, 0).astype(jnp.float32)
            both = ret[done].astype(jnp.float32) + ret_mate[done].astype(jnp.float32)
            add_back(chunk_of(done), both, scale0, scale1)

        return carry

    def forward_wait(step):
        rows = pl.ds(pl.multiple_of((1 - core) * PIECE, PIECE), PIECE)
        copy(FW + step, got.at[step, rows], got.at[step, rows], partner).wait_recv()

    lax.fori_loop(0, total_steps + DELAY + 1, step_fn, 0)

    if edges:

        @pl.when(has_edge)
        def _():
            def one(k, carry):
                edge_back(k, ship_edge.at[k]).wait_recv()
                add_back(k, ret_edge[k], edge_out0, edge_out1)
                return carry

            lax.fori_loop(0, STEPS, one, 0)

    out[...] = own[:, :feat] / own[:, feat:]

    def finish(step, carry):
        cross_copy(step).wait_send()
        forward_copy(step).wait_send()
        back_copy(step).wait_send()
        back_mate(step).wait_send()
        return carry

    lax.fori_loop(0, total_steps, finish, 0)

    def finish_chunk(k, carry):
        for block in range(2):
            mate_copy(k, block).wait_send()
        if edges:

            @pl.when(has_edge)
            def _():
                edge_back(k, ship_edge.at[k]).wait_send()

            @pl.when(is_edge)
            def _():
                for which in range(2):
                    pre_copy(k, which).wait_send()

            @pl.when(is_host)
            def _():
                post_copy(k).wait_send()

        return carry

    lax.fori_loop(0, STEPS, finish_chunk, 0)


def slots_plan(slots, edges, spectra, scores, reach):
    rows, bins = spectra.shape
    feat = scores.shape[1]
    width = bins + feat
    steps = slots * STEPS
    extra = STEPS if edges else 1
    vmem = pl.BlockSpec(memory_space=pltpu.VMEM)
    bf16 = jnp.bfloat16
    return pl.pallas_call(
        functools.partial(slots_kernel, slots, edges),
        out_shape=jax.ShapeDtypeStruct((rows, feat), jnp.float32),
        in_specs=[pl.BlockSpec(memory_space=pltpu.SMEM)] + [pl.BlockSpec(memory_space=pltpu.HBM)] * 2,
        out_specs=vmem,
        scratch_shapes=[
            pltpu.VMEM((rows, bins), bf16),
            pltpu.VMEM((rows, feat), bf16),
            pltpu.VMEM((rows, width), bf16),
            pltpu.VMEM((STEPS, 2, PIECE, width), bf16),
            pltpu.VMEM((extra, PIECE, width), bf16),
            pltpu.VMEM((steps, PIECE, width), bf16),
            pltpu.VMEM((steps, CHUNK, width), bf16),
            pltpu.VMEM((extra, CHUNK, width), bf16),
            pltpu.VMEM((rows, 2 * feat), jnp.float32),
            pltpu.VMEM((CHUNK, 2 * feat), jnp.float32),
            pltpu.VMEM((steps, LINES, feat), bf16),
            pltpu.VMEM((extra, LINES, feat), bf16),
            pltpu.VMEM((steps, LINES, feat), bf16),
            pltpu.VMEM((steps, LINES, feat), bf16),
            pltpu.VMEM((extra, LINES, feat), bf16),
            pltpu.SemaphoreType.DMA((2 * STEPS + 1,)),
            pltpu.SemaphoreType.DMA((60,)),
            pltpu.SemaphoreType.DMA((60,)),
        ],
        compiler_params=pltpu.CompilerParams(
            collective_id=4 + 2 * (slots - 1) + int(edges),
            has_side_effects=True,
            vmem_limit_bytes=48 * 2**20,
        ),
        cost_estimate=pl.CostEstimate(
            flops=8 * 2 * BLOCK * BLOCK * bins,
            bytes_accessed=2 * rows * width,
            transcendentals=rows * bins,
        ),
        name="slots",
    )(reach, spectra, scores)


TICKS = 2 * STEPS
QUARTER = CHUNK // 4
LEAD = 3
OPEN = 2
P_EX, P_XS, P_FW, P_RX, P_RF, P_PRE, P_POST, P_PF, P_RE = 0, 8, 16, 24, 32, 40, 44, 48, 52


def pair_kernel(parity, reach, spectra, marks, out, raw, scores, units, mate, lend, borrow, offer, offer_pair, got, own, part,
                ship, ret, ret_mate, ret_edge, load_sem, send_sem, recv_sem):
    bins = spectra.shape[1]
    feat = marks.shape[1]
    subs = lax.axis_size("sub")
    count = lax.axis_size("blk") * subs
    position = lax.axis_index("blk") * subs + lax.axis_index("sub")
    place = lax.rem(position, GROUP)
    group = position // GROUP
    side = lax.rem(place, 2)
    core = place // 2
    base = position - place
    upper = lax.rem(group + parity, 2)
    across = position + 1 - 2 * side
    partner = position + 2 - 4 * core
    corner = across + 2 - 4 * core
    shift = jnp.where(upper == 1, count - GROUP, GROUP)
    pair = lax.rem(position + shift, count)
    pair_base = pair - place
    low_base = jnp.where(upper == 1, pair_base, base)

    def place_of(device):
        return (device // subs, lax.rem(device, subs))

    def copy(index, source, target, device):
        return pltpu.make_async_remote_copy(
            src_ref=source,
            dst_ref=target,
            send_sem=send_sem.at[index],
            recv_sem=recv_sem.at[index],
            device_id=place_of(device),
            device_id_type=MESH,
        )

    def load_copy(k, block):
        rows = pl.ds(pl.multiple_of(block * BLOCK + k * CHUNK, CHUNK), CHUNK)
        return pltpu.make_async_copy(spectra.at[rows], raw.at[rows], load_sem.at[2 * k + block])

    mark_copy = pltpu.make_async_copy(marks, scores, load_sem.at[2 * STEPS])
    for block in range(2):
        load_copy(0, block).start()
    mark_copy.start()
    for k in range(1, STEPS):
        for block in range(2):
            load_copy(k, block).start()

    barrier = pltpu.get_barrier_semaphore()
    for device in (across, partner, corner, pair):
        pl.semaphore_signal(barrier, inc=1, device_id=place_of(device), device_id_type=MESH)

    def active(boundary):
        within = boundary < count - 1
        at = jnp.minimum(boundary, count - 2)
        a, b = reach[2 * at], reach[2 * at + 1]
        right = jnp.where(within & (b == 2), 1, 0)
        left = jnp.where(within & ((a == 2) | (b == 1)), 1, 0)
        return right, left

    def lanes(first):
        (r0, l0), (r1, l1), (r2, l2) = [active(first + i) for i in range(3)]
        result = []
        for d1, d2, d3 in ((r0, l1, r2), (l0, r1, l2)):
            f1, f2, f3 = d1, d2 * (1 - d1), d3 * (1 - d1) * (1 - d2)
            result.append(((f1, f2, f3), (d1 - f1, d2 - f2, d3 - f3)))
        return result

    going, coming = lanes(base)
    pair_going, pair_coming = lanes(pair_base)
    edge_right, edge_left = active(low_base + 3)
    up = upper
    down = 1 - upper

    def pick(options):
        value = options[-1]
        for i in range(len(options) - 2, -1, -1):
            value = jnp.where(place == i, options[i], value)
        return value

    def lane_flags(which):
        q, r = going[which], coming[which]
        last = 1 if which else 0
        right_out = pick([q[0], r[1], q[2], 0])
        left_out = pick([0, r[0], q[1], r[2]])
        mate_right = pick([q[2], last * edge_right * down, q[0], r[1]])
        mate_left = pick([q[1], r[2], last * edge_left * up, r[0]])
        right_in = pick([last * edge_right * up, q[0], r[1], q[2]])
        left_in = pick([r[0], q[1], r[2], last * edge_left * down])
        return right_out, left_out, mate_right, mate_left, right_in, left_in

    own_lane, pair_lane = lane_flags(0), lane_flags(1)
    edge_out0 = jnp.where(place == 0, edge_left * up, 0)
    edge_out1 = jnp.where(place == 3, edge_right * down, 0)
    pair_sum = jnp.where(
        side == 0,
        sum(pair_going[1]) + edge_left * down,
        sum(pair_coming[1]) + edge_right * up,
    )

    own0, own1 = reach[2 * position], reach[2 * position + 1]
    close0 = jnp.where(own0 == 2, 1, 0)
    close1 = jnp.where(own1 == 1, 1, 0)
    inside = jnp.where(own0 >= 1, 1.0, 0.0).astype(jnp.float32)

    sends_edge = ((upper == 0) & (place == 0)) | ((upper == 1) & (place == 3))
    takes_edge = ((upper == 1) & (place == 0)) | ((upper == 0) & (place == 3))

    def shared(tick):
        return (tick >= OPEN) & (tick < OPEN + STEPS)

    def alone(tick):
        return ((tick >= 0) & (tick < OPEN)) | ((tick >= OPEN + STEPS) & (tick < TICKS))

    def chunk_of(tick):
        return jnp.where(tick < OPEN, tick, tick - STEPS)

    def normalize(k, which):
        def one(block, carry):
            row = k * CHUNK + which * PIECE
            source = pl.ds(pl.multiple_of(block * BLOCK + row, 64), 64)
            values = raw[source, :].astype(jnp.float32)
            total = jnp.sum(values, axis=1, keepdims=True)
            unit = jnp.sqrt(values) * (1.0 / jnp.sqrt(total + 1e-06))
            units[source, :bins] = unit.astype(jnp.bfloat16)
            units[source, bins:] = scores[source, :]
            return carry

        lax.fori_loop(0, 2, one, 0)

    def half_rows(tick, which):
        return got.at[pl.ds(pl.multiple_of(tick * CHUNK + which * PIECE, PIECE), PIECE)]

    def quarter_rows(tick, which, level):
        start = tick * CHUNK + which * PIECE + level * QUARTER
        return got.at[pl.ds(pl.multiple_of(start, QUARTER), QUARTER)]

    def mate_copy(k, block):
        rows = pl.ds(pl.multiple_of(block * BLOCK + k * CHUNK + (1 - core) * PIECE, PIECE), PIECE)
        return copy(P_EX + 2 * k + block, units.at[rows], mate.at[k, block], partner)

    def pre_copy(k):
        return copy(P_PRE + k, lend.at[k], borrow.at[k], pair)

    def cross_alone(tick):
        return copy(P_XS + tick, offer.at[chunk_of(tick)], half_rows(tick, core), across)

    def cross_shared(tick):
        return copy(P_XS + tick, offer_pair.at[tick - OPEN], quarter_rows(tick, core, upper), across)

    def forward_alone(tick, which):
        rows = half_rows(tick, which)
        return copy(P_FW + tick, rows, rows, partner)

    def forward_shared(tick, which):
        rows = quarter_rows(tick, which, upper)
        return copy(P_FW + tick, rows, rows, partner)

    def post_copy(k, level):
        rows = quarter_rows(k + OPEN, core, level)
        return copy(P_POST + k, rows, rows, pair)

    def post_forward(k, which):
        rows = quarter_rows(k + OPEN, which, 1 - upper)
        return copy(P_PF + k, rows, rows, partner)

    def back_copy(tick):
        return copy(P_RX + tick, ship.at[tick], ret.at[tick], across)

    def back_mate(tick):
        return copy(P_RF + tick, ret.at[tick], ret_mate.at[tick], partner)

    def back_corner():
        return copy(P_RF + TICKS - 1, ship.at[TICKS - 1], ret_mate.at[TICKS - 1], corner)

    def edge_back(k):
        return copy(P_RE + k, ret_mate.at[k + OPEN], ret_edge.at[k], pair)

    def choose_rows(flags, k, start, i):
        right_out, left_out, mate_right, mate_left = flags
        at = pl.ds(pl.multiple_of(start + i * 16, 16), 16)
        first = k * CHUNK + core * PIECE + start + i * 16
        mine0 = pl.ds(pl.multiple_of(first, 16), 16)
        mine1 = pl.ds(pl.multiple_of(BLOCK + first, 16), 16)
        value = jnp.where(right_out == 1, units[mine1, :], units[mine0, :])
        value = jnp.where(mate_right == 1, mate[k, 1, at, :], value)
        return jnp.where(mate_left == 1, mate[k, 0, at, :], value)

    pair_right_out = pair_lane[0] + edge_out1
    pair_flags = (pair_right_out,) + pair_lane[1:4]

    def offer_to_pair(k):
        def one(i, carry):
            rows = pl.ds(pl.multiple_of(i * 16, 16), 16)
            lend[k, rows, :] = choose_rows(pair_flags, k, (1 - upper) * QUARTER, i)
            return carry

        lax.fori_loop(0, QUARTER // 16, one, 0)
        pre_copy(k).start()

    def send_alone(tick):
        k = chunk_of(tick)

        def one(i, carry):
            rows = pl.ds(pl.multiple_of(i * 16, 16), 16)
            offer[k, rows, :] = choose_rows(own_lane[:4], k, 0, i)
            return carry

        lax.fori_loop(0, PIECE // 16, one, 0)
        cross_alone(tick).start()

    def send_shared(tick):
        k = tick - OPEN
        pre_copy(k).wait_recv()

        def one(i, carry):
            rows = pl.ds(pl.multiple_of(i * 16, 16), 16)
            value = choose_rows(pair_flags, k, upper * QUARTER, i)
            offer_pair[k, rows, :] = jnp.where(pair_sum > 0, borrow[k, rows, :], value)
            return carry

        lax.fori_loop(0, QUARTER // 16, one, 0)
        cross_shared(tick).start()

    def send(tick):
        @pl.when(alone(tick))
        def _():
            send_alone(tick)

        @pl.when(shared(tick))
        def _():
            send_shared(tick)

    def local_pairs():
        def one(row, carry):
            rows = pl.ds(pl.multiple_of(row * BLOCK, BLOCK), BLOCK)
            cosine = lax.dot_general(
                units[rows, :bins],
                units[:, :bins],
                (((1,), (1,)), ((), ())),
                preferred_element_type=jnp.float32,
            )
            column = lax.broadcasted_iota(jnp.int32, (1, 2 * BLOCK), 1) // BLOCK
            scale = jnp.where(column == row, 1.0, inside)
            weight = (cosine * cosine * cosine * scale).astype(jnp.bfloat16)
            extended = jnp.concatenate([units[:, bins:], jnp.ones((2 * BLOCK, feat), jnp.bfloat16)], axis=1)
            own[rows, :] = jnp.dot(weight, extended, preferred_element_type=jnp.float32)
            return carry

        lax.fori_loop(0, 2, one, 0)

    def chunk_pairs(tick, chunks, flags):
        first = (flags[4] + flags[5] * close0).astype(jnp.float32)
        second = (flags[4] + flags[5] * close1).astype(jnp.float32)
        size = chunks * CHUNK
        rows = pl.ds(pl.multiple_of(tick * CHUNK, CHUNK), size)
        cosine = lax.dot_general(
            got[rows, :bins],
            units[:, :bins],
            (((1,), (1,)), ((), ())),
            preferred_element_type=jnp.float32,
        )
        column = lax.broadcasted_iota(jnp.int32, (1, 2 * BLOCK), 1)
        scale = jnp.where(column < BLOCK, first, second)
        weight = (cosine * cosine * cosine * scale).astype(jnp.bfloat16)
        extended = jnp.concatenate([units[:, bins:], jnp.ones((2 * BLOCK, feat), jnp.bfloat16)], axis=1)
        part[:size, :] = jnp.dot(weight, extended, preferred_element_type=jnp.float32)
        extended = jnp.concatenate([got[rows, bins:], jnp.ones((size, feat), jnp.bfloat16)], axis=1)
        own[...] += lax.dot_general(
            weight, extended, (((0,), (0,)), ((), ())), preferred_element_type=jnp.float32
        )
        for i in range(chunks):
            lines = slice(i * CHUNK, i * CHUNK + CHUNK)
            ship[tick + i, :CHUNK, :] = part[lines, :feat].astype(jnp.bfloat16)
            line = part[lines, feat:].T[:8, :]
            high_part = line.astype(jnp.bfloat16).astype(jnp.float32)
            ship[tick + i, CHUNK:, :] = jnp.concatenate([high_part, line - high_part], axis=0).astype(
                jnp.bfloat16
            )
            back_copy(tick + i).start()

    mark_copy.wait()

    def prepare(k, carry):
        for block in range(2):
            load_copy(k, block).wait()
        normalize(k, 1 - core)

        @pl.when(k == 0)
        def _():
            pl.semaphore_wait(barrier, 4)

        for block in range(2):
            mate_copy(k, block).start()
        normalize(k, core)

        @pl.when(k == 0)
        def _():
            lend_rows(0)
            send_alone(0)

        @pl.when(k >= 2)
        def _():
            lend_rows(k - 1)
            send(k - 1)

        return carry

    def lend_rows(k):
        for block in range(2):
            mate_copy(k, block).wait_recv()
        offer_to_pair(k)

    lax.fori_loop(0, STEPS, prepare, 0)
    lend_rows(STEPS - 1)
    local_pairs()

    def shared_pairs(k):
        for i in range(2):
            forward_shared(k + i + OPEN, 1 - core).wait_recv()
            post_forward(k + i, 1 - core).wait_recv()
        chunk_pairs(k + OPEN, 2, pair_lane)

    def collect(tick):
        back_copy(tick).wait_recv()
        back_mate(tick).start()

    def tick_fn(tick, carry):
        @pl.when((tick >= OPEN + 2) & (tick < OPEN + 2 + STEPS))
        def _():
            post_copy(tick - OPEN - 2, 1 - upper).wait_recv()
            post_forward(tick - OPEN - 2, core).start()

        @pl.when(tick == TICKS - 1)
        def _():
            forward_alone(TICKS - 2, 1 - core).wait_recv()
            chunk_pairs(TICKS - 2, 1, own_lane)
            shared_pairs(2)

        @pl.when(alone(tick))
        def _():
            cross_alone(tick).wait_recv()
            forward_alone(tick, core).start()

        @pl.when(shared(tick))
        def _():
            cross_shared(tick).wait_recv()
            forward_shared(tick, core).start()
            post_copy(tick - OPEN, upper).start()

        @pl.when(tick + LEAD < TICKS)
        def _():
            send(tick + LEAD)

        @pl.when(tick == OPEN)
        def _():
            for i in range(OPEN):
                forward_alone(i, 1 - core).wait_recv()
            chunk_pairs(0, 2, own_lane)

        @pl.when(tick == OPEN + STEPS)
        def _():
            shared_pairs(0)
            for i in range(OPEN):
                collect(i)

        @pl.when(tick == TICKS - 1)
        def _():
            forward_alone(TICKS - 1, 1 - core).wait_recv()
            chunk_pairs(TICKS - 1, 1, own_lane)
            back_corner().start()

        return carry

    lax.fori_loop(0, TICKS, tick_fn, 0)

    def collect_fn(tick, carry):
        collect(tick)
        return carry

    lax.fori_loop(OPEN, TICKS - 1, collect_fn, 0)

    def shared_fn(k, carry):
        back_mate(k + OPEN).wait_recv()

        @pl.when(sends_edge)
        def _():
            edge_back(k).start()

        return carry

    lax.fori_loop(0, STEPS, shared_fn, 0)

    def close(k, carry):
        tick = jnp.where(k < OPEN, k, k + STEPS)

        @pl.when(k == STEPS - 1)
        def _():
            back_copy(TICKS - 1).wait_recv()

        back_mate(tick).wait_recv()

        @pl.when(takes_edge)
        def _():
            edge_back(k).wait_recv()

        def both(at):
            return ret[at].astype(jnp.float32) + ret_mate[at].astype(jnp.float32)

        alone_sum, shared_sum = both(tick), both(k + OPEN)
        edge_sum = jnp.where(takes_edge, ret_edge[k].astype(jnp.float32), 0.0)
        for block, edge_flag in enumerate((edge_out0, edge_out1)):
            lines = (
                alone_sum * own_lane[1 - block].astype(jnp.float32)
                + shared_sum * pair_lane[1 - block].astype(jnp.float32)
                + edge_sum * edge_flag.astype(jnp.float32)
            )
            line = lines[CHUNK : CHUNK + 1, :] + lines[CHUNK + 8 : CHUNK + 9, :]
            degree = jnp.broadcast_to(line, (CHUNK, CHUNK)).T
            rows = pl.ds(pl.multiple_of(block * BLOCK + k * CHUNK, CHUNK), CHUNK)
            out[rows, :] = (own[rows, :feat] + lines[:CHUNK, :]) / (own[rows, feat:] + degree)
        return carry

    lax.fori_loop(0, STEPS, close, 0)

    def finish(tick, carry):
        @pl.when(alone(tick))
        def _():
            cross_alone(tick).wait_send()
            forward_alone(tick, core).wait_send()

        @pl.when(shared(tick))
        def _():
            cross_shared(tick).wait_send()
            forward_shared(tick, core).wait_send()

        back_copy(tick).wait_send()
        back_mate(tick).wait_send()
        return carry

    lax.fori_loop(0, TICKS, finish, 0)

    def finish_chunk(k, carry):
        for block in range(2):
            mate_copy(k, block).wait_send()
        pre_copy(k).wait_send()
        post_copy(k, upper).wait_send()
        post_forward(k, core).wait_send()

        @pl.when(sends_edge)
        def _():
            edge_back(k).wait_send()

        return carry

    lax.fori_loop(0, STEPS, finish_chunk, 0)


def pair_plan(parity, spectra, scores, reach):
    rows, bins = spectra.shape
    feat = scores.shape[1]
    width = bins + feat
    vmem = pl.BlockSpec(memory_space=pltpu.VMEM)
    bf16 = jnp.bfloat16
    return pl.pallas_call(
        functools.partial(pair_kernel, parity),
        out_shape=jax.ShapeDtypeStruct((rows, feat), jnp.float32),
        in_specs=[pl.BlockSpec(memory_space=pltpu.SMEM)] + [pl.BlockSpec(memory_space=pltpu.HBM)] * 2,
        out_specs=vmem,
        scratch_shapes=[
            pltpu.VMEM((rows, bins), bf16),
            pltpu.VMEM((rows, feat), bf16),
            pltpu.VMEM((rows, width), bf16),
            pltpu.VMEM((STEPS, 2, PIECE, width), bf16),
            pltpu.VMEM((STEPS, QUARTER, width), bf16),
            pltpu.VMEM((STEPS, QUARTER, width), bf16),
            pltpu.VMEM((STEPS, PIECE, width), bf16),
            pltpu.VMEM((STEPS, QUARTER, width), bf16),
            pltpu.VMEM((TICKS * CHUNK, width), bf16),
            pltpu.VMEM((rows, 2 * feat), jnp.float32),
            pltpu.VMEM((2 * CHUNK, 2 * feat), jnp.float32),
            pltpu.VMEM((TICKS, LINES, feat), bf16),
            pltpu.VMEM((TICKS, LINES, feat), bf16),
            pltpu.VMEM((TICKS, LINES, feat), bf16),
            pltpu.VMEM((STEPS, LINES, feat), bf16),
            pltpu.SemaphoreType.DMA((2 * STEPS + 1,)),
            pltpu.SemaphoreType.DMA((56,)),
            pltpu.SemaphoreType.DMA((56,)),
        ],
        compiler_params=pltpu.CompilerParams(
            collective_id=8 + parity,
            has_side_effects=True,
            vmem_limit_bytes=48 * 2**20,
        ),
        cost_estimate=pl.CostEstimate(
            flops=8 * 2 * BLOCK * BLOCK * bins,
            bytes_accessed=2 * rows * width,
            transcendentals=rows * bins,
        ),
        name="pairs",
    )(reach, spectra, scores)


def branch(reach):
    size = reach.shape[0]
    group = 2 * GROUP
    margin = 2
    padded = jnp.pad(reach, (margin, size))
    index = lax.iota(jnp.int32, size)

    def at(shift):
        return padded[margin + shift : margin + shift + size]

    def right(boundary):
        return jnp.where(at(2 * boundary + 1) == 2, 1, 0)

    def left(boundary):
        return jnp.where((at(2 * boundary) == 2) | (at(2 * boundary + 1) == 1), 1, 0)

    def lanes(first):
        going = right(first) + left(first + 1) + right(first + 2)
        coming = left(first) + right(first + 1) + left(first + 2)
        return going, coming

    def over(lane):
        return jnp.maximum(lane - 1, 0)

    def flag(condition, place):
        return jnp.where(condition, 2**place, 0)

    odd = lax.rem(index, 2 * group) == group
    hosts = jnp.where(odd, 1, 0)
    going, coming = lanes(0)
    next_going, next_coming = lanes(GROUP)
    last_going, last_coming = lanes((size - group) // 2)
    edge_right, edge_left = right(3), left(3)
    edge = edge_right + edge_left > 0
    over_going, over_coming = over(going), over(coming)
    shared = jnp.maximum(
        over_going + over(next_going) + edge_left, over_coming + over(next_coming) + edge_right
    )
    two = jnp.maximum(going + hosts * (left(-1) + edge_left), coming + hosts * (right(-1) + edge_right))
    wrapped = jnp.maximum(over_going + over(last_going), over_coming + over(last_coming))
    full = over_going + over_coming > 0
    misses = (
        flag(full | edge, 0)
        | flag(jnp.where(odd, edge, shared > 1), 1)
        | flag(jnp.where(odd, shared > 1, edge), 2)
        | flag(two > 2, 3)
        | flag((index == 0) & (wrapped > 1), 2)
    )
    misses = jnp.where(lax.rem(index, group) == 0, misses, 0)
    missed = lax.reduce(misses, jnp.int32(0), lax.bitwise_or, (0,))
    return 31 - lax.clz(~missed & (missed + 1))


def body(spectra, class_scores, reach):
    if reach.shape[0] % 16:
        return plan(True, True, spectra, class_scores, reach)
    branches = [
        functools.partial(slots_plan, 1, False),
        functools.partial(pair_plan, 0),
        functools.partial(pair_plan, 1),
        functools.partial(slots_plan, 2, True),
        functools.partial(plan, True, True),
    ]
    return lax.switch(branch(reach), branches, spectra, class_scores, reach)


def solution(mesh):
    return jax.shard_map(
        body,
        mesh=mesh,
        in_specs=(P(AXES, None), P(AXES, None), P()),
        out_specs=P(AXES, None),
        check_vma=False,
    )
```

```python
import functools

import jax
import jax.numpy as jnp
from jax import lax
from jax.experimental import pallas as pl
from jax.experimental.pallas import tpu as pltpu
from jax.sharding import PartitionSpec as P

BLOCK = 512
AXES = ("blk", "sub")
GROUP = 4
MESH = pl.DeviceIdType.MESH
HALF = BLOCK // 2
PART = HALF + 16 * (HALF // 128)
SHIP = 2 * PART
NEAR, FAR, EDGE = 2, 3, 4


def kernel(two_blocks, group_edge, reach, spectra, scores, out, units, own, part, ship, ret, offer, kept,
           send_sem, recv_sem):
    bins = spectra.shape[1]
    feat = scores.shape[1]
    subs = lax.axis_size("sub")
    count = lax.axis_size("blk") * subs
    position = lax.axis_index("blk") * subs + lax.axis_index("sub")
    place = lax.rem(position, GROUP)
    odd = lax.rem(place, 2)
    across = position + 1 - 2 * odd
    core = jnp.where(place < 2, position + 2, position - 2)
    beside = position - 1 + 2 * odd
    middle = (place == 1) | (place == 2)
    outer = jnp.logical_not(middle)
    low = place < 2
    high = jnp.logical_not(low)
    has_edge = ((place == 0) & (position > 0)) | ((place == 3) & (position < count - 1))
    first = odd
    second = 1 - odd

    def copy(index, source, target, device):
        return pltpu.make_async_remote_copy(
            src_ref=source,
            dst_ref=target,
            send_sem=send_sem.at[index],
            recv_sem=recv_sem.at[index],
            device_id=(device // subs, lax.rem(device, subs)),
            device_id_type=MESH,
        )

    barrier = pltpu.get_barrier_semaphore()

    def greet(device):
        pl.semaphore_signal(
            barrier,
            inc=1,
            device_id=(device // subs, lax.rem(device, subs)),
            device_id_type=MESH,
        )

    greet(across)
    greet(core)
    beside_used = middle if two_blocks else (place < 0)
    if group_edge:
        beside_used = beside_used | has_edge

    @pl.when(beside_used)
    def _():
        greet(beside)

    def normalize(block):
        def step(i, carry):
            rows = pl.ds(pl.multiple_of(i * 64, 64), 64)
            source = pl.ds(pl.multiple_of(block * BLOCK + i * 64, 64), 64)
            values = spectra[source, :].astype(jnp.float32)
            total = jnp.sum(values, axis=1, keepdims=True)
            unit = jnp.sqrt(values) * (1.0 / jnp.sqrt(total + 1e-06))
            units[block, rows, :bins] = unit.astype(jnp.bfloat16)
            units[block, rows, bins:] = scores[source, :]
            return carry

        lax.fori_loop(0, BLOCK // 64, step, 0)

    def own_reach(index):
        return reach[2 * position + index]

    previous = jnp.maximum(2 * position - 2, 0)

    def flag(condition):
        return jnp.where(condition, 1.0, 0.0).astype(jnp.float32)

    to_next0 = flag(own_reach(0) >= 2)
    to_next1 = flag(own_reach(1) >= 1)
    to_next2 = flag(own_reach(1) >= 2)
    from_prev0 = flag(reach[previous] >= 2)
    from_prev1 = flag(reach[previous + 1] >= 1)
    from_prev2 = flag(reach[previous + 1] >= 2)
    inside = flag(own_reach(0) >= 1)

    def weights(row, column, scale, start=0, size=BLOCK):
        cosine = lax.dot_general(
            units[row, :, :bins],
            units[column, start : start + size, :bins],
            (((1,), (1,)), ((), ())),
            preferred_element_type=jnp.float32,
        )
        return (cosine * cosine * cosine * scale).astype(jnp.bfloat16)

    def forward(column, weight, start=0, size=BLOCK):
        column_scores = units[column, start : start + size, bins:]
        extended = jnp.concatenate([column_scores, jnp.ones_like(column_scores)], axis=1)
        return jnp.dot(weight, extended, preferred_element_type=jnp.float32)

    def local_pairs():
        def step(row, carry):
            own[row] = forward(row, weights(row, row, 1.0))
            own[row] += forward(1 - row, weights(row, 1 - row, inside))
            return carry

        lax.fori_loop(0, 2, step, 0)

    def remote_pairs(column, slot, scale0, scale1, halves=(0, 1)):
        start, size = halves[0] * HALF, HALF * len(halves)
        part[...] = jnp.zeros_like(part)

        def step(row, carry):
            scale = jnp.where(row == 0, scale0, scale1)
            weight = weights(row, column, scale, start, size)
            own[row] += forward(column, weight, start, size)
            part[:size, :] += lax.dot_general(
                weight,
                units[row, :, bins:],
                (((0,), (0,)), ((), ())),
                preferred_element_type=jnp.float32,
            )
            sums = jnp.dot(
                jnp.ones((8, BLOCK), jnp.bfloat16), weight, preferred_element_type=jnp.float32
            )
            for q in range(size // 128):
                part[BLOCK + 8 * q : BLOCK + 8 * q + 8, :] += sums[:, 128 * q : 128 * q + 128]
            return carry

        lax.fori_loop(0, 2, step, 0)
        for place_in, half in enumerate(halves):
            base = half * PART
            ship[slot, base : base + HALF, :] = part[
                place_in * HALF : place_in * HALF + HALF, :
            ].astype(jnp.bfloat16)
            for q in range(HALF // 128):
                row = BLOCK + 8 * (place_in * (HALF // 128) + q)
                line = part[row : row + 8, :]
                high_part = line.astype(jnp.bfloat16).astype(jnp.float32)
                ship[slot, base + HALF + 16 * q : base + HALF + 16 * q + 16, :] = jnp.concatenate(
                    [high_part, line - high_part], axis=0
                ).astype(jnp.bfloat16)

    def add_back(block, slot, scale=1.0, halves=(0, 1)):
        for half in halves:
            base = half * PART
            rows = slice(half * HALF, half * HALF + HALF)
            own[block, rows, :feat] += ret[slot, base : base + HALF, :].astype(jnp.float32) * scale
            for q in range(HALF // 128):
                line = ret[slot, base + HALF + 16 * q : base + HALF + 16 * q + 16, :]
                line = line.astype(jnp.float32)
                line = (line[0:1, :] + line[8:9, :]) * scale
                rows = slice(half * HALF + 128 * q, half * HALF + 128 * q + 128)
                own[block, rows, feat:] += jnp.broadcast_to(line, (128, 128)).T

    if group_edge:
        edge_copy = copy(0, units.at[first], units.at[EDGE], beside)
        edge_back = copy(1, ship.at[2], ret.at[2], beside)

    normalize(first)

    @pl.when(beside_used)
    def _():
        pl.semaphore_wait(barrier, 3)

    @pl.when(jnp.logical_not(beside_used))
    def _():
        pl.semaphore_wait(barrier, 2)

    if two_blocks:
        first_copy = copy(2, units.at[first], units.at[NEAR], across)
        second_copies = [
            copy(
                3 + 5 * h,
                units.at[second, pl.ds(h * HALF, HALF)],
                units.at[FAR, pl.ds(h * HALF, HALF)],
                across,
            )
            for h in range(2)
        ]
        pass_copy = copy(4, units.at[NEAR], units.at[NEAR], core)
        first_back = copy(5, ship.at[0], ret.at[0], across)
        second_backs = [
            copy(
                6 + 3 * h,
                ship.at[1, pl.ds(h * PART, PART)],
                ret.at[1, pl.ds(h * PART, PART)],
                across,
            )
            for h in range(2)
        ]
        beside_back = copy(7, ship.at[0], ret.at[2], beside)

        @pl.when(middle)
        def _():
            first_copy.start()

    if group_edge:

        @pl.when(has_edge)
        def _():
            edge_copy.start()

    normalize(second)

    def edge_pairs():
        @pl.when(has_edge)
        def _():
            edge_copy.wait_recv()
            is_left = place == 3
            remote_pairs(
                EDGE,
                2,
                jnp.where(is_left, to_next0, 0.0),
                jnp.where(is_left, to_next1, from_prev2),
            )
            edge_back.start()

    def edge_end():
        @pl.when(has_edge)
        def _():
            edge_back.wait_recv()
            add_back(first, 2)
            edge_copy.wait_send()
            edge_back.wait_send()

    if two_blocks:
        local_pairs()

        @pl.when(middle)
        def _():
            first_copy.wait_send()
            for half in range(2):
                second_copies[half].start()
            pass_copy.wait_recv()
            is_left = place == 1
            remote_pairs(
                NEAR,
                0,
                jnp.where(is_left, to_next0, 0.0),
                jnp.where(is_left, to_next1, from_prev2),
            )
            beside_back.start()
            beside_back.wait_recv()
            add_back(first, 2)
            first_back.wait_recv()
            add_back(first, 0)
            for half in range(2):
                second_copies[half].wait_send()
                second_backs[half].wait_recv()
                add_back(second, 1, halves=(half,))
            beside_back.wait_send()

        @pl.when(outer)
        def _():
            first_copy.wait_recv()
            pass_copy.start()
            is_left = place == 0
            remote_pairs(
                NEAR,
                0,
                jnp.where(is_left, 0.0, from_prev0),
                jnp.where(is_left, to_next2, 0.0),
            )
            first_back.start()

        if group_edge:
            edge_pairs()

        @pl.when(outer)
        def _():
            is_left = place == 0
            for half in range(2):
                second_copies[half].wait_recv()
                remote_pairs(
                    FAR,
                    1,
                    jnp.where(is_left, to_next0, from_prev1),
                    jnp.where(is_left, to_next1, from_prev2),
                    halves=(half,),
                )
                second_backs[half].start()
            pass_copy.wait_send()
            first_back.wait_send()
            for half in range(2):
                second_backs[half].wait_send()

    else:
        leads = jnp.where(place < 3, jnp.maximum(to_next0, to_next1), 0.0)
        follows = jnp.where(place > 0, jnp.maximum(from_prev0, from_prev1), 0.0)
        has_role = jnp.maximum(leads, follows)
        gather_copies, cross_copies, pass_copies = [], [], []
        for half in range(2):
            rows = pl.ds(half * HALF, HALF)
            near = units.at[NEAR, rows]
            gather_copies.append(copy(2 + 6 * half, offer.at[rows], kept.at[rows], core))
            cross_copies.append(copy(3 + 6 * half, offer.at[rows], near, across))
            pass_copies.append(copy(4 + 6 * half, near, near, core))
        gather_back = copy(5, ship.at[0], ret.at[0], core)
        cross_back = copy(6, ship.at[0], ret.at[1], across)
        pass_back = copy(7, ret.at[1], ret.at[1], core)

        def blend(target, yes, no, scale, rows):
            def step(i, carry):
                chunk = pl.ds(pl.multiple_of(i * rows, rows), rows)
                a = yes[chunk, :].astype(jnp.float32) * scale
                b = no[chunk, :].astype(jnp.float32) * (1.0 - scale)
                target[chunk, :] = (a + b).astype(target.dtype)
                return carry

            lax.fori_loop(0, target.shape[0] // rows, step, 0)

        for half in range(2):
            rows = pl.ds(half * HALF, HALF)
            blend(offer.at[rows], units.at[1, rows], units.at[0, rows], leads, 64)

            @pl.when(high)
            def _():
                gather_copies[half].start()

        @pl.when(low)
        def _():
            for half in range(2):
                rows = pl.ds(half * HALF, HALF)
                gather_copies[half].wait_recv()
                blend(offer.at[rows], offer.at[rows], kept.at[rows], has_role, 64)
                cross_copies[half].start()

        local_pairs()

        @pl.when(low)
        def _():
            for half in range(2):
                cross_copies[half].wait_recv()
                pass_copies[half].start()

        @pl.when(high)
        def _():
            for half in range(2):
                pass_copies[half].wait_recv()

        remote_pairs(
            NEAR,
            0,
            jnp.where(place < 3, to_next0, 0.0) * leads,
            jnp.where(place < 3, to_next1, 0.0) * leads + from_prev2 * follows,
        )

        @pl.when(high)
        def _():
            gather_back.start()

        @pl.when(low)
        def _():
            gather_back.wait_recv()
            blend(ship.at[0], ship.at[0], ret.at[0], has_role, SHIP)
            cross_back.start()

        if group_edge:
            edge_pairs()

        @pl.when(low)
        def _():
            cross_back.wait_recv()
            pass_back.start()

        @pl.when(high)
        def _():
            pass_back.wait_recv()

        add_back(1, 1, leads)
        add_back(0, 1, follows)

        @pl.when(low)
        def _():
            for half in range(2):
                cross_copies[half].wait_send()
                pass_copies[half].wait_send()
            cross_back.wait_send()
            pass_back.wait_send()

        @pl.when(high)
        def _():
            for half in range(2):
                gather_copies[half].wait_send()
            gather_back.wait_send()

    if group_edge:
        edge_end()

    for block in range(2):
        out[block * BLOCK : (block + 1) * BLOCK, :] = own[block, :, :feat] / own[block, :, feat:]


def plan(two_blocks, group_edge, spectra, scores, reach):
    rows, bins = spectra.shape
    feat = scores.shape[1]
    width = bins + feat
    vmem = pl.BlockSpec(memory_space=pltpu.VMEM)
    return pl.pallas_call(
        functools.partial(kernel, two_blocks, group_edge),
        out_shape=jax.ShapeDtypeStruct((rows, feat), jnp.float32),
        in_specs=[pl.BlockSpec(memory_space=pltpu.SMEM), vmem, vmem],
        out_specs=vmem,
        scratch_shapes=[
            pltpu.VMEM((5, BLOCK, width), jnp.bfloat16),
            pltpu.VMEM((2, BLOCK, 2 * feat), jnp.float32),
            pltpu.VMEM((BLOCK + 8 * (BLOCK // 128), feat), jnp.float32),
            pltpu.VMEM((3, SHIP, feat), jnp.bfloat16),
            pltpu.VMEM((3, SHIP, feat), jnp.bfloat16),
            pltpu.VMEM((16 if two_blocks else BLOCK, width), jnp.bfloat16),
            pltpu.VMEM((16 if two_blocks else BLOCK, width), jnp.bfloat16),
            pltpu.SemaphoreType.DMA((12,)),
            pltpu.SemaphoreType.DMA((12,)),
        ],
        compiler_params=pltpu.CompilerParams(
            collective_id=2 * int(two_blocks) + int(group_edge),
            has_side_effects=True,
            vmem_limit_bytes=48 * 2**20,
        ),
        cost_estimate=pl.CostEstimate(
            flops=8 * 2 * BLOCK * BLOCK * bins,
            bytes_accessed=2 * rows * width,
            transcendentals=rows * bins,
        ),
        name="network",
    )(reach, spectra, scores)


CHUNK = 128
PIECE = CHUNK // 2
STEPS = BLOCK // CHUNK
LINES = CHUNK + 16
AHEAD = 3
DELAY = 4
EX, XS, FW, PRE, POST, RX, RF, RE = 0, 8, 16, 24, 32, 40, 48, 56


def slots_kernel(slots, edges, turn, reach, spectra, marks, out, raw, scores, units, mate, pre, offer, got, past, own, part, ship,
                 ship_edge, ret, ret_mate, ret_edge, load_sem, send_sem, recv_sem):
    bins = spectra.shape[1]
    feat = marks.shape[1]
    total_steps = slots * STEPS
    subs = lax.axis_size("sub")
    count = lax.axis_size("blk") * subs
    position = lax.axis_index("blk") * subs + lax.axis_index("sub")
    place = lax.rem(position, GROUP)
    group = position // GROUP
    side = lax.rem(place, 2)
    core = place // 2
    base = position - place
    odd_group = lax.rem(group + turn, 2) == 1
    even_group = lax.rem(group + turn, 2) == 0
    across = position + 1 - 2 * side
    partner = position + 2 - 4 * core
    corner = across + 2 - 4 * core
    at_end = (place == 0) | (place == 3)
    has_edge = ((place == 0) & (position > 0)) | ((place == 3) & (position < count - 1))
    beside = jnp.where(place == 0, position - 1, position + 1)
    is_edge = has_edge & even_group
    host = jnp.where(side == 0, base - GROUP, base + GROUP) + side
    is_host = odd_group & jnp.where(side == 1, base >= GROUP, base + GROUP < count)
    guest = jnp.where(side == 0, base + GROUP, base - GROUP + 3)

    def place_of(device):
        return (device // subs, lax.rem(device, subs))

    def copy(index, source, target, device):
        return pltpu.make_async_remote_copy(
            src_ref=source,
            dst_ref=target,
            send_sem=send_sem.at[index],
            recv_sem=recv_sem.at[index],
            device_id=place_of(device),
            device_id_type=MESH,
        )

    def load_copy(k, block):
        rows = pl.ds(pl.multiple_of(block * BLOCK + k * CHUNK, CHUNK), CHUNK)
        return pltpu.make_async_copy(spectra.at[rows], raw.at[rows], load_sem.at[2 * k + block])

    mark_copy = pltpu.make_async_copy(marks, scores, load_sem.at[2 * STEPS])
    for block in range(2):
        load_copy(0, block).start()
    mark_copy.start()
    for k in range(1, STEPS):
        for block in range(2):
            load_copy(k, block).start()

    barrier = pltpu.get_barrier_semaphore()

    def greet(device):
        pl.semaphore_signal(barrier, inc=1, device_id=place_of(device), device_id_type=MESH)

    greet(across)
    greet(partner)
    greet(corner)
    if edges:

        @pl.when(has_edge)
        def _():
            greet(beside)

        @pl.when(is_edge)
        def _():
            greet(host)
            greet(host + 2)

        @pl.when(is_host)
        def _():
            greet(guest)

    def active(boundary):
        inside = (boundary >= 0) & (boundary < count - 1)
        at = jnp.clip(boundary, 0, count - 2)
        a, b = reach[2 * at], reach[2 * at + 1]
        right = jnp.where(inside & (b == 2), 1, 0)
        left = jnp.where(inside & ((a == 2) | (b == 1)), 1, 0)
        return right, left

    bounds = [active(base + i - 1) for i in range(5)]
    rights = [b[0] for b in bounds]
    lefts = [b[1] for b in bounds]
    hosts = jnp.where(odd_group, 1, 0) if edges else 0

    def assign(inner, late, early):
        d1, d2, d3 = inner
        if slots == 1:
            return ((d1, d2, d3, late * hosts, early * hosts),)
        late, early = late * hosts, early * hosts
        free = 1 - late
        f1 = d1 * free
        f2 = d2 * (1 - d1) * free
        f3 = d3 * (1 - d1) * (1 - d2) * free
        return ((f1, f2, f3, late, 0), (d1 - f1, d2 - f2, d3 - f3, 0, early))

    going = assign((rights[1], lefts[2], rights[3]), lefts[0], lefts[4])
    coming = assign((lefts[1], rights[2], lefts[3]), rights[4], rights[0])

    def pick(options, index):
        value = options[-1]
        for i in range(len(options) - 2, -1, -1):
            value = jnp.where(index == i, options[i], value)
        return value

    def slot_flags(slot):
        q, r = going[slot], coming[slot]
        right_out = pick([q[0], r[1], q[2], r[3]], place)
        left_out = pick([q[3], r[0], q[1], r[2]], place)
        mate_right = pick([q[2], r[3], q[0], r[1]], place)
        mate_left = pick([q[1], r[2], q[3], r[0]], place)
        guest_in = jnp.where(side == 0, q[4], r[4])
        right_in = pick([r[4], q[0], r[1], q[2]], place)
        left_in = pick([r[0], q[1], r[2], q[4]], place)
        return right_out, left_out, mate_right, mate_left, guest_in, right_in, left_in

    flags = [slot_flags(s) for s in range(slots)]

    def flag_at(step, which):
        if slots == 1:
            return flags[0][which]
        return jnp.where(step < STEPS, flags[0][which], flags[1][which])

    own0, own1 = reach[2 * position], reach[2 * position + 1]
    close0 = jnp.where(own0 == 2, 1, 0)
    close1 = jnp.where(own1 == 1, 1, 0)
    inside = jnp.where(own0 >= 1, 1.0, 0.0).astype(jnp.float32)

    edge_right_in = jnp.where(place == 0, rights[0], 0)
    edge_left_in = jnp.where(place == 3, lefts[4], 0)
    edge_out0 = jnp.where(place == 0, lefts[0], 0).astype(jnp.float32)
    edge_out1 = jnp.where(place == 3, rights[4], 0).astype(jnp.float32)

    def chunk_of(step):
        return lax.rem(step, STEPS)

    def normalize(k, which):
        def one(block, carry):
            row = k * CHUNK + which * PIECE
            source = pl.ds(pl.multiple_of(block * BLOCK + row, 64), 64)
            values = raw[source, :].astype(jnp.float32)
            total = jnp.sum(values, axis=1, keepdims=True)
            unit = jnp.sqrt(values) * (1.0 / jnp.sqrt(total + 1e-06))
            units[source, :bins] = unit.astype(jnp.bfloat16)
            units[source, bins:] = scores[source, :]
            return carry

        lax.fori_loop(0, 2, one, 0)

    def piece(block, k, which):
        start = block * BLOCK + k * CHUNK + which * PIECE
        return units.at[pl.ds(pl.multiple_of(start, PIECE), PIECE)]

    def mate_copy(k, block):
        return copy(EX + 2 * k + block, piece(block, k, 1 - core), mate.at[k, block], partner)

    def pre_copy(k, which):
        block = jnp.where(place == 0, 0, 1)
        return copy(PRE + 2 * k + which, piece(block, k, which), pre.at[k], host + 2 * which)

    def pre_recv(k):
        return copy(PRE + 2 * k + core, pre.at[k], pre.at[k], across)

    def cross_copy(step):
        rows = pl.ds(pl.multiple_of(core * PIECE, PIECE), PIECE)
        return copy(XS + step, offer.at[step], got.at[step, rows], across)

    def forward_copy(step):
        rows = pl.ds(pl.multiple_of(core * PIECE, PIECE), PIECE)
        return copy(FW + step, got.at[step, rows], got.at[step, rows], partner)

    def post_copy(step):
        rows = pl.ds(pl.multiple_of(core * PIECE, PIECE), PIECE)
        return copy(POST + 2 * step + core, got.at[step, rows], past.at[step, rows], guest)

    def post_recv(k, which):
        rows = pl.ds(which * PIECE, PIECE)
        return copy(POST + 2 * k + which, past.at[k, rows], past.at[k, rows], across)

    def back_copy(step):
        return copy(RX + step, ship.at[step], ret.at[step], across)

    def back_mate(step):
        return copy(RF + step, ret.at[step], ret_mate.at[step], partner)

    final = total_steps - 1

    def back_corner():
        return copy(RF + final, ship.at[final], ret_mate.at[final], corner)

    def edge_back(k, source):
        return copy(RE + k, source, ret_edge.at[k], beside)

    early_slot = slots - 1

    def send(step):
        k = chunk_of(step)

        @pl.when(step < STEPS)
        def _():
            for block in range(2):
                mate_copy(k, block).wait_recv()

        right_out = flag_at(step, 0)
        mate_right = flag_at(step, 2)
        mate_left = flag_at(step, 3)
        guest_in = flag_at(step, 4)

        def one(i, carry):
            at = pl.ds(pl.multiple_of(i * 16, 16), 16)
            first = k * CHUNK + core * PIECE + i * 16
            mine0 = pl.ds(pl.multiple_of(first, 16), 16)
            mine1 = pl.ds(pl.multiple_of(BLOCK + first, 16), 16)
            value = jnp.where(right_out == 1, units[mine1, :], units[mine0, :])
            value = jnp.where(mate_right == 1, mate[k, 1, at, :], value)
            value = jnp.where(mate_left == 1, mate[k, 0, at, :], value)
            offer[step, at, :] = value
            return carry

        lax.fori_loop(0, PIECE // 16, one, 0)
        if edges:

            @pl.when(is_host & (step >= early_slot * STEPS))
            def _():
                pre_recv(k).wait_recv()

                def swap(i, carry):
                    at = pl.ds(pl.multiple_of(i * 16, 16), 16)
                    offer[step, at, :] = jnp.where(guest_in == 1, pre[k, at, :], offer[step, at, :])
                    return carry

                lax.fori_loop(0, PIECE // 16, swap, 0)

        cross_copy(step).start()

    def local_pairs():
        def one(row, carry):
            rows = pl.ds(pl.multiple_of(row * BLOCK, BLOCK), BLOCK)
            cosine = lax.dot_general(
                units[rows, :bins],
                units[:, :bins],
                (((1,), (1,)), ((), ())),
                preferred_element_type=jnp.float32,
            )
            column = lax.broadcasted_iota(jnp.int32, (1, 2 * BLOCK), 1) // BLOCK
            scale = jnp.where(column == row, 1.0, inside)
            weight = (cosine * cosine * cosine * scale).astype(jnp.bfloat16)
            extended = jnp.concatenate([units[:, bins:], jnp.ones((2 * BLOCK, feat), jnp.bfloat16)], axis=1)
            own[rows, :] = jnp.dot(weight, extended, preferred_element_type=jnp.float32)
            return carry

        lax.fori_loop(0, 2, one, 0)

    def chunk_pairs(read, scale0, scale1, target):
        cosine = lax.dot_general(
            read(slice(0, bins)),
            units[:, :bins],
            (((1,), (1,)), ((), ())),
            preferred_element_type=jnp.float32,
        )
        column = lax.broadcasted_iota(jnp.int32, (1, 2 * BLOCK), 1)
        scale = jnp.where(column < BLOCK, scale0.astype(jnp.float32), scale1.astype(jnp.float32))
        weight = (cosine * cosine * cosine * scale).astype(jnp.bfloat16)
        extended = jnp.concatenate([units[:, bins:], jnp.ones((2 * BLOCK, feat), jnp.bfloat16)], axis=1)
        part[...] = jnp.dot(weight, extended, preferred_element_type=jnp.float32)
        column_scores = read(slice(bins, bins + feat))
        extended = jnp.concatenate([column_scores, jnp.ones_like(column_scores)], axis=1)
        own[...] += lax.dot_general(
            weight, extended, (((0,), (0,)), ((), ())), preferred_element_type=jnp.float32
        )
        target[:CHUNK, :] = part[:, :feat].astype(jnp.bfloat16)
        line = part[:, feat:].T[:8, :]
        high_part = line.astype(jnp.bfloat16).astype(jnp.float32)
        target[CHUNK:, :] = jnp.concatenate([high_part, line - high_part], axis=0).astype(jnp.bfloat16)

    def add_back(k, lines, scale0, scale1):
        sums = lines[:CHUNK, :].astype(jnp.float32)
        line = lines[CHUNK:, :].astype(jnp.float32)
        line = line[0:1, :] + line[8:9, :]
        degree = jnp.broadcast_to(line, (CHUNK, CHUNK)).T
        for block, scale in enumerate((scale0, scale1)):
            rows = pl.ds(pl.multiple_of(block * BLOCK + k * CHUNK, CHUNK), CHUNK)
            own[rows, :feat] += sums * scale
            own[rows, feat:] += degree * scale

    greetings = 3
    if edges:
        greetings = (
            3 + jnp.where(has_edge, 1, 0) + jnp.where(is_edge, 2, 0) + jnp.where(is_host, 1, 0)
        )

    mark_copy.wait()

    def prepare(k, carry):
        for block in range(2):
            load_copy(k, block).wait()
        normalize(k, 1 - core)

        @pl.when(k == 0)
        def _():
            pl.semaphore_wait(barrier, greetings)

        for block in range(2):
            mate_copy(k, block).start()
        normalize(k, core)
        if edges:

            @pl.when(is_edge)
            def _():
                for which in range(2):
                    pre_copy(k, which).start()

        @pl.when(k < AHEAD)
        def _():
            send(k)

        return carry

    lax.fori_loop(0, STEPS, prepare, 0)
    local_pairs()

    def edge_step(k):
        for which in range(2):
            post_recv(k, which).wait_recv()
        first = edge_right_in + edge_left_in * close0
        second = edge_right_in + edge_left_in * close1
        chunk_pairs(lambda columns: past[k, :, columns], first, second, ship_edge.at[k])
        edge_back(k, ship_edge.at[k]).start()

    def step_fn(step, carry):
        @pl.when(step < total_steps)
        def _():
            cross_copy(step).wait_recv()
            forward_copy(step).start()
            if edges:

                @pl.when(is_host & (step < STEPS))
                def _():
                    post_copy(step).start()

            @pl.when(step + AHEAD < total_steps)
            def _():
                send(step + AHEAD)

            forward_wait(step)
            right_in = flag_at(step, 5)
            left_in = flag_at(step, 6)
            first = right_in + left_in * close0
            second = right_in + left_in * close1
            chunk_pairs(lambda columns: got[step, :, columns], first, second, ship.at[step])
            back_copy(step).start()

            @pl.when(step == final)
            def _():
                back_corner().start()

            if edges:

                @pl.when(has_edge & odd_group & (step >= early_slot * STEPS))
                def _():
                    edge_back(chunk_of(step), ship.at[step]).start()

        if edges:

            @pl.when(is_edge & (step >= STEPS - 1) & (step < 2 * STEPS - 1))
            def _():
                edge_step(step - (STEPS - 1))

        @pl.when((step >= DELAY) & (step < total_steps + DELAY))
        def _():
            back_copy(step - DELAY).wait_recv()

            @pl.when(step - DELAY < final)
            def _():
                back_mate(step - DELAY).start()

        @pl.when(step > DELAY)
        def _():
            done = step - DELAY - 1
            back_mate(done).wait_recv()
            scale0 = flag_at(done, 1).astype(jnp.float32)
            scale1 = flag_at(done, 0).astype(jnp.float32)
            both = ret[done].astype(jnp.float32) + ret_mate[done].astype(jnp.float32)
            add_back(chunk_of(done), both, scale0, scale1)

        return carry

    def forward_wait(step):
        rows = pl.ds(pl.multiple_of((1 - core) * PIECE, PIECE), PIECE)
        copy(FW + step, got.at[step, rows], got.at[step, rows], partner).wait_recv()

    lax.fori_loop(0, total_steps + DELAY + 1, step_fn, 0)

    if edges:

        @pl.when(has_edge)
        def _():
            def one(k, carry):
                edge_back(k, ship_edge.at[k]).wait_recv()
                add_back(k, ret_edge[k], edge_out0, edge_out1)
                return carry

            lax.fori_loop(0, STEPS, one, 0)

    out[...] = own[:, :feat] / own[:, feat:]

    def finish(step, carry):
        cross_copy(step).wait_send()
        forward_copy(step).wait_send()
        back_copy(step).wait_send()
        back_mate(step).wait_send()
        return carry

    lax.fori_loop(0, total_steps, finish, 0)

    def finish_chunk(k, carry):
        for block in range(2):
            mate_copy(k, block).wait_send()
        if edges:

            @pl.when(has_edge)
            def _():
                edge_back(k, ship_edge.at[k]).wait_send()

            @pl.when(is_edge)
            def _():
                for which in range(2):
                    pre_copy(k, which).wait_send()

            @pl.when(is_host)
            def _():
                post_copy(k).wait_send()

        return carry

    lax.fori_loop(0, STEPS, finish_chunk, 0)


def slots_plan(slots, edges, turn, spectra, scores, reach):
    rows, bins = spectra.shape
    feat = scores.shape[1]
    width = bins + feat
    steps = slots * STEPS
    extra = STEPS if edges else 1
    vmem = pl.BlockSpec(memory_space=pltpu.VMEM)
    bf16 = jnp.bfloat16
    return pl.pallas_call(
        functools.partial(slots_kernel, slots, edges, turn),
        out_shape=jax.ShapeDtypeStruct((rows, feat), jnp.float32),
        in_specs=[pl.BlockSpec(memory_space=pltpu.SMEM)] + [pl.BlockSpec(memory_space=pltpu.HBM)] * 2,
        out_specs=vmem,
        scratch_shapes=[
            pltpu.VMEM((rows, bins), bf16),
            pltpu.VMEM((rows, feat), bf16),
            pltpu.VMEM((rows, width), bf16),
            pltpu.VMEM((STEPS, 2, PIECE, width), bf16),
            pltpu.VMEM((extra, PIECE, width), bf16),
            pltpu.VMEM((steps, PIECE, width), bf16),
            pltpu.VMEM((steps, CHUNK, width), bf16),
            pltpu.VMEM((extra, CHUNK, width), bf16),
            pltpu.VMEM((rows, 2 * feat), jnp.float32),
            pltpu.VMEM((CHUNK, 2 * feat), jnp.float32),
            pltpu.VMEM((steps, LINES, feat), bf16),
            pltpu.VMEM((extra, LINES, feat), bf16),
            pltpu.VMEM((steps, LINES, feat), bf16),
            pltpu.VMEM((steps, LINES, feat), bf16),
            pltpu.VMEM((extra, LINES, feat), bf16),
            pltpu.SemaphoreType.DMA((2 * STEPS + 1,)),
            pltpu.SemaphoreType.DMA((60,)),
            pltpu.SemaphoreType.DMA((60,)),
        ],
        compiler_params=pltpu.CompilerParams(
            collective_id=4 + 2 * (slots - 1) + int(edges) + 3 * turn,
            has_side_effects=True,
            vmem_limit_bytes=48 * 2**20,
        ),
        cost_estimate=pl.CostEstimate(
            flops=8 * 2 * BLOCK * BLOCK * bins,
            bytes_accessed=2 * rows * width,
            transcendentals=rows * bins,
        ),
        name="slots",
    )(reach, spectra, scores)


TICKS = 2 * STEPS
QUARTER = CHUNK // 4
LEAD = 3
OPEN = 2
P_EX, P_XS, P_FW, P_RX, P_RF, P_PRE, P_POST, P_PF, P_RE = 0, 8, 16, 24, 32, 40, 44, 48, 52


def pair_kernel(parity, reach, spectra, marks, out, raw, scores, units, mate, lend, borrow, offer, offer_pair, got, own, part,
                ship, ret, ret_mate, ret_edge, load_sem, send_sem, recv_sem):
    bins = spectra.shape[1]
    feat = marks.shape[1]
    subs = lax.axis_size("sub")
    count = lax.axis_size("blk") * subs
    position = lax.axis_index("blk") * subs + lax.axis_index("sub")
    place = lax.rem(position, GROUP)
    group = position // GROUP
    side = lax.rem(place, 2)
    core = place // 2
    base = position - place
    upper = lax.rem(group + parity, 2)
    across = position + 1 - 2 * side
    partner = position + 2 - 4 * core
    corner = across + 2 - 4 * core
    shift = jnp.where(upper == 1, count - GROUP, GROUP)
    pair = lax.rem(position + shift, count)
    pair_base = pair - place
    low_base = jnp.where(upper == 1, pair_base, base)

    def place_of(device):
        return (device // subs, lax.rem(device, subs))

    def copy(index, source, target, device):
        return pltpu.make_async_remote_copy(
            src_ref=source,
            dst_ref=target,
            send_sem=send_sem.at[index],
            recv_sem=recv_sem.at[index],
            device_id=place_of(device),
            device_id_type=MESH,
        )

    def load_copy(k, block):
        rows = pl.ds(pl.multiple_of(block * BLOCK + k * CHUNK, CHUNK), CHUNK)
        return pltpu.make_async_copy(spectra.at[rows], raw.at[rows], load_sem.at[2 * k + block])

    mark_copy = pltpu.make_async_copy(marks, scores, load_sem.at[2 * STEPS])
    for block in range(2):
        load_copy(0, block).start()
    mark_copy.start()
    for k in range(1, STEPS):
        for block in range(2):
            load_copy(k, block).start()

    barrier = pltpu.get_barrier_semaphore()
    for device in (across, partner, corner, pair):
        pl.semaphore_signal(barrier, inc=1, device_id=place_of(device), device_id_type=MESH)

    def active(boundary):
        within = boundary < count - 1
        at = jnp.minimum(boundary, count - 2)
        a, b = reach[2 * at], reach[2 * at + 1]
        right = jnp.where(within & (b == 2), 1, 0)
        left = jnp.where(within & ((a == 2) | (b == 1)), 1, 0)
        return right, left

    def lanes(first):
        (r0, l0), (r1, l1), (r2, l2) = [active(first + i) for i in range(3)]
        result = []
        for d1, d2, d3 in ((r0, l1, r2), (l0, r1, l2)):
            f1, f2, f3 = d1, d2 * (1 - d1), d3 * (1 - d1) * (1 - d2)
            result.append(((f1, f2, f3), (d1 - f1, d2 - f2, d3 - f3)))
        return result

    going, coming = lanes(base)
    pair_going, pair_coming = lanes(pair_base)
    edge_right, edge_left = active(low_base + 3)
    up = upper
    down = 1 - upper

    def pick(options):
        value = options[-1]
        for i in range(len(options) - 2, -1, -1):
            value = jnp.where(place == i, options[i], value)
        return value

    def lane_flags(which):
        q, r = going[which], coming[which]
        last = 1 if which else 0
        right_out = pick([q[0], r[1], q[2], 0])
        left_out = pick([0, r[0], q[1], r[2]])
        mate_right = pick([q[2], last * edge_right * down, q[0], r[1]])
        mate_left = pick([q[1], r[2], last * edge_left * up, r[0]])
        right_in = pick([last * edge_right * up, q[0], r[1], q[2]])
        left_in = pick([r[0], q[1], r[2], last * edge_left * down])
        return right_out, left_out, mate_right, mate_left, right_in, left_in

    own_lane, pair_lane = lane_flags(0), lane_flags(1)
    edge_out0 = jnp.where(place == 0, edge_left * up, 0)
    edge_out1 = jnp.where(place == 3, edge_right * down, 0)
    pair_sum = jnp.where(
        side == 0,
        sum(pair_going[1]) + edge_left * down,
        sum(pair_coming[1]) + edge_right * up,
    )

    own0, own1 = reach[2 * position], reach[2 * position + 1]
    close0 = jnp.where(own0 == 2, 1, 0)
    close1 = jnp.where(own1 == 1, 1, 0)
    inside = jnp.where(own0 >= 1, 1.0, 0.0).astype(jnp.float32)

    sends_edge = ((upper == 0) & (place == 0)) | ((upper == 1) & (place == 3))
    takes_edge = ((upper == 1) & (place == 0)) | ((upper == 0) & (place == 3))

    def shared(tick):
        return (tick >= OPEN) & (tick < OPEN + STEPS)

    def alone(tick):
        return ((tick >= 0) & (tick < OPEN)) | ((tick >= OPEN + STEPS) & (tick < TICKS))

    def chunk_of(tick):
        return jnp.where(tick < OPEN, tick, tick - STEPS)

    def normalize(k, which):
        def one(block, carry):
            row = k * CHUNK + which * PIECE
            source = pl.ds(pl.multiple_of(block * BLOCK + row, 64), 64)
            values = raw[source, :].astype(jnp.float32)
            total = jnp.sum(values, axis=1, keepdims=True)
            unit = jnp.sqrt(values) * (1.0 / jnp.sqrt(total + 1e-06))
            units[source, :bins] = unit.astype(jnp.bfloat16)
            units[source, bins:] = scores[source, :]
            return carry

        lax.fori_loop(0, 2, one, 0)

    def half_rows(tick, which):
        return got.at[pl.ds(pl.multiple_of(tick * CHUNK + which * PIECE, PIECE), PIECE)]

    def quarter_rows(tick, which, level):
        start = tick * CHUNK + which * PIECE + level * QUARTER
        return got.at[pl.ds(pl.multiple_of(start, QUARTER), QUARTER)]

    def mate_copy(k, block):
        rows = pl.ds(pl.multiple_of(block * BLOCK + k * CHUNK + (1 - core) * PIECE, PIECE), PIECE)
        return copy(P_EX + 2 * k + block, units.at[rows], mate.at[k, block], partner)

    def pre_copy(k):
        return copy(P_PRE + k, lend.at[k], borrow.at[k], pair)

    def cross_alone(tick):
        return copy(P_XS + tick, offer.at[chunk_of(tick)], half_rows(tick, core), across)

    def cross_shared(tick):
        return copy(P_XS + tick, offer_pair.at[tick - OPEN], quarter_rows(tick, core, upper), across)

    def forward_alone(tick, which):
        rows = half_rows(tick, which)
        return copy(P_FW + tick, rows, rows, partner)

    def forward_shared(tick, which):
        rows = quarter_rows(tick, which, upper)
        return copy(P_FW + tick, rows, rows, partner)

    def post_copy(k, level):
        rows = quarter_rows(k + OPEN, core, level)
        return copy(P_POST + k, rows, rows, pair)

    def post_forward(k, which):
        rows = quarter_rows(k + OPEN, which, 1 - upper)
        return copy(P_PF + k, rows, rows, partner)

    def back_copy(tick):
        return copy(P_RX + tick, ship.at[tick], ret.at[tick], across)

    def back_mate(tick):
        return copy(P_RF + tick, ret.at[tick], ret_mate.at[tick], partner)

    def back_corner():
        return copy(P_RF + TICKS - 1, ship.at[TICKS - 1], ret_mate.at[TICKS - 1], corner)

    def edge_back(k):
        return copy(P_RE + k, ret_mate.at[k + OPEN], ret_edge.at[k], pair)

    def choose_rows(flags, k, start, i):
        right_out, left_out, mate_right, mate_left = flags
        at = pl.ds(pl.multiple_of(start + i * 16, 16), 16)
        first = k * CHUNK + core * PIECE + start + i * 16
        mine0 = pl.ds(pl.multiple_of(first, 16), 16)
        mine1 = pl.ds(pl.multiple_of(BLOCK + first, 16), 16)
        value = jnp.where(right_out == 1, units[mine1, :], units[mine0, :])
        value = jnp.where(mate_right == 1, mate[k, 1, at, :], value)
        return jnp.where(mate_left == 1, mate[k, 0, at, :], value)

    pair_right_out = pair_lane[0] + edge_out1
    pair_flags = (pair_right_out,) + pair_lane[1:4]

    def offer_to_pair(k):
        def one(i, carry):
            rows = pl.ds(pl.multiple_of(i * 16, 16), 16)
            lend[k, rows, :] = choose_rows(pair_flags, k, (1 - upper) * QUARTER, i)
            return carry

        lax.fori_loop(0, QUARTER // 16, one, 0)
        pre_copy(k).start()

    def send_alone(tick):
        k = chunk_of(tick)

        def one(i, carry):
            rows = pl.ds(pl.multiple_of(i * 16, 16), 16)
            offer[k, rows, :] = choose_rows(own_lane[:4], k, 0, i)
            return carry

        lax.fori_loop(0, PIECE // 16, one, 0)
        cross_alone(tick).start()

    def send_shared(tick):
        k = tick - OPEN
        pre_copy(k).wait_recv()

        def one(i, carry):
            rows = pl.ds(pl.multiple_of(i * 16, 16), 16)
            value = choose_rows(pair_flags, k, upper * QUARTER, i)
            offer_pair[k, rows, :] = jnp.where(pair_sum > 0, borrow[k, rows, :], value)
            return carry

        lax.fori_loop(0, QUARTER // 16, one, 0)
        cross_shared(tick).start()

    def send(tick):
        @pl.when(alone(tick))
        def _():
            send_alone(tick)

        @pl.when(shared(tick))
        def _():
            send_shared(tick)

    def local_pairs():
        def one(row, carry):
            rows = pl.ds(pl.multiple_of(row * BLOCK, BLOCK), BLOCK)
            cosine = lax.dot_general(
                units[rows, :bins],
                units[:, :bins],
                (((1,), (1,)), ((), ())),
                preferred_element_type=jnp.float32,
            )
            column = lax.broadcasted_iota(jnp.int32, (1, 2 * BLOCK), 1) // BLOCK
            scale = jnp.where(column == row, 1.0, inside)
            weight = (cosine * cosine * cosine * scale).astype(jnp.bfloat16)
            extended = jnp.concatenate([units[:, bins:], jnp.ones((2 * BLOCK, feat), jnp.bfloat16)], axis=1)
            own[rows, :] = jnp.dot(weight, extended, preferred_element_type=jnp.float32)
            return carry

        lax.fori_loop(0, 2, one, 0)

    def chunk_pairs(tick, chunks, flags):
        first = (flags[4] + flags[5] * close0).astype(jnp.float32)
        second = (flags[4] + flags[5] * close1).astype(jnp.float32)
        size = chunks * CHUNK
        rows = pl.ds(pl.multiple_of(tick * CHUNK, CHUNK), size)
        cosine = lax.dot_general(
            got[rows, :bins],
            units[:, :bins],
            (((1,), (1,)), ((), ())),
            preferred_element_type=jnp.float32,
        )
        column = lax.broadcasted_iota(jnp.int32, (1, 2 * BLOCK), 1)
        scale = jnp.where(column < BLOCK, first, second)
        weight = (cosine * cosine * cosine * scale).astype(jnp.bfloat16)
        extended = jnp.concatenate([units[:, bins:], jnp.ones((2 * BLOCK, feat), jnp.bfloat16)], axis=1)
        part[:size, :] = jnp.dot(weight, extended, preferred_element_type=jnp.float32)
        extended = jnp.concatenate([got[rows, bins:], jnp.ones((size, feat), jnp.bfloat16)], axis=1)
        own[...] += lax.dot_general(
            weight, extended, (((0,), (0,)), ((), ())), preferred_element_type=jnp.float32
        )
        for i in range(chunks):
            lines = slice(i * CHUNK, i * CHUNK + CHUNK)
            ship[tick + i, :CHUNK, :] = part[lines, :feat].astype(jnp.bfloat16)
            line = part[lines, feat:].T[:8, :]
            high_part = line.astype(jnp.bfloat16).astype(jnp.float32)
            ship[tick + i, CHUNK:, :] = jnp.concatenate([high_part, line - high_part], axis=0).astype(
                jnp.bfloat16
            )
            back_copy(tick + i).start()

    mark_copy.wait()

    def prepare(k, carry):
        for block in range(2):
            load_copy(k, block).wait()
        normalize(k, 1 - core)

        @pl.when(k == 0)
        def _():
            pl.semaphore_wait(barrier, 4)

        for block in range(2):
            mate_copy(k, block).start()
        normalize(k, core)

        @pl.when(k == 0)
        def _():
            lend_rows(0)
            send_alone(0)

        @pl.when(k >= 2)
        def _():
            lend_rows(k - 1)
            send(k - 1)

        return carry

    def lend_rows(k):
        for block in range(2):
            mate_copy(k, block).wait_recv()
        offer_to_pair(k)

    lax.fori_loop(0, STEPS, prepare, 0)
    lend_rows(STEPS - 1)
    local_pairs()

    def collect(tick):
        back_copy(tick).wait_recv()
        back_mate(tick).start()

    def tick_fn(tick, carry):
        @pl.when((tick >= OPEN + 2) & (tick < OPEN + 2 + STEPS))
        def _():
            post_copy(tick - OPEN - 2, 1 - upper).wait_recv()
            post_forward(tick - OPEN - 2, core).start()

        opening = tick == OPEN + 1
        middle = tick == OPEN + STEPS

        @pl.when(opening)
        def _():
            for i in range(OPEN):
                forward_alone(i, 1 - core).wait_recv()

        @pl.when(middle | (tick == TICKS - 1))
        def _():
            first = jnp.where(middle, 0, 2)
            for i in range(2):
                forward_shared(first + i + OPEN, 1 - core).wait_recv()
                post_forward(first + i, 1 - core).wait_recv()

        @pl.when(opening | middle | (tick == TICKS - 1))
        def _():
            start = jnp.where(opening, 0, jnp.where(middle, OPEN, OPEN + 2))
            flags = [jnp.where(opening, a, b) for a, b in zip(own_lane, pair_lane)]
            chunk_pairs(start, 2, flags)

        @pl.when((tick == TICKS - 1) | (tick == TICKS))
        def _():
            forward_alone(tick - 1, 1 - core).wait_recv()
            chunk_pairs(tick - 1, 1, own_lane)

        @pl.when(alone(tick))
        def _():
            cross_alone(tick).wait_recv()
            forward_alone(tick, core).start()

        @pl.when(shared(tick))
        def _():
            cross_shared(tick).wait_recv()
            forward_shared(tick, core).start()
            post_copy(tick - OPEN, upper).start()

        @pl.when(tick + LEAD < TICKS)
        def _():
            send(tick + LEAD)

        @pl.when(tick == OPEN + STEPS)
        def _():
            for i in range(OPEN):
                collect(i)

        return carry

    lax.fori_loop(0, TICKS + 1, tick_fn, 0)
    back_corner().start()

    def collect_fn(tick, carry):
        collect(tick)
        return carry

    lax.fori_loop(OPEN, TICKS - 1, collect_fn, 0)

    def shared_fn(k, carry):
        back_mate(k + OPEN).wait_recv()

        @pl.when(sends_edge)
        def _():
            edge_back(k).start()

        return carry

    lax.fori_loop(0, STEPS, shared_fn, 0)

    def close(k, carry):
        tick = jnp.where(k < OPEN, k, k + STEPS)

        @pl.when(k == STEPS - 1)
        def _():
            back_copy(TICKS - 1).wait_recv()

        back_mate(tick).wait_recv()

        @pl.when(takes_edge)
        def _():
            edge_back(k).wait_recv()

        def both(at):
            return ret[at].astype(jnp.float32) + ret_mate[at].astype(jnp.float32)

        alone_sum, shared_sum = both(tick), both(k + OPEN)
        edge_sum = jnp.where(takes_edge, ret_edge[k].astype(jnp.float32), 0.0)
        for block, edge_flag in enumerate((edge_out0, edge_out1)):
            lines = (
                alone_sum * own_lane[1 - block].astype(jnp.float32)
                + shared_sum * pair_lane[1 - block].astype(jnp.float32)
                + edge_sum * edge_flag.astype(jnp.float32)
            )
            line = lines[CHUNK : CHUNK + 1, :] + lines[CHUNK + 8 : CHUNK + 9, :]
            degree = jnp.broadcast_to(line, (CHUNK, CHUNK)).T
            rows = pl.ds(pl.multiple_of(block * BLOCK + k * CHUNK, CHUNK), CHUNK)
            out[rows, :] = (own[rows, :feat] + lines[:CHUNK, :]) / (own[rows, feat:] + degree)
        return carry

    lax.fori_loop(0, STEPS, close, 0)

    def finish(tick, carry):
        @pl.when(alone(tick))
        def _():
            cross_alone(tick).wait_send()
            forward_alone(tick, core).wait_send()

        @pl.when(shared(tick))
        def _():
            cross_shared(tick).wait_send()
            forward_shared(tick, core).wait_send()

        back_copy(tick).wait_send()
        back_mate(tick).wait_send()
        return carry

    lax.fori_loop(0, TICKS, finish, 0)

    def finish_chunk(k, carry):
        for block in range(2):
            mate_copy(k, block).wait_send()
        pre_copy(k).wait_send()
        post_copy(k, upper).wait_send()
        post_forward(k, core).wait_send()

        @pl.when(sends_edge)
        def _():
            edge_back(k).wait_send()

        return carry

    lax.fori_loop(0, STEPS, finish_chunk, 0)


def pair_plan(parity, spectra, scores, reach):
    rows, bins = spectra.shape
    feat = scores.shape[1]
    width = bins + feat
    vmem = pl.BlockSpec(memory_space=pltpu.VMEM)
    bf16 = jnp.bfloat16
    return pl.pallas_call(
        functools.partial(pair_kernel, parity),
        out_shape=jax.ShapeDtypeStruct((rows, feat), jnp.float32),
        in_specs=[pl.BlockSpec(memory_space=pltpu.SMEM)] + [pl.BlockSpec(memory_space=pltpu.HBM)] * 2,
        out_specs=vmem,
        scratch_shapes=[
            pltpu.VMEM((rows, bins), bf16),
            pltpu.VMEM((rows, feat), bf16),
            pltpu.VMEM((rows, width), bf16),
            pltpu.VMEM((STEPS, 2, PIECE, width), bf16),
            pltpu.VMEM((STEPS, QUARTER, width), bf16),
            pltpu.VMEM((STEPS, QUARTER, width), bf16),
            pltpu.VMEM((STEPS, PIECE, width), bf16),
            pltpu.VMEM((STEPS, QUARTER, width), bf16),
            pltpu.VMEM((TICKS * CHUNK, width), bf16),
            pltpu.VMEM((rows, 2 * feat), jnp.float32),
            pltpu.VMEM((2 * CHUNK, 2 * feat), jnp.float32),
            pltpu.VMEM((TICKS, LINES, feat), bf16),
            pltpu.VMEM((TICKS, LINES, feat), bf16),
            pltpu.VMEM((TICKS, LINES, feat), bf16),
            pltpu.VMEM((STEPS, LINES, feat), bf16),
            pltpu.SemaphoreType.DMA((2 * STEPS + 1,)),
            pltpu.SemaphoreType.DMA((56,)),
            pltpu.SemaphoreType.DMA((56,)),
        ],
        compiler_params=pltpu.CompilerParams(
            collective_id=8 + parity,
            has_side_effects=True,
            vmem_limit_bytes=48 * 2**20,
        ),
        cost_estimate=pl.CostEstimate(
            flops=8 * 2 * BLOCK * BLOCK * bins,
            bytes_accessed=2 * rows * width,
            transcendentals=rows * bins,
        ),
        name="pairs",
    )(reach, spectra, scores)


def branch(reach):
    size = reach.shape[0]
    group = 2 * GROUP
    margin = 2
    padded = jnp.pad(reach, (margin, size))
    index = lax.iota(jnp.int32, size)

    def at(shift):
        return padded[margin + shift : margin + shift + size]

    def right(boundary):
        return jnp.where(at(2 * boundary + 1) == 2, 1, 0)

    def left(boundary):
        return jnp.where((at(2 * boundary) == 2) | (at(2 * boundary + 1) == 1), 1, 0)

    def lanes(first):
        going = right(first) + left(first + 1) + right(first + 2)
        coming = left(first) + right(first + 1) + left(first + 2)
        return going, coming

    def over(lane):
        return jnp.maximum(lane - 1, 0)

    def flag(condition, place):
        return jnp.where(condition, 2**place, 0)

    odd = lax.rem(index, 2 * group) == group
    going, coming = lanes(0)
    next_going, next_coming = lanes(GROUP)
    last_going, last_coming = lanes((size - group) // 2)
    edge_right, edge_left = right(3), left(3)
    edge = edge_right + edge_left > 0
    over_going, over_coming = over(going), over(coming)
    shared = jnp.maximum(
        over_going + over(next_going) + edge_left, over_coming + over(next_coming) + edge_right
    )
    more_going = going + left(-1) + edge_left
    more_coming = coming + right(-1) + edge_right
    plain = jnp.maximum(going, coming)
    more = jnp.maximum(more_going, more_coming)
    wrapped = jnp.maximum(over_going + over(last_going), over_coming + over(last_coming))
    full = over_going + over_coming > 0
    misses = (
        flag(full | edge, 0)
        | flag(jnp.where(odd, edge, shared > 1), 1)
        | flag(jnp.where(odd, shared > 1, edge), 2)
        | flag(jnp.where(odd, more, plain) > 2, 3)
        | flag(jnp.where(odd, plain, more) > 2, 4)
        | flag((index == 0) & (wrapped > 1), 2)
    )
    misses = jnp.where(lax.rem(index, group) == 0, misses, 0)
    missed = lax.reduce(misses, jnp.int32(0), lax.bitwise_or, (0,))
    return 31 - lax.clz(~missed & (missed + 1))


def body(spectra, class_scores, reach):
    if reach.shape[0] % 16:
        return plan(True, True, spectra, class_scores, reach)
    branches = [
        functools.partial(slots_plan, 1, False, 0),
        functools.partial(pair_plan, 0),
        functools.partial(pair_plan, 1),
        functools.partial(slots_plan, 2, True, 0),
        functools.partial(slots_plan, 2, True, 1),
        functools.partial(plan, True, True),
    ]
    return lax.switch(branch(reach), branches, spectra, class_scores, reach)


def solution(mesh):
    return jax.shard_map(
        body,
        mesh=mesh,
        in_specs=(P(AXES, None), P(AXES, None), P()),
        out_specs=P(AXES, None),
        check_vma=False,
    )
```

```python
import functools

import jax
import jax.numpy as jnp
from jax import lax
from jax.experimental import pallas as pl
from jax.experimental.pallas import tpu as pltpu
from jax.sharding import PartitionSpec as P

BLOCK = 512
AXES = ("blk", "sub")
GROUP = 4
MESH = pl.DeviceIdType.MESH
HALF = BLOCK // 2
PART = HALF + 16 * (HALF // 128)
SHIP = 2 * PART
NEAR, FAR, EDGE = 2, 3, 4


def kernel(two_blocks, group_edge, reach, spectra, scores, out, units, own, part, ship, ret, offer, kept,
           send_sem, recv_sem):
    bins = spectra.shape[1]
    feat = scores.shape[1]
    subs = lax.axis_size("sub")
    count = lax.axis_size("blk") * subs
    position = lax.axis_index("blk") * subs + lax.axis_index("sub")
    place = lax.rem(position, GROUP)
    odd = lax.rem(place, 2)
    across = position + 1 - 2 * odd
    core = jnp.where(place < 2, position + 2, position - 2)
    beside = position - 1 + 2 * odd
    middle = (place == 1) | (place == 2)
    outer = jnp.logical_not(middle)
    low = place < 2
    high = jnp.logical_not(low)
    has_edge = ((place == 0) & (position > 0)) | ((place == 3) & (position < count - 1))
    first = odd
    second = 1 - odd

    def copy(index, source, target, device):
        return pltpu.make_async_remote_copy(
            src_ref=source,
            dst_ref=target,
            send_sem=send_sem.at[index],
            recv_sem=recv_sem.at[index],
            device_id=(device // subs, lax.rem(device, subs)),
            device_id_type=MESH,
        )

    barrier = pltpu.get_barrier_semaphore()

    def greet(device):
        pl.semaphore_signal(
            barrier,
            inc=1,
            device_id=(device // subs, lax.rem(device, subs)),
            device_id_type=MESH,
        )

    greet(across)
    greet(core)
    beside_used = middle if two_blocks else (place < 0)
    if group_edge:
        beside_used = beside_used | has_edge

    @pl.when(beside_used)
    def _():
        greet(beside)

    def normalize(block):
        def step(i, carry):
            rows = pl.ds(pl.multiple_of(i * 64, 64), 64)
            source = pl.ds(pl.multiple_of(block * BLOCK + i * 64, 64), 64)
            values = spectra[source, :].astype(jnp.float32)
            total = jnp.sum(values, axis=1, keepdims=True)
            unit = jnp.sqrt(values) * (1.0 / jnp.sqrt(total + 1e-06))
            units[block, rows, :bins] = unit.astype(jnp.bfloat16)
            units[block, rows, bins:] = scores[source, :]
            return carry

        lax.fori_loop(0, BLOCK // 64, step, 0)

    def own_reach(index):
        return reach[2 * position + index]

    previous = jnp.maximum(2 * position - 2, 0)

    def flag(condition):
        return jnp.where(condition, 1.0, 0.0).astype(jnp.float32)

    to_next0 = flag(own_reach(0) >= 2)
    to_next1 = flag(own_reach(1) >= 1)
    to_next2 = flag(own_reach(1) >= 2)
    from_prev0 = flag(reach[previous] >= 2)
    from_prev1 = flag(reach[previous + 1] >= 1)
    from_prev2 = flag(reach[previous + 1] >= 2)
    inside = flag(own_reach(0) >= 1)

    def weights(row, column, scale, start=0, size=BLOCK):
        cosine = lax.dot_general(
            units[row, :, :bins],
            units[column, start : start + size, :bins],
            (((1,), (1,)), ((), ())),
            preferred_element_type=jnp.float32,
        )
        return (cosine * cosine * cosine * scale).astype(jnp.bfloat16)

    def forward(column, weight, start=0, size=BLOCK):
        column_scores = units[column, start : start + size, bins:]
        extended = jnp.concatenate([column_scores, jnp.ones_like(column_scores)], axis=1)
        return jnp.dot(weight, extended, preferred_element_type=jnp.float32)

    def local_pairs():
        def step(row, carry):
            own[row] = forward(row, weights(row, row, 1.0))
            own[row] += forward(1 - row, weights(row, 1 - row, inside))
            return carry

        lax.fori_loop(0, 2, step, 0)

    def remote_pairs(column, slot, scale0, scale1, halves=(0, 1)):
        start, size = halves[0] * HALF, HALF * len(halves)
        part[...] = jnp.zeros_like(part)

        def step(row, carry):
            scale = jnp.where(row == 0, scale0, scale1)
            weight = weights(row, column, scale, start, size)
            own[row] += forward(column, weight, start, size)
            part[:size, :] += lax.dot_general(
                weight,
                units[row, :, bins:],
                (((0,), (0,)), ((), ())),
                preferred_element_type=jnp.float32,
            )
            sums = jnp.dot(
                jnp.ones((8, BLOCK), jnp.bfloat16), weight, preferred_element_type=jnp.float32
            )
            for q in range(size // 128):
                part[BLOCK + 8 * q : BLOCK + 8 * q + 8, :] += sums[:, 128 * q : 128 * q + 128]
            return carry

        lax.fori_loop(0, 2, step, 0)
        for place_in, half in enumerate(halves):
            base = half * PART
            ship[slot, base : base + HALF, :] = part[
                place_in * HALF : place_in * HALF + HALF, :
            ].astype(jnp.bfloat16)
            for q in range(HALF // 128):
                row = BLOCK + 8 * (place_in * (HALF // 128) + q)
                line = part[row : row + 8, :]
                high_part = line.astype(jnp.bfloat16).astype(jnp.float32)
                ship[slot, base + HALF + 16 * q : base + HALF + 16 * q + 16, :] = jnp.concatenate(
                    [high_part, line - high_part], axis=0
                ).astype(jnp.bfloat16)

    def add_back(block, slot, scale=1.0, halves=(0, 1)):
        for half in halves:
            base = half * PART
            rows = slice(half * HALF, half * HALF + HALF)
            own[block, rows, :feat] += ret[slot, base : base + HALF, :].astype(jnp.float32) * scale
            for q in range(HALF // 128):
                line = ret[slot, base + HALF + 16 * q : base + HALF + 16 * q + 16, :]
                line = line.astype(jnp.float32)
                line = (line[0:1, :] + line[8:9, :]) * scale
                rows = slice(half * HALF + 128 * q, half * HALF + 128 * q + 128)
                own[block, rows, feat:] += jnp.broadcast_to(line, (128, 128)).T

    if group_edge:
        edge_copy = copy(0, units.at[first], units.at[EDGE], beside)
        edge_back = copy(1, ship.at[2], ret.at[2], beside)

    normalize(first)

    @pl.when(beside_used)
    def _():
        pl.semaphore_wait(barrier, 3)

    @pl.when(jnp.logical_not(beside_used))
    def _():
        pl.semaphore_wait(barrier, 2)

    if two_blocks:
        first_copy = copy(2, units.at[first], units.at[NEAR], across)
        second_copies = [
            copy(
                3 + 5 * h,
                units.at[second, pl.ds(h * HALF, HALF)],
                units.at[FAR, pl.ds(h * HALF, HALF)],
                across,
            )
            for h in range(2)
        ]
        pass_copy = copy(4, units.at[NEAR], units.at[NEAR], core)
        first_back = copy(5, ship.at[0], ret.at[0], across)
        second_backs = [
            copy(
                6 + 3 * h,
                ship.at[1, pl.ds(h * PART, PART)],
                ret.at[1, pl.ds(h * PART, PART)],
                across,
            )
            for h in range(2)
        ]
        beside_back = copy(7, ship.at[0], ret.at[2], beside)

        @pl.when(middle)
        def _():
            first_copy.start()

    if group_edge:

        @pl.when(has_edge)
        def _():
            edge_copy.start()

    normalize(second)

    def edge_pairs():
        @pl.when(has_edge)
        def _():
            edge_copy.wait_recv()
            is_left = place == 3
            remote_pairs(
                EDGE,
                2,
                jnp.where(is_left, to_next0, 0.0),
                jnp.where(is_left, to_next1, from_prev2),
            )
            edge_back.start()

    def edge_end():
        @pl.when(has_edge)
        def _():
            edge_back.wait_recv()
            add_back(first, 2)
            edge_copy.wait_send()
            edge_back.wait_send()

    if two_blocks:
        local_pairs()

        @pl.when(middle)
        def _():
            first_copy.wait_send()
            for half in range(2):
                second_copies[half].start()
            pass_copy.wait_recv()
            is_left = place == 1
            remote_pairs(
                NEAR,
                0,
                jnp.where(is_left, to_next0, 0.0),
                jnp.where(is_left, to_next1, from_prev2),
            )
            beside_back.start()
            beside_back.wait_recv()
            add_back(first, 2)
            first_back.wait_recv()
            add_back(first, 0)
            for half in range(2):
                second_copies[half].wait_send()
                second_backs[half].wait_recv()
                add_back(second, 1, halves=(half,))
            beside_back.wait_send()

        @pl.when(outer)
        def _():
            first_copy.wait_recv()
            pass_copy.start()
            is_left = place == 0
            remote_pairs(
                NEAR,
                0,
                jnp.where(is_left, 0.0, from_prev0),
                jnp.where(is_left, to_next2, 0.0),
            )
            first_back.start()

        if group_edge:
            edge_pairs()

        @pl.when(outer)
        def _():
            is_left = place == 0
            for half in range(2):
                second_copies[half].wait_recv()
                remote_pairs(
                    FAR,
                    1,
                    jnp.where(is_left, to_next0, from_prev1),
                    jnp.where(is_left, to_next1, from_prev2),
                    halves=(half,),
                )
                second_backs[half].start()
            pass_copy.wait_send()
            first_back.wait_send()
            for half in range(2):
                second_backs[half].wait_send()

    else:
        leads = jnp.where(place < 3, jnp.maximum(to_next0, to_next1), 0.0)
        follows = jnp.where(place > 0, jnp.maximum(from_prev0, from_prev1), 0.0)
        has_role = jnp.maximum(leads, follows)
        gather_copies, cross_copies, pass_copies = [], [], []
        for half in range(2):
            rows = pl.ds(half * HALF, HALF)
            near = units.at[NEAR, rows]
            gather_copies.append(copy(2 + 6 * half, offer.at[rows], kept.at[rows], core))
            cross_copies.append(copy(3 + 6 * half, offer.at[rows], near, across))
            pass_copies.append(copy(4 + 6 * half, near, near, core))
        gather_back = copy(5, ship.at[0], ret.at[0], core)
        cross_back = copy(6, ship.at[0], ret.at[1], across)
        pass_back = copy(7, ret.at[1], ret.at[1], core)

        def blend(target, yes, no, scale, rows):
            def step(i, carry):
                chunk = pl.ds(pl.multiple_of(i * rows, rows), rows)
                a = yes[chunk, :].astype(jnp.float32) * scale
                b = no[chunk, :].astype(jnp.float32) * (1.0 - scale)
                target[chunk, :] = (a + b).astype(target.dtype)
                return carry

            lax.fori_loop(0, target.shape[0] // rows, step, 0)

        for half in range(2):
            rows = pl.ds(half * HALF, HALF)
            blend(offer.at[rows], units.at[1, rows], units.at[0, rows], leads, 64)

            @pl.when(high)
            def _():
                gather_copies[half].start()

        @pl.when(low)
        def _():
            for half in range(2):
                rows = pl.ds(half * HALF, HALF)
                gather_copies[half].wait_recv()
                blend(offer.at[rows], offer.at[rows], kept.at[rows], has_role, 64)
                cross_copies[half].start()

        local_pairs()

        @pl.when(low)
        def _():
            for half in range(2):
                cross_copies[half].wait_recv()
                pass_copies[half].start()

        @pl.when(high)
        def _():
            for half in range(2):
                pass_copies[half].wait_recv()

        remote_pairs(
            NEAR,
            0,
            jnp.where(place < 3, to_next0, 0.0) * leads,
            jnp.where(place < 3, to_next1, 0.0) * leads + from_prev2 * follows,
        )

        @pl.when(high)
        def _():
            gather_back.start()

        @pl.when(low)
        def _():
            gather_back.wait_recv()
            blend(ship.at[0], ship.at[0], ret.at[0], has_role, SHIP)
            cross_back.start()

        if group_edge:
            edge_pairs()

        @pl.when(low)
        def _():
            cross_back.wait_recv()
            pass_back.start()

        @pl.when(high)
        def _():
            pass_back.wait_recv()

        add_back(1, 1, leads)
        add_back(0, 1, follows)

        @pl.when(low)
        def _():
            for half in range(2):
                cross_copies[half].wait_send()
                pass_copies[half].wait_send()
            cross_back.wait_send()
            pass_back.wait_send()

        @pl.when(high)
        def _():
            for half in range(2):
                gather_copies[half].wait_send()
            gather_back.wait_send()

    if group_edge:
        edge_end()

    for block in range(2):
        out[block * BLOCK : (block + 1) * BLOCK, :] = own[block, :, :feat] / own[block, :, feat:]


def plan(two_blocks, group_edge, spectra, scores, reach):
    rows, bins = spectra.shape
    feat = scores.shape[1]
    width = bins + feat
    vmem = pl.BlockSpec(memory_space=pltpu.VMEM)
    return pl.pallas_call(
        functools.partial(kernel, two_blocks, group_edge),
        out_shape=jax.ShapeDtypeStruct((rows, feat), jnp.float32),
        in_specs=[pl.BlockSpec(memory_space=pltpu.SMEM), vmem, vmem],
        out_specs=vmem,
        scratch_shapes=[
            pltpu.VMEM((5, BLOCK, width), jnp.bfloat16),
            pltpu.VMEM((2, BLOCK, 2 * feat), jnp.float32),
            pltpu.VMEM((BLOCK + 8 * (BLOCK // 128), feat), jnp.float32),
            pltpu.VMEM((3, SHIP, feat), jnp.bfloat16),
            pltpu.VMEM((3, SHIP, feat), jnp.bfloat16),
            pltpu.VMEM((16 if two_blocks else BLOCK, width), jnp.bfloat16),
            pltpu.VMEM((16 if two_blocks else BLOCK, width), jnp.bfloat16),
            pltpu.SemaphoreType.DMA((12,)),
            pltpu.SemaphoreType.DMA((12,)),
        ],
        compiler_params=pltpu.CompilerParams(
            collective_id=2 * int(two_blocks) + int(group_edge),
            has_side_effects=True,
            vmem_limit_bytes=48 * 2**20,
        ),
        cost_estimate=pl.CostEstimate(
            flops=8 * 2 * BLOCK * BLOCK * bins,
            bytes_accessed=2 * rows * width,
            transcendentals=rows * bins,
        ),
        name="network",
    )(reach, spectra, scores)


CHUNK = 128
PIECE = CHUNK // 2
STEPS = BLOCK // CHUNK
LINES = CHUNK + 16
AHEAD = 4
DELAY = 5
EX, XS, FW, PRE, POST, RX, RF, RE = 0, 8, 16, 24, 32, 40, 48, 56


def slots_kernel(slots, edges, turn, reach, spectra, marks, out, raw, scores, units, mate, pre, offer, got, past, own, part, ship,
                 ship_edge, ret, ret_mate, ret_edge, load_sem, send_sem, recv_sem):
    bins = spectra.shape[1]
    feat = marks.shape[1]
    total_steps = slots * STEPS
    subs = lax.axis_size("sub")
    count = lax.axis_size("blk") * subs
    position = lax.axis_index("blk") * subs + lax.axis_index("sub")
    place = lax.rem(position, GROUP)
    group = position // GROUP
    side = lax.rem(place, 2)
    core = place // 2
    base = position - place
    odd_group = lax.rem(group + turn, 2) == 1
    even_group = lax.rem(group + turn, 2) == 0
    across = position + 1 - 2 * side
    partner = position + 2 - 4 * core
    corner = across + 2 - 4 * core
    at_end = (place == 0) | (place == 3)
    has_edge = ((place == 0) & (position > 0)) | ((place == 3) & (position < count - 1))
    beside = jnp.where(place == 0, position - 1, position + 1)
    is_edge = has_edge & even_group
    host = jnp.where(side == 0, base - GROUP, base + GROUP) + side
    is_host = odd_group & jnp.where(side == 1, base >= GROUP, base + GROUP < count)
    guest = jnp.where(side == 0, base + GROUP, base - GROUP + 3)

    def place_of(device):
        return (device // subs, lax.rem(device, subs))

    def copy(index, source, target, device):
        return pltpu.make_async_remote_copy(
            src_ref=source,
            dst_ref=target,
            send_sem=send_sem.at[index],
            recv_sem=recv_sem.at[index],
            device_id=place_of(device),
            device_id_type=MESH,
        )

    def load_copy(k, block):
        rows = pl.ds(pl.multiple_of(block * BLOCK + k * CHUNK, CHUNK), CHUNK)
        return pltpu.make_async_copy(spectra.at[rows], raw.at[rows], load_sem.at[2 * k + block])

    mark_copy = pltpu.make_async_copy(marks, scores, load_sem.at[2 * STEPS])
    for block in range(2):
        load_copy(0, block).start()
    mark_copy.start()
    for k in range(1, STEPS):
        for block in range(2):
            load_copy(k, block).start()

    barrier = pltpu.get_barrier_semaphore()

    def greet(device):
        pl.semaphore_signal(barrier, inc=1, device_id=place_of(device), device_id_type=MESH)

    greet(across)
    greet(partner)
    greet(corner)
    if edges:

        @pl.when(has_edge)
        def _():
            greet(beside)

        @pl.when(is_edge)
        def _():
            greet(host)
            greet(host + 2)

        @pl.when(is_host)
        def _():
            greet(guest)

    def active(boundary):
        inside = (boundary >= 0) & (boundary < count - 1)
        at = jnp.clip(boundary, 0, count - 2)
        a, b = reach[2 * at], reach[2 * at + 1]
        right = jnp.where(inside & (b == 2), 1, 0)
        left = jnp.where(inside & ((a == 2) | (b == 1)), 1, 0)
        return right, left

    bounds = [active(base + i - 1) for i in range(5)]
    rights = [b[0] for b in bounds]
    lefts = [b[1] for b in bounds]
    hosts = jnp.where(odd_group, 1, 0) if edges else 0

    def assign(inner, late, early):
        d1, d2, d3 = inner
        if slots == 1:
            return ((d1, d2, d3, late * hosts, early * hosts),)
        late, early = late * hosts, early * hosts
        free = 1 - late
        f1 = d1 * free
        f2 = d2 * (1 - d1) * free
        f3 = d3 * (1 - d1) * (1 - d2) * free
        return ((f1, f2, f3, late, 0), (d1 - f1, d2 - f2, d3 - f3, 0, early))

    going = assign((rights[1], lefts[2], rights[3]), lefts[0], lefts[4])
    coming = assign((lefts[1], rights[2], lefts[3]), rights[4], rights[0])

    def pick(options, index):
        value = options[-1]
        for i in range(len(options) - 2, -1, -1):
            value = jnp.where(index == i, options[i], value)
        return value

    def slot_flags(slot):
        q, r = going[slot], coming[slot]
        right_out = pick([q[0], r[1], q[2], r[3]], place)
        left_out = pick([q[3], r[0], q[1], r[2]], place)
        mate_right = pick([q[2], r[3], q[0], r[1]], place)
        mate_left = pick([q[1], r[2], q[3], r[0]], place)
        guest_in = jnp.where(side == 0, q[4], r[4])
        right_in = pick([r[4], q[0], r[1], q[2]], place)
        left_in = pick([r[0], q[1], r[2], q[4]], place)
        return right_out, left_out, mate_right, mate_left, guest_in, right_in, left_in

    flags = [slot_flags(s) for s in range(slots)]

    def flag_at(step, which):
        if slots == 1:
            return flags[0][which]
        return jnp.where(step < STEPS, flags[0][which], flags[1][which])

    own0, own1 = reach[2 * position], reach[2 * position + 1]
    close0 = jnp.where(own0 == 2, 1, 0)
    close1 = jnp.where(own1 == 1, 1, 0)
    inside = jnp.where(own0 >= 1, 1.0, 0.0).astype(jnp.float32)

    edge_right_in = jnp.where(place == 0, rights[0], 0)
    edge_left_in = jnp.where(place == 3, lefts[4], 0)
    edge_out0 = jnp.where(place == 0, lefts[0], 0).astype(jnp.float32)
    edge_out1 = jnp.where(place == 3, rights[4], 0).astype(jnp.float32)

    def chunk_of(step):
        return lax.rem(step, STEPS)

    def normalize(k, which):
        def one(block, carry):
            row = k * CHUNK + which * PIECE
            source = pl.ds(pl.multiple_of(block * BLOCK + row, 64), 64)
            values = raw[source, :].astype(jnp.float32)
            total = jnp.sum(values, axis=1, keepdims=True)
            unit = jnp.sqrt(values) * (1.0 / jnp.sqrt(total + 1e-06))
            units[source, :bins] = unit.astype(jnp.bfloat16)
            units[source, bins:] = scores[source, :]
            return carry

        lax.fori_loop(0, 2, one, 0)

    def piece(block, k, which):
        start = block * BLOCK + k * CHUNK + which * PIECE
        return units.at[pl.ds(pl.multiple_of(start, PIECE), PIECE)]

    def mate_copy(k, block):
        return copy(EX + 2 * k + block, piece(block, k, 1 - core), mate.at[k, block], partner)

    def pre_copy(k, which):
        block = jnp.where(place == 0, 0, 1)
        return copy(PRE + 2 * k + which, piece(block, k, which), pre.at[k], host + 2 * which)

    def pre_recv(k):
        return copy(PRE + 2 * k + core, pre.at[k], pre.at[k], across)

    def cross_copy(step):
        rows = pl.ds(pl.multiple_of(core * PIECE, PIECE), PIECE)
        return copy(XS + step, offer.at[step], got.at[step, rows], across)

    def forward_copy(step):
        rows = pl.ds(pl.multiple_of(core * PIECE, PIECE), PIECE)
        return copy(FW + step, got.at[step, rows], got.at[step, rows], partner)

    def post_copy(step):
        rows = pl.ds(pl.multiple_of(core * PIECE, PIECE), PIECE)
        return copy(POST + 2 * step + core, got.at[step, rows], past.at[step, rows], guest)

    def post_recv(k, which):
        rows = pl.ds(which * PIECE, PIECE)
        return copy(POST + 2 * k + which, past.at[k, rows], past.at[k, rows], across)

    def back_copy(step):
        return copy(RX + step, ship.at[step], ret.at[step], across)

    def back_mate(step):
        return copy(RF + step, ret.at[step], ret_mate.at[step], partner)

    final = total_steps - 1

    def back_corner():
        return copy(RF + final, ship.at[final], ret_mate.at[final], corner)

    def edge_back(k, source):
        return copy(RE + k, source, ret_edge.at[k], beside)

    early_slot = slots - 1

    def send(step):
        k = chunk_of(step)

        @pl.when(step < STEPS)
        def _():
            for block in range(2):
                mate_copy(k, block).wait_recv()

        right_out = flag_at(step, 0)
        mate_right = flag_at(step, 2)
        mate_left = flag_at(step, 3)
        guest_in = flag_at(step, 4)

        def one(i, carry):
            at = pl.ds(pl.multiple_of(i * 16, 16), 16)
            first = k * CHUNK + core * PIECE + i * 16
            mine0 = pl.ds(pl.multiple_of(first, 16), 16)
            mine1 = pl.ds(pl.multiple_of(BLOCK + first, 16), 16)
            value = jnp.where(right_out == 1, units[mine1, :], units[mine0, :])
            value = jnp.where(mate_right == 1, mate[k, 1, at, :], value)
            value = jnp.where(mate_left == 1, mate[k, 0, at, :], value)
            offer[step, at, :] = value
            return carry

        lax.fori_loop(0, PIECE // 16, one, 0)
        if edges:

            @pl.when(is_host & (step >= early_slot * STEPS))
            def _():
                pre_recv(k).wait_recv()

                def swap(i, carry):
                    at = pl.ds(pl.multiple_of(i * 16, 16), 16)
                    offer[step, at, :] = jnp.where(guest_in == 1, pre[k, at, :], offer[step, at, :])
                    return carry

                lax.fori_loop(0, PIECE // 16, swap, 0)

        cross_copy(step).start()

    def local_pairs():
        def one(row, carry):
            rows = pl.ds(pl.multiple_of(row * BLOCK, BLOCK), BLOCK)
            cosine = lax.dot_general(
                units[rows, :bins],
                units[:, :bins],
                (((1,), (1,)), ((), ())),
                preferred_element_type=jnp.float32,
            )
            column = lax.broadcasted_iota(jnp.int32, (1, 2 * BLOCK), 1) // BLOCK
            scale = jnp.where(column == row, 1.0, inside)
            weight = (cosine * cosine * cosine * scale).astype(jnp.bfloat16)
            extended = jnp.concatenate([units[:, bins:], jnp.ones((2 * BLOCK, feat), jnp.bfloat16)], axis=1)
            own[rows, :] = jnp.dot(weight, extended, preferred_element_type=jnp.float32)
            return carry

        lax.fori_loop(0, 2, one, 0)

    def chunk_pairs(read, scale0, scale1, target):
        cosine = lax.dot_general(
            read(slice(0, bins)),
            units[:, :bins],
            (((1,), (1,)), ((), ())),
            preferred_element_type=jnp.float32,
        )
        column = lax.broadcasted_iota(jnp.int32, (1, 2 * BLOCK), 1)
        scale = jnp.where(column < BLOCK, scale0.astype(jnp.float32), scale1.astype(jnp.float32))
        weight = (cosine * cosine * cosine * scale).astype(jnp.bfloat16)
        extended = jnp.concatenate([units[:, bins:], jnp.ones((2 * BLOCK, feat), jnp.bfloat16)], axis=1)
        part[...] = jnp.dot(weight, extended, preferred_element_type=jnp.float32)
        column_scores = read(slice(bins, bins + feat))
        extended = jnp.concatenate([column_scores, jnp.ones_like(column_scores)], axis=1)
        own[...] += lax.dot_general(
            weight, extended, (((0,), (0,)), ((), ())), preferred_element_type=jnp.float32
        )
        target[:CHUNK, :] = part[:, :feat].astype(jnp.bfloat16)
        line = part[:, feat:].T[:8, :]
        high_part = line.astype(jnp.bfloat16).astype(jnp.float32)
        target[CHUNK:, :] = jnp.concatenate([high_part, line - high_part], axis=0).astype(jnp.bfloat16)

    def add_back(k, lines, scale0, scale1):
        sums = lines[:CHUNK, :].astype(jnp.float32)
        line = lines[CHUNK:, :].astype(jnp.float32)
        line = line[0:1, :] + line[8:9, :]
        degree = jnp.broadcast_to(line, (CHUNK, CHUNK)).T
        for block, scale in enumerate((scale0, scale1)):
            rows = pl.ds(pl.multiple_of(block * BLOCK + k * CHUNK, CHUNK), CHUNK)
            own[rows, :feat] += sums * scale
            own[rows, feat:] += degree * scale

    greetings = 3
    if edges:
        greetings = (
            3 + jnp.where(has_edge, 1, 0) + jnp.where(is_edge, 2, 0) + jnp.where(is_host, 1, 0)
        )

    mark_copy.wait()

    def prepare(k, carry):
        for block in range(2):
            load_copy(k, block).wait()
        normalize(k, 1 - core)

        @pl.when(k == 0)
        def _():
            pl.semaphore_wait(barrier, greetings)

        for block in range(2):
            mate_copy(k, block).start()
        normalize(k, core)
        if edges:

            @pl.when(is_edge)
            def _():
                for which in range(2):
                    pre_copy(k, which).start()

        @pl.when(k < AHEAD)
        def _():
            send(k)

        return carry

    lax.fori_loop(0, STEPS, prepare, 0)
    local_pairs()

    def edge_step(k):
        for which in range(2):
            post_recv(k, which).wait_recv()
        first = edge_right_in + edge_left_in * close0
        second = edge_right_in + edge_left_in * close1
        chunk_pairs(lambda columns: past[k, :, columns], first, second, ship_edge.at[k])
        edge_back(k, ship_edge.at[k]).start()

    def step_fn(step, carry):
        @pl.when(step < total_steps)
        def _():
            cross_copy(step).wait_recv()
            forward_copy(step).start()
            if edges:

                @pl.when(is_host & (step < STEPS))
                def _():
                    post_copy(step).start()

            @pl.when(step + AHEAD < total_steps)
            def _():
                send(step + AHEAD)

            forward_wait(step)
            right_in = flag_at(step, 5)
            left_in = flag_at(step, 6)
            first = right_in + left_in * close0
            second = right_in + left_in * close1
            chunk_pairs(lambda columns: got[step, :, columns], first, second, ship.at[step])
            back_copy(step).start()

            @pl.when(step == final)
            def _():
                back_corner().start()

            if edges:

                @pl.when(has_edge & odd_group & (step >= early_slot * STEPS))
                def _():
                    edge_back(chunk_of(step), ship.at[step]).start()

        if edges:

            @pl.when(is_edge & (step >= STEPS - 1) & (step < 2 * STEPS - 1))
            def _():
                edge_step(step - (STEPS - 1))

        @pl.when((step >= DELAY) & (step < total_steps + DELAY))
        def _():
            back_copy(step - DELAY).wait_recv()

            @pl.when(step - DELAY < final)
            def _():
                back_mate(step - DELAY).start()

        @pl.when(step > DELAY)
        def _():
            done = step - DELAY - 1
            back_mate(done).wait_recv()
            scale0 = flag_at(done, 1).astype(jnp.float32)
            scale1 = flag_at(done, 0).astype(jnp.float32)
            both = ret[done].astype(jnp.float32) + ret_mate[done].astype(jnp.float32)
            add_back(chunk_of(done), both, scale0, scale1)

        return carry

    def forward_wait(step):
        rows = pl.ds(pl.multiple_of((1 - core) * PIECE, PIECE), PIECE)
        copy(FW + step, got.at[step, rows], got.at[step, rows], partner).wait_recv()

    lax.fori_loop(0, total_steps + DELAY + 1, step_fn, 0)

    if edges:

        @pl.when(has_edge)
        def _():
            def one(k, carry):
                edge_back(k, ship_edge.at[k]).wait_recv()
                add_back(k, ret_edge[k], edge_out0, edge_out1)
                return carry

            lax.fori_loop(0, STEPS, one, 0)

    out[...] = own[:, :feat] / own[:, feat:]

    def finish(step, carry):
        cross_copy(step).wait_send()
        forward_copy(step).wait_send()
        back_copy(step).wait_send()
        back_mate(step).wait_send()
        return carry

    lax.fori_loop(0, total_steps, finish, 0)

    def finish_chunk(k, carry):
        for block in range(2):
            mate_copy(k, block).wait_send()
        if edges:

            @pl.when(has_edge)
            def _():
                edge_back(k, ship_edge.at[k]).wait_send()

            @pl.when(is_edge)
            def _():
                for which in range(2):
                    pre_copy(k, which).wait_send()

            @pl.when(is_host)
            def _():
                post_copy(k).wait_send()

        return carry

    lax.fori_loop(0, STEPS, finish_chunk, 0)


def slots_plan(slots, edges, turn, spectra, scores, reach):
    rows, bins = spectra.shape
    feat = scores.shape[1]
    width = bins + feat
    steps = slots * STEPS
    extra = STEPS if edges else 1
    vmem = pl.BlockSpec(memory_space=pltpu.VMEM)
    bf16 = jnp.bfloat16
    return pl.pallas_call(
        functools.partial(slots_kernel, slots, edges, turn),
        out_shape=jax.ShapeDtypeStruct((rows, feat), jnp.float32),
        in_specs=[pl.BlockSpec(memory_space=pltpu.SMEM)] + [pl.BlockSpec(memory_space=pltpu.HBM)] * 2,
        out_specs=vmem,
        scratch_shapes=[
            pltpu.VMEM((rows, bins), bf16),
            pltpu.VMEM((rows, feat), bf16),
            pltpu.VMEM((rows, width), bf16),
            pltpu.VMEM((STEPS, 2, PIECE, width), bf16),
            pltpu.VMEM((extra, PIECE, width), bf16),
            pltpu.VMEM((steps, PIECE, width), bf16),
            pltpu.VMEM((steps, CHUNK, width), bf16),
            pltpu.VMEM((extra, CHUNK, width), bf16),
            pltpu.VMEM((rows, 2 * feat), jnp.float32),
            pltpu.VMEM((CHUNK, 2 * feat), jnp.float32),
            pltpu.VMEM((steps, LINES, feat), bf16),
            pltpu.VMEM((extra, LINES, feat), bf16),
            pltpu.VMEM((steps, LINES, feat), bf16),
            pltpu.VMEM((steps, LINES, feat), bf16),
            pltpu.VMEM((extra, LINES, feat), bf16),
            pltpu.SemaphoreType.DMA((2 * STEPS + 1,)),
            pltpu.SemaphoreType.DMA((60,)),
            pltpu.SemaphoreType.DMA((60,)),
        ],
        compiler_params=pltpu.CompilerParams(
            collective_id=4 + 2 * (slots - 1) + int(edges) + 3 * turn,
            has_side_effects=True,
            vmem_limit_bytes=48 * 2**20,
        ),
        cost_estimate=pl.CostEstimate(
            flops=8 * 2 * BLOCK * BLOCK * bins,
            bytes_accessed=2 * rows * width,
            transcendentals=rows * bins,
        ),
        name="slots",
    )(reach, spectra, scores)


TICKS = 2 * STEPS
QUARTER = CHUNK // 4
LEAD = 3
OPEN = 2
P_EX, P_XS, P_FW, P_RX, P_RF, P_PRE, P_POST, P_PF, P_RE = 0, 8, 16, 24, 32, 40, 44, 48, 52


def pair_kernel(parity, reach, spectra, marks, out, raw, scores, units, mate, lend, borrow, offer, offer_pair, got, own, part,
                ship, ret, ret_mate, ret_edge, load_sem, send_sem, recv_sem):
    bins = spectra.shape[1]
    feat = marks.shape[1]
    subs = lax.axis_size("sub")
    count = lax.axis_size("blk") * subs
    position = lax.axis_index("blk") * subs + lax.axis_index("sub")
    place = lax.rem(position, GROUP)
    group = position // GROUP
    side = lax.rem(place, 2)
    core = place // 2
    base = position - place
    upper = lax.rem(group + parity, 2)
    across = position + 1 - 2 * side
    partner = position + 2 - 4 * core
    corner = across + 2 - 4 * core
    shift = jnp.where(upper == 1, count - GROUP, GROUP)
    pair = lax.rem(position + shift, count)
    pair_base = pair - place
    low_base = jnp.where(upper == 1, pair_base, base)

    def place_of(device):
        return (device // subs, lax.rem(device, subs))

    def copy(index, source, target, device):
        return pltpu.make_async_remote_copy(
            src_ref=source,
            dst_ref=target,
            send_sem=send_sem.at[index],
            recv_sem=recv_sem.at[index],
            device_id=place_of(device),
            device_id_type=MESH,
        )

    def load_copy(k, block):
        rows = pl.ds(pl.multiple_of(block * BLOCK + k * CHUNK, CHUNK), CHUNK)
        return pltpu.make_async_copy(spectra.at[rows], raw.at[rows], load_sem.at[2 * k + block])

    mark_copy = pltpu.make_async_copy(marks, scores, load_sem.at[2 * STEPS])
    for block in range(2):
        load_copy(0, block).start()
    mark_copy.start()
    for k in range(1, STEPS):
        for block in range(2):
            load_copy(k, block).start()

    barrier = pltpu.get_barrier_semaphore()
    for device in (across, partner, corner, pair):
        pl.semaphore_signal(barrier, inc=1, device_id=place_of(device), device_id_type=MESH)

    def active(boundary):
        within = boundary < count - 1
        at = jnp.minimum(boundary, count - 2)
        a, b = reach[2 * at], reach[2 * at + 1]
        right = jnp.where(within & (b == 2), 1, 0)
        left = jnp.where(within & ((a == 2) | (b == 1)), 1, 0)
        return right, left

    def lanes(first):
        (r0, l0), (r1, l1), (r2, l2) = [active(first + i) for i in range(3)]
        result = []
        for d1, d2, d3 in ((r0, l1, r2), (l0, r1, l2)):
            f1, f2, f3 = d1, d2 * (1 - d1), d3 * (1 - d1) * (1 - d2)
            result.append(((f1, f2, f3), (d1 - f1, d2 - f2, d3 - f3)))
        return result

    going, coming = lanes(base)
    pair_going, pair_coming = lanes(pair_base)
    edge_right, edge_left = active(low_base + 3)
    up = upper
    down = 1 - upper

    def pick(options):
        value = options[-1]
        for i in range(len(options) - 2, -1, -1):
            value = jnp.where(place == i, options[i], value)
        return value

    def lane_flags(which):
        q, r = going[which], coming[which]
        last = 1 if which else 0
        right_out = pick([q[0], r[1], q[2], 0])
        left_out = pick([0, r[0], q[1], r[2]])
        mate_right = pick([q[2], last * edge_right * down, q[0], r[1]])
        mate_left = pick([q[1], r[2], last * edge_left * up, r[0]])
        right_in = pick([last * edge_right * up, q[0], r[1], q[2]])
        left_in = pick([r[0], q[1], r[2], last * edge_left * down])
        return right_out, left_out, mate_right, mate_left, right_in, left_in

    own_lane, pair_lane = lane_flags(0), lane_flags(1)
    edge_out0 = jnp.where(place == 0, edge_left * up, 0)
    edge_out1 = jnp.where(place == 3, edge_right * down, 0)
    pair_sum = jnp.where(
        side == 0,
        sum(pair_going[1]) + edge_left * down,
        sum(pair_coming[1]) + edge_right * up,
    )

    own0, own1 = reach[2 * position], reach[2 * position + 1]
    close0 = jnp.where(own0 == 2, 1, 0)
    close1 = jnp.where(own1 == 1, 1, 0)
    inside = jnp.where(own0 >= 1, 1.0, 0.0).astype(jnp.float32)

    sends_edge = ((upper == 0) & (place == 0)) | ((upper == 1) & (place == 3))
    takes_edge = ((upper == 1) & (place == 0)) | ((upper == 0) & (place == 3))

    def shared(tick):
        return (tick >= OPEN) & (tick < OPEN + STEPS)

    def alone(tick):
        return ((tick >= 0) & (tick < OPEN)) | ((tick >= OPEN + STEPS) & (tick < TICKS))

    def chunk_of(tick):
        return jnp.where(tick < OPEN, tick, tick - STEPS)

    def normalize(k, which):
        def one(block, carry):
            row = k * CHUNK + which * PIECE
            source = pl.ds(pl.multiple_of(block * BLOCK + row, 64), 64)
            values = raw[source, :].astype(jnp.float32)
            total = jnp.sum(values, axis=1, keepdims=True)
            unit = jnp.sqrt(values) * (1.0 / jnp.sqrt(total + 1e-06))
            units[source, :bins] = unit.astype(jnp.bfloat16)
            units[source, bins:] = scores[source, :]
            return carry

        lax.fori_loop(0, 2, one, 0)

    def half_rows(tick, which):
        return got.at[pl.ds(pl.multiple_of(tick * CHUNK + which * PIECE, PIECE), PIECE)]

    def quarter_rows(tick, which, level):
        start = tick * CHUNK + which * PIECE + level * QUARTER
        return got.at[pl.ds(pl.multiple_of(start, QUARTER), QUARTER)]

    def mate_copy(k, block):
        rows = pl.ds(pl.multiple_of(block * BLOCK + k * CHUNK + (1 - core) * PIECE, PIECE), PIECE)
        return copy(P_EX + 2 * k + block, units.at[rows], mate.at[k, block], partner)

    def pre_copy(k):
        return copy(P_PRE + k, lend.at[k], borrow.at[k], pair)

    def cross_alone(tick):
        return copy(P_XS + tick, offer.at[chunk_of(tick)], half_rows(tick, core), across)

    def cross_shared(tick):
        return copy(P_XS + tick, offer_pair.at[tick - OPEN], quarter_rows(tick, core, upper), across)

    def forward_alone(tick, which):
        rows = half_rows(tick, which)
        return copy(P_FW + tick, rows, rows, partner)

    def forward_shared(tick, which):
        rows = quarter_rows(tick, which, upper)
        return copy(P_FW + tick, rows, rows, partner)

    def post_copy(k, level):
        rows = quarter_rows(k + OPEN, core, level)
        return copy(P_POST + k, rows, rows, pair)

    def post_forward(k, which):
        rows = quarter_rows(k + OPEN, which, 1 - upper)
        return copy(P_PF + k, rows, rows, partner)

    def back_copy(tick):
        return copy(P_RX + tick, ship.at[tick], ret.at[tick], across)

    def back_mate(tick):
        return copy(P_RF + tick, ret.at[tick], ret_mate.at[tick], partner)

    def back_corner():
        return copy(P_RF + TICKS - 1, ship.at[TICKS - 1], ret_mate.at[TICKS - 1], corner)

    def edge_back(k):
        return copy(P_RE + k, ret_mate.at[k + OPEN], ret_edge.at[k], pair)

    def choose_rows(flags, k, start, i):
        right_out, left_out, mate_right, mate_left = flags
        at = pl.ds(pl.multiple_of(start + i * 16, 16), 16)
        first = k * CHUNK + core * PIECE + start + i * 16
        mine0 = pl.ds(pl.multiple_of(first, 16), 16)
        mine1 = pl.ds(pl.multiple_of(BLOCK + first, 16), 16)
        value = jnp.where(right_out == 1, units[mine1, :], units[mine0, :])
        value = jnp.where(mate_right == 1, mate[k, 1, at, :], value)
        return jnp.where(mate_left == 1, mate[k, 0, at, :], value)

    pair_right_out = pair_lane[0] + edge_out1
    pair_flags = (pair_right_out,) + pair_lane[1:4]

    def offer_to_pair(k):
        def one(i, carry):
            rows = pl.ds(pl.multiple_of(i * 16, 16), 16)
            lend[k, rows, :] = choose_rows(pair_flags, k, (1 - upper) * QUARTER, i)
            return carry

        lax.fori_loop(0, QUARTER // 16, one, 0)
        pre_copy(k).start()

    def send_alone(tick):
        k = chunk_of(tick)

        def one(i, carry):
            rows = pl.ds(pl.multiple_of(i * 16, 16), 16)
            offer[k, rows, :] = choose_rows(own_lane[:4], k, 0, i)
            return carry

        lax.fori_loop(0, PIECE // 16, one, 0)
        cross_alone(tick).start()

    def send_shared(tick):
        k = tick - OPEN
        pre_copy(k).wait_recv()

        def one(i, carry):
            rows = pl.ds(pl.multiple_of(i * 16, 16), 16)
            value = choose_rows(pair_flags, k, upper * QUARTER, i)
            offer_pair[k, rows, :] = jnp.where(pair_sum > 0, borrow[k, rows, :], value)
            return carry

        lax.fori_loop(0, QUARTER // 16, one, 0)
        cross_shared(tick).start()

    def send(tick):
        @pl.when(alone(tick))
        def _():
            send_alone(tick)

        @pl.when(shared(tick))
        def _():
            send_shared(tick)

    def local_pairs():
        def one(row, carry):
            rows = pl.ds(pl.multiple_of(row * BLOCK, BLOCK), BLOCK)
            cosine = lax.dot_general(
                units[rows, :bins],
                units[:, :bins],
                (((1,), (1,)), ((), ())),
                preferred_element_type=jnp.float32,
            )
            column = lax.broadcasted_iota(jnp.int32, (1, 2 * BLOCK), 1) // BLOCK
            scale = jnp.where(column == row, 1.0, inside)
            weight = (cosine * cosine * cosine * scale).astype(jnp.bfloat16)
            extended = jnp.concatenate([units[:, bins:], jnp.ones((2 * BLOCK, feat), jnp.bfloat16)], axis=1)
            own[rows, :] = jnp.dot(weight, extended, preferred_element_type=jnp.float32)
            return carry

        lax.fori_loop(0, 2, one, 0)

    def chunk_pairs(tick, chunks, flags):
        first = (flags[4] + flags[5] * close0).astype(jnp.float32)
        second = (flags[4] + flags[5] * close1).astype(jnp.float32)
        size = chunks * CHUNK
        rows = pl.ds(pl.multiple_of(tick * CHUNK, CHUNK), size)
        cosine = lax.dot_general(
            got[rows, :bins],
            units[:, :bins],
            (((1,), (1,)), ((), ())),
            preferred_element_type=jnp.float32,
        )
        column = lax.broadcasted_iota(jnp.int32, (1, 2 * BLOCK), 1)
        scale = jnp.where(column < BLOCK, first, second)
        weight = (cosine * cosine * cosine * scale).astype(jnp.bfloat16)
        extended = jnp.concatenate([units[:, bins:], jnp.ones((2 * BLOCK, feat), jnp.bfloat16)], axis=1)
        part[:size, :] = jnp.dot(weight, extended, preferred_element_type=jnp.float32)
        extended = jnp.concatenate([got[rows, bins:], jnp.ones((size, feat), jnp.bfloat16)], axis=1)
        own[...] += lax.dot_general(
            weight, extended, (((0,), (0,)), ((), ())), preferred_element_type=jnp.float32
        )
        for i in range(chunks):
            lines = slice(i * CHUNK, i * CHUNK + CHUNK)
            ship[tick + i, :CHUNK, :] = part[lines, :feat].astype(jnp.bfloat16)
            line = part[lines, feat:].T[:8, :]
            high_part = line.astype(jnp.bfloat16).astype(jnp.float32)
            ship[tick + i, CHUNK:, :] = jnp.concatenate([high_part, line - high_part], axis=0).astype(
                jnp.bfloat16
            )
            back_copy(tick + i).start()

    mark_copy.wait()

    def prepare(k, carry):
        for block in range(2):
            load_copy(k, block).wait()
        normalize(k, 1 - core)

        @pl.when(k == 0)
        def _():
            pl.semaphore_wait(barrier, 4)

        for block in range(2):
            mate_copy(k, block).start()
        normalize(k, core)

        @pl.when(k == 0)
        def _():
            lend_rows(0)
            send_alone(0)

        @pl.when(k >= 2)
        def _():
            lend_rows(k - 1)
            send(k - 1)

        return carry

    def lend_rows(k):
        for block in range(2):
            mate_copy(k, block).wait_recv()
        offer_to_pair(k)

    lax.fori_loop(0, STEPS, prepare, 0)
    lend_rows(STEPS - 1)
    local_pairs()

    def collect(tick):
        back_copy(tick).wait_recv()
        back_mate(tick).start()

    def tick_fn(tick, carry):
        @pl.when((tick >= OPEN + 2) & (tick < OPEN + 2 + STEPS))
        def _():
            post_copy(tick - OPEN - 2, 1 - upper).wait_recv()
            post_forward(tick - OPEN - 2, core).start()

        opening = tick == OPEN + 1
        middle = tick == OPEN + STEPS

        @pl.when(opening)
        def _():
            for i in range(OPEN):
                forward_alone(i, 1 - core).wait_recv()

        @pl.when(middle | (tick == TICKS - 1))
        def _():
            first = jnp.where(middle, 0, 2)
            for i in range(2):
                forward_shared(first + i + OPEN, 1 - core).wait_recv()
                post_forward(first + i, 1 - core).wait_recv()

        @pl.when(opening | middle | (tick == TICKS - 1))
        def _():
            start = jnp.where(opening, 0, jnp.where(middle, OPEN, OPEN + 2))
            flags = [jnp.where(opening, a, b) for a, b in zip(own_lane, pair_lane)]
            chunk_pairs(start, 2, flags)

        @pl.when((tick == TICKS - 1) | (tick == TICKS))
        def _():
            forward_alone(tick - 1, 1 - core).wait_recv()
            chunk_pairs(tick - 1, 1, own_lane)

        @pl.when(alone(tick))
        def _():
            cross_alone(tick).wait_recv()
            forward_alone(tick, core).start()

        @pl.when(shared(tick))
        def _():
            cross_shared(tick).wait_recv()
            forward_shared(tick, core).start()
            post_copy(tick - OPEN, upper).start()

        @pl.when(tick + LEAD < TICKS)
        def _():
            send(tick + LEAD)

        @pl.when(tick == OPEN + STEPS)
        def _():
            for i in range(OPEN):
                collect(i)

        return carry

    lax.fori_loop(0, TICKS + 1, tick_fn, 0)
    back_corner().start()

    def collect_fn(tick, carry):
        collect(tick)
        return carry

    lax.fori_loop(OPEN, TICKS - 1, collect_fn, 0)

    def shared_fn(k, carry):
        back_mate(k + OPEN).wait_recv()

        @pl.when(sends_edge)
        def _():
            edge_back(k).start()

        return carry

    lax.fori_loop(0, STEPS, shared_fn, 0)

    def close(k, carry):
        tick = jnp.where(k < OPEN, k, k + STEPS)

        @pl.when(k == STEPS - 1)
        def _():
            back_copy(TICKS - 1).wait_recv()

        back_mate(tick).wait_recv()

        @pl.when(takes_edge)
        def _():
            edge_back(k).wait_recv()

        def both(at):
            return ret[at].astype(jnp.float32) + ret_mate[at].astype(jnp.float32)

        alone_sum, shared_sum = both(tick), both(k + OPEN)
        edge_sum = jnp.where(takes_edge, ret_edge[k].astype(jnp.float32), 0.0)
        for block, edge_flag in enumerate((edge_out0, edge_out1)):
            lines = (
                alone_sum * own_lane[1 - block].astype(jnp.float32)
                + shared_sum * pair_lane[1 - block].astype(jnp.float32)
                + edge_sum * edge_flag.astype(jnp.float32)
            )
            line = lines[CHUNK : CHUNK + 1, :] + lines[CHUNK + 8 : CHUNK + 9, :]
            degree = jnp.broadcast_to(line, (CHUNK, CHUNK)).T
            rows = pl.ds(pl.multiple_of(block * BLOCK + k * CHUNK, CHUNK), CHUNK)
            out[rows, :] = (own[rows, :feat] + lines[:CHUNK, :]) / (own[rows, feat:] + degree)
        return carry

    lax.fori_loop(0, STEPS, close, 0)

    def finish(tick, carry):
        @pl.when(alone(tick))
        def _():
            cross_alone(tick).wait_send()
            forward_alone(tick, core).wait_send()

        @pl.when(shared(tick))
        def _():
            cross_shared(tick).wait_send()
            forward_shared(tick, core).wait_send()

        back_copy(tick).wait_send()
        back_mate(tick).wait_send()
        return carry

    lax.fori_loop(0, TICKS, finish, 0)

    def finish_chunk(k, carry):
        for block in range(2):
            mate_copy(k, block).wait_send()
        pre_copy(k).wait_send()
        post_copy(k, upper).wait_send()
        post_forward(k, core).wait_send()

        @pl.when(sends_edge)
        def _():
            edge_back(k).wait_send()

        return carry

    lax.fori_loop(0, STEPS, finish_chunk, 0)


def pair_plan(parity, spectra, scores, reach):
    rows, bins = spectra.shape
    feat = scores.shape[1]
    width = bins + feat
    vmem = pl.BlockSpec(memory_space=pltpu.VMEM)
    bf16 = jnp.bfloat16
    return pl.pallas_call(
        functools.partial(pair_kernel, parity),
        out_shape=jax.ShapeDtypeStruct((rows, feat), jnp.float32),
        in_specs=[pl.BlockSpec(memory_space=pltpu.SMEM)] + [pl.BlockSpec(memory_space=pltpu.HBM)] * 2,
        out_specs=vmem,
        scratch_shapes=[
            pltpu.VMEM((rows, bins), bf16),
            pltpu.VMEM((rows, feat), bf16),
            pltpu.VMEM((rows, width), bf16),
            pltpu.VMEM((STEPS, 2, PIECE, width), bf16),
            pltpu.VMEM((STEPS, QUARTER, width), bf16),
            pltpu.VMEM((STEPS, QUARTER, width), bf16),
            pltpu.VMEM((STEPS, PIECE, width), bf16),
            pltpu.VMEM((STEPS, QUARTER, width), bf16),
            pltpu.VMEM((TICKS * CHUNK, width), bf16),
            pltpu.VMEM((rows, 2 * feat), jnp.float32),
            pltpu.VMEM((2 * CHUNK, 2 * feat), jnp.float32),
            pltpu.VMEM((TICKS, LINES, feat), bf16),
            pltpu.VMEM((TICKS, LINES, feat), bf16),
            pltpu.VMEM((TICKS, LINES, feat), bf16),
            pltpu.VMEM((STEPS, LINES, feat), bf16),
            pltpu.SemaphoreType.DMA((2 * STEPS + 1,)),
            pltpu.SemaphoreType.DMA((56,)),
            pltpu.SemaphoreType.DMA((56,)),
        ],
        compiler_params=pltpu.CompilerParams(
            collective_id=8 + parity,
            has_side_effects=True,
            vmem_limit_bytes=48 * 2**20,
        ),
        cost_estimate=pl.CostEstimate(
            flops=8 * 2 * BLOCK * BLOCK * bins,
            bytes_accessed=2 * rows * width,
            transcendentals=rows * bins,
        ),
        name="pairs",
    )(reach, spectra, scores)


def branch(reach):
    size = reach.shape[0]
    group = 2 * GROUP
    margin = 2
    padded = jnp.pad(reach, (margin, size))
    index = lax.iota(jnp.int32, size)

    def at(shift):
        return padded[margin + shift : margin + shift + size]

    def right(boundary):
        return jnp.where(at(2 * boundary + 1) == 2, 1, 0)

    def left(boundary):
        return jnp.where((at(2 * boundary) == 2) | (at(2 * boundary + 1) == 1), 1, 0)

    def lanes(first):
        going = right(first) + left(first + 1) + right(first + 2)
        coming = left(first) + right(first + 1) + left(first + 2)
        return going, coming

    def over(lane):
        return jnp.maximum(lane - 1, 0)

    def flag(condition, place):
        return jnp.where(condition, 2**place, 0)

    odd = lax.rem(index, 2 * group) == group
    going, coming = lanes(0)
    next_going, next_coming = lanes(GROUP)
    last_going, last_coming = lanes((size - group) // 2)
    edge_right, edge_left = right(3), left(3)
    edge = edge_right + edge_left > 0
    over_going, over_coming = over(going), over(coming)
    shared = jnp.maximum(
        over_going + over(next_going) + edge_left, over_coming + over(next_coming) + edge_right
    )
    more_going = going + left(-1) + edge_left
    more_coming = coming + right(-1) + edge_right
    plain = jnp.maximum(going, coming)
    more = jnp.maximum(more_going, more_coming)
    wrapped = jnp.maximum(over_going + over(last_going), over_coming + over(last_coming))
    full = over_going + over_coming > 0
    misses = (
        flag(full | edge, 0)
        | flag(jnp.where(odd, edge, shared > 1), 1)
        | flag(jnp.where(odd, shared > 1, edge), 2)
        | flag(jnp.where(odd, more, plain) > 2, 3)
        | flag(jnp.where(odd, plain, more) > 2, 4)
        | flag((index == 0) & (wrapped > 1), 2)
    )
    misses = jnp.where(lax.rem(index, group) == 0, misses, 0)
    missed = lax.reduce(misses, jnp.int32(0), lax.bitwise_or, (0,))
    return 31 - lax.clz(~missed & (missed + 1))


def body(spectra, class_scores, reach):
    if reach.shape[0] % 16:
        return plan(True, True, spectra, class_scores, reach)
    branches = [
        functools.partial(slots_plan, 1, False, 0),
        functools.partial(pair_plan, 0),
        functools.partial(pair_plan, 1),
        functools.partial(slots_plan, 2, True, 0),
        functools.partial(slots_plan, 2, True, 1),
        functools.partial(plan, True, True),
    ]
    return lax.switch(branch(reach), branches, spectra, class_scores, reach)


def solution(mesh):
    return jax.shard_map(
        body,
        mesh=mesh,
        in_specs=(P(AXES, None), P(AXES, None), P()),
        out_specs=P(AXES, None),
        check_vma=False,
    )
```
